256 devices in a mesh: ta: 8 (over z_lo, core), ha: 8 (over z_hi, y), wa: 4 (over x).
Axes of the slice: x: 4, y: 4, z: 8 (z_hi: 2, z_lo: 4; z = z_hi * 4 + z_lo), core: 2. Of those that a mesh axis runs over, the one named last changes fastest.
Arguments:
- query: bfloat16 [16, 32, 64, 1536], P('ta', 'ha', 'wa')
- key: bfloat16 [16, 32, 64, 1536], P('ta', 'ha', 'wa')
- value: bfloat16 [16, 32, 64, 1536], P('ta', 'ha', 'wa'), may hold values from -6 to 6
- d_out: bfloat16 [16, 32, 64, 1536], P('ta', 'ha', 'wa'), may hold values from -6 to 6
- text_key: bfloat16 [256, 1536], P(('ta', 'ha', 'wa')), may hold values from -6 to 6
- text_value: bfloat16 [256, 1536], P(('ta', 'ha', 'wa')), may hold values from -6 to 6
- block_pattern: int32 [8, 16, 16, 27], P('ta', 'ha', 'wa'), may hold values from 0 to 1, as said below
- text_length: int32 [1], replicated, may hold values from 32 to 256
Outputs:
- attended: bfloat16 [16, 32, 64, 1536], P('ta', 'ha', 'wa')
- query_grad: bfloat16 [16, 32, 64, 1536], P('ta', 'ha', 'wa')
- key_grad: bfloat16 [16, 32, 64, 1536], P('ta', 'ha', 'wa')
- value_grad: bfloat16 [16, 32, 64, 1536], P('ta', 'ha', 'wa')
- text_key_grad: bfloat16 [256, 1536], P(('ta', 'ha', 'wa'))
- text_value_grad: bfloat16 [256, 1536], P(('ta', 'ha', 'wa'))
The draws below stay inside these ranges and needn't reach their ends.
Inputs may be any that keep to these rules, and one draw needn't show every extreme that they name: `block_pattern`: entry 13 (offset 0, 0, 0) is always 1.
All inputs are finite; a program needn't handle non-finite values.
Results may differ from the reference program's by a relative error of at most 0.013.
Values may be sent and summed in bfloat16 or wider, within the bound.
No kernel may reach another device: no remote copies, remote signals or barrier semaphores. Data moves between devices by JAX's collectives and lax.ppermute only.
A program may use at most 192 MiB of HBM per device.

```python
import jax
import jax.numpy as jnp
from jax import lax

HEADS = 12
HEAD = 128
HD = 1536
TEXT = 256
TILE_T = 2
TILE_H = 2
TILE_W = 4
FRAMES = 16
LAT_ROWS = 32
LAT_COLS = 64


def draw_query(key, part):
    key = jax.random.fold_in(key, 11)
    full_shape = (FRAMES, LAT_ROWS, LAT_COLS, HD)
    return jax.random.normal(key, full_shape, jnp.float32).astype(jnp.bfloat16)


def draw_key(key, part):
    key = jax.random.fold_in(key, 12)
    full_shape = (FRAMES, LAT_ROWS, LAT_COLS, HD)
    return jax.random.normal(key, full_shape, jnp.float32).astype(jnp.bfloat16)


def draw_block_pattern(key, part):
    key = jax.random.fold_in(key, 21)
    grid_shape = (FRAMES // TILE_T, LAT_ROWS // TILE_H, LAT_COLS // TILE_W)
    rates = jax.random.randint(jax.random.fold_in(key, 1), grid_shape + (1,), 2, 9)
    rolled = jax.random.randint(jax.random.fold_in(key, 2), grid_shape + (27,), 0, 8)
    centre = lax.broadcasted_iota(jnp.int32, grid_shape + (27,), 3) == 13
    return jnp.where(jnp.logical_or(rolled < rates, centre), 1, 0).astype(jnp.int32)


def shard_levels(own_key, dims, cuts, smallest, largest):
    gain = 1.0
    for position, blocks in cuts:
        steps = jax.random.uniform(jax.random.fold_in(jax.random.fold_in(own_key, 6), position), (blocks,), jnp.float32, smallest / len(cuts), largest / len(cuts))
        gain = gain * jnp.repeat(jnp.exp(steps), dims[position] // blocks).reshape((-1,) + (1,) * (len(dims) - 1 - position))
    return gain


def centred(key, shape, spread, bound, shards=(), kind=jnp.bfloat16):
    drawn = spread * jax.random.normal(key, shape, jnp.float32)
    if shards:
        drawn = drawn * shard_levels(key, shape, shards, -0.22, 0.18)
    return jnp.clip(drawn, -bound, bound).astype(kind)


def setup_inputs(seed: int = 0) -> dict:
    key_list = jax.random.split(jax.random.key(seed), 9)
    return {
        "query": draw_query(jax.random.fold_in(key_list[8], 71), 0),
        "key": draw_key(jax.random.fold_in(key_list[8], 71), 0),
        "value": centred(key_list[2], (FRAMES, LAT_ROWS, LAT_COLS, HD), 1.0, 6.0, ((0, 8), (1, 8), (2, 4))),
        "d_out": centred(key_list[3], (FRAMES, LAT_ROWS, LAT_COLS, HD), 1.0, 6.0, ((0, 8), (1, 8), (2, 4))),
        "text_key": centred(key_list[4], (TEXT, HD), 1.0, 6.0, ((0, 256),)),
        "text_value": centred(key_list[5], (TEXT, HD), 1.0, 6.0, ((0, 256),)),
        "block_pattern": draw_block_pattern(jax.random.fold_in(key_list[8], 71), 0),
        "text_length": jax.random.randint(key_list[7], (1,), 32, TEXT + 1).astype(jnp.int32),
    }


NEGATIVE = -1e30


def to_tiles(field):
    frames, rows, cols, chans = field.shape
    shaped = field.reshape(frames // TILE_T, TILE_T, rows // TILE_H, TILE_H, cols // TILE_W, TILE_W, chans)
    shaped = jnp.transpose(shaped, (0, 2, 4, 1, 3, 5, 6))
    return shaped.reshape(frames // TILE_T, rows // TILE_H, cols // TILE_W, TILE_T * TILE_H * TILE_W, chans)


def from_tiles(tiled, frames, rows, cols):
    chans = tiled.shape[-1]
    shaped = tiled.reshape(frames // TILE_T, rows // TILE_H, cols // TILE_W, TILE_T, TILE_H, TILE_W, chans)
    shaped = jnp.transpose(shaped, (0, 3, 1, 4, 2, 5, 6))
    return shaped.reshape(frames, rows, cols, chans)


def pad_tiles(tiled):
    widths = [(1, 1), (1, 1), (1, 1)] + [(0, 0)] * (tiled.ndim - 3)
    return jnp.pad(tiled, widths)


def neighbours(padded, first, second, third):
    extent = (3, 3, 3) + padded.shape[3:]
    starts = [jnp.asarray(first).astype(jnp.int32), jnp.asarray(second).astype(jnp.int32), jnp.asarray(third).astype(jnp.int32)]
    starts = starts + [jnp.zeros((), jnp.int32)] * (padded.ndim - 3)
    block = lax.dynamic_slice(padded, starts, extent)
    return block.reshape((27,) + padded.shape[3:])


def reference(query, key, value, d_out, text_key, text_value, block_pattern, text_length):
    frames, rows, cols, width = query.shape
    score_scale = HEAD ** -0.5
    tile_rows = TILE_T * TILE_H * TILE_W
    q_tiles = to_tiles(query)
    k_tiles = to_tiles(key)
    v_tiles = to_tiles(value)
    g_tiles = to_tiles(d_out)
    grid_t, grid_h, grid_w = q_tiles.shape[:3]
    k_padded = pad_tiles(k_tiles)
    v_padded = pad_tiles(v_tiles)
    valid_padded = pad_tiles(jnp.ones((grid_t, grid_h, grid_w), jnp.int32))
    text_ok = jnp.arange(TEXT, dtype=jnp.int32) < text_length[0]

    def query_tile(first, second, third):
        q_here = q_tiles[first, second, third].astype(jnp.float32).reshape(tile_rows, HEADS, HEAD)
        g_here = g_tiles[first, second, third].astype(jnp.float32).reshape(tile_rows, HEADS, HEAD)
        key_rows = jnp.concatenate([neighbours(k_padded, first, second, third).reshape(27 * tile_rows, width), text_key], 0)
        value_rows = jnp.concatenate([neighbours(v_padded, first, second, third).reshape(27 * tile_rows, width), text_value], 0)
        key_f32 = key_rows.astype(jnp.float32).reshape(-1, HEADS, HEAD)
        value_f32 = value_rows.astype(jnp.float32).reshape(-1, HEADS, HEAD)
        tile_ok = (block_pattern[first, second, third] * neighbours(valid_padded, first, second, third)) > 0
        allowed = jnp.concatenate([jnp.repeat(tile_ok, tile_rows), text_ok])
        scores = jnp.einsum("qhd,khd->hqk", q_here, key_f32) * score_scale
        scores = jnp.where(allowed[None, None, :], scores, NEGATIVE)
        row_max = jnp.max(scores, axis=2, keepdims=True)
        exponent = jnp.exp(scores - row_max)
        row_sum = jnp.sum(exponent, axis=2, keepdims=True)
        softmax = exponent / row_sum
        log_norm = (row_max + jnp.log(row_sum))[:, :, 0]
        weights = softmax.astype(jnp.bfloat16).astype(jnp.float32)
        attended = jnp.einsum("hqk,khd->qhd", weights, value_f32).reshape(tile_rows, width).astype(jnp.bfloat16)
        row_delta = jnp.sum(g_here * attended.astype(jnp.float32).reshape(tile_rows, HEADS, HEAD), axis=2).T
        dprob = jnp.einsum("qhd,khd->hqk", g_here, value_f32)
        dscore = (softmax * (dprob - row_delta[:, :, None])).astype(jnp.bfloat16).astype(jnp.float32)
        query_grad = (score_scale * jnp.einsum("hqk,khd->qhd", dscore, key_f32)).reshape(tile_rows, width).astype(jnp.bfloat16)
        text_dk = score_scale * jnp.einsum("hqk,qhd->khd", dscore[:, :, 27 * tile_rows:], q_here).reshape(TEXT, width)
        text_dv = jnp.einsum("hqk,qhd->khd", weights[:, :, 27 * tile_rows:], g_here).reshape(TEXT, width)
        return attended, query_grad, log_norm, row_delta, text_dk, text_dv

    thirds = jnp.arange(grid_w, dtype=jnp.int32)

    def query_row(flat):
        first = flat // grid_h
        second = flat % grid_h
        results = jax.vmap(lambda third: query_tile(first, second, third))(thirds)
        attended, query_grad, log_norm, row_delta, text_dk, text_dv = results
        return attended, query_grad, log_norm, row_delta, jnp.sum(text_dk, 0), jnp.sum(text_dv, 0)

    attended, query_grad, log_norm, row_delta, text_dk, text_dv = lax.map(query_row, jnp.arange(grid_t * grid_h, dtype=jnp.int32))
    attended_tiles = attended.reshape(grid_t, grid_h, grid_w, tile_rows, width)
    query_grad_tiles = query_grad.reshape(grid_t, grid_h, grid_w, tile_rows, width)
    norm_padded = pad_tiles(log_norm.reshape(grid_t, grid_h, grid_w, HEADS, tile_rows))
    delta_padded = pad_tiles(row_delta.reshape(grid_t, grid_h, grid_w, HEADS, tile_rows))
    q_padded = pad_tiles(q_tiles)
    g_padded = pad_tiles(g_tiles)
    pattern_padded = pad_tiles(block_pattern)
    offsets = jnp.arange(27, dtype=jnp.int32)

    def key_tile(first, second, third):
        k_here = k_tiles[first, second, third].astype(jnp.float32).reshape(tile_rows, HEADS, HEAD)
        v_here = v_tiles[first, second, third].astype(jnp.float32).reshape(tile_rows, HEADS, HEAD)
        q_near = neighbours(q_padded, first, second, third).astype(jnp.float32).reshape(27 * tile_rows, HEADS, HEAD)
        g_near = neighbours(g_padded, first, second, third).astype(jnp.float32).reshape(27 * tile_rows, HEADS, HEAD)
        norm_near = jnp.transpose(neighbours(norm_padded, first, second, third), (1, 0, 2)).reshape(HEADS, 27 * tile_rows)
        delta_near = jnp.transpose(neighbours(delta_padded, first, second, third), (1, 0, 2)).reshape(HEADS, 27 * tile_rows)
        pattern_near = neighbours(pattern_padded, first, second, third)
        tile_ok = pattern_near[offsets, 26 - offsets] > 0
        allowed = jnp.repeat(tile_ok, tile_rows)
        scores = jnp.einsum("qhd,khd->hqk", q_near, k_here) * score_scale
        softmax = jnp.where(allowed[None, :, None], jnp.exp(scores - norm_near[:, :, None]), 0.0)
        weights = softmax.astype(jnp.bfloat16).astype(jnp.float32)
        dprob = jnp.einsum("qhd,khd->hqk", g_near, v_here)
        dscore = (softmax * (dprob - delta_near[:, :, None])).astype(jnp.bfloat16).astype(jnp.float32)
        key_grad = score_scale * jnp.einsum("hqk,qhd->khd", dscore, q_near).reshape(tile_rows, width)
        value_grad = jnp.einsum("hqk,qhd->khd", weights, g_near).reshape(tile_rows, width)
        return key_grad.astype(jnp.bfloat16), value_grad.astype(jnp.bfloat16)

    def key_row(flat):
        first = flat // grid_h
        second = flat % grid_h
        return jax.vmap(lambda third: key_tile(first, second, third))(thirds)

    key_grad, value_grad = lax.map(key_row, jnp.arange(grid_t * grid_h, dtype=jnp.int32))
    key_grad = key_grad.reshape(grid_t, grid_h, grid_w, tile_rows, width)
    value_grad = value_grad.reshape(grid_t, grid_h, grid_w, tile_rows, width)
    return (from_tiles(attended_tiles, frames, rows, cols),
            from_tiles(query_grad_tiles, frames, rows, cols),
            from_tiles(key_grad, frames, rows, cols),
            from_tiles(value_grad, frames, rows, cols),
            jnp.sum(text_dk, 0).astype(jnp.bfloat16),
            jnp.sum(text_dv, 0).astype(jnp.bfloat16))
```

```python
import functools

import jax
import jax.numpy as jnp
import numpy as np
from jax import lax
from jax.experimental import pallas as pl
from jax.experimental.pallas import tpu as pltpu
from jax.sharding import PartitionSpec as P

HEAD = 128
PAIR = 2 * HEAD
TILE_T = 2
TILE_H = 2
TILE_W = 4
TILE = TILE_T * TILE_H * TILE_W
NEGATIVE = -1e30
EXTRA = 16
VMEM = 48 * 1024 * 1024
F32 = jnp.float32
BF16 = jnp.bfloat16

ROWS = 4
COLS = 16
TILES_H = ROWS // TILE_H
TILES_W = COLS // TILE_W
CUBE = TILE_T * ROWS * COLS
WIDE_W = TILES_W + 2
WIDE_H = TILES_H + 2
WINDOW = WIDE_W * WIDE_H * TILE


def natural_index(row):
    tile_w = row >> 5
    tile_h = (row >> 4) & 1
    t = (row >> 3) & 1
    h = (row >> 2) & 1
    w = row & 3
    return t * (ROWS * COLS) + (tile_h * TILE_H + h) * COLS + tile_w * TILE_W + w


def pack_kernel(first_ref, second_ref, *rest, extra):
    out_ref = rest[-1]
    row = lax.broadcasted_iota(jnp.int32, (CUBE, CUBE), 0)
    col = lax.broadcasted_iota(jnp.int32, (CUBE, CUBE), 1)
    order = jnp.where(natural_index(row) == col, 1.0, 0.0).astype(BF16)
    first = jnp.dot(order, first_ref[...], preferred_element_type=F32).astype(BF16)
    second = jnp.dot(order, second_ref[...], preferred_element_type=F32).astype(BF16)
    heads = first.shape[1] // HEAD
    for i in range(heads):
        out_ref[0, :CUBE, i * PAIR : i * PAIR + HEAD] = first[:, i * HEAD : (i + 1) * HEAD]
        out_ref[0, :CUBE, i * PAIR + HEAD : (i + 1) * PAIR] = second[:, i * HEAD : (i + 1) * HEAD]
    if extra:
        pattern_ref, text_key_ref, text_value_ref = rest[:3]
        text_key = text_key_ref[...].astype(F32)
        text_value = text_value_ref[...].astype(F32)
        for i in range(heads):
            for part, source in enumerate((text_key, text_value)):
                if i == 0 and part == 0:
                    top = pattern_ref[...]
                else:
                    top = jnp.zeros((8, HEAD), F32)
                line = jnp.broadcast_to(source[:, i * HEAD : (i + 1) * HEAD], (8, HEAD))
                place = (2 * i + part) * HEAD
                out_ref[0, CUBE:, place : place + HEAD] = jnp.concatenate([top, line], 0).astype(
                    BF16
                )


def pack(first, second, groups, extras=()):
    width = first.shape[1] // groups
    rows = CUBE + (EXTRA if extras else 0)
    specs = [pl.BlockSpec((CUBE, width), lambda g: (0, g))] * 2
    if extras:
        specs.append(pl.BlockSpec((8, HEAD), lambda g: (0, 0)))
        specs += [pl.BlockSpec((1, width), lambda g: (0, g))] * 2
    return pl.pallas_call(
        functools.partial(pack_kernel, extra=bool(extras)),
        grid=(groups,),
        in_specs=specs,
        out_specs=pl.BlockSpec((1, rows, 2 * width), lambda g: (g, 0, 0)),
        out_shape=jax.ShapeDtypeStruct((groups, rows, 2 * width), BF16),
        compiler_params=pltpu.CompilerParams(vmem_limit_bytes=VMEM),
    )(first, second, *extras)


def unpack_kernel(packed_ref, first_ref, second_ref, *rest):
    row = lax.broadcasted_iota(jnp.int32, (CUBE, CUBE), 0)
    col = lax.broadcasted_iota(jnp.int32, (CUBE, CUBE), 1)
    order = jnp.where(natural_index(col) == row, 1.0, 0.0).astype(BF16)
    both = jnp.dot(order, packed_ref[0, :CUBE, :], preferred_element_type=F32).astype(BF16)
    heads = both.shape[1] // PAIR
    for i in range(heads):
        first_ref[:, i * HEAD : (i + 1) * HEAD] = both[:, i * PAIR : i * PAIR + HEAD]
        second_ref[:, i * HEAD : (i + 1) * HEAD] = both[:, i * PAIR + HEAD : (i + 1) * PAIR]
    if rest:
        line = packed_ref[0, CUBE:, :].astype(F32)[:1]
        for i in range(heads):
            for part, target in enumerate(rest):
                place = (2 * i + part) * HEAD
                target[:, i * HEAD : (i + 1) * HEAD] = line[:, place : place + HEAD].astype(BF16)


def unpack(packed, with_text):
    groups, rows, width = packed.shape
    half = width // 2
    out_specs = [pl.BlockSpec((CUBE, half), lambda g: (0, g))] * 2
    out_shape = [jax.ShapeDtypeStruct((CUBE, groups * half), BF16)] * 2
    if with_text:
        out_specs += [pl.BlockSpec((1, half), lambda g: (0, g))] * 2
        out_shape += [jax.ShapeDtypeStruct((1, groups * half), BF16)] * 2
    return pl.pallas_call(
        unpack_kernel,
        grid=(groups,),
        in_specs=[pl.BlockSpec((1, rows, width), lambda g: (g, 0, 0))],
        out_specs=out_specs,
        out_shape=out_shape,
        compiler_params=pltpu.CompilerParams(vmem_limit_bytes=VMEM),
    )(packed)


def window_start(block, blocks):
    return min(max(block * TILES_W - 1, 0), blocks * TILES_W - WIDE_W)


def attention_kernel(
    length_ref,
    allow_ref,
    qg_ref,
    here_ref,
    below_ref,
    above_ref,
    text_ref,
    od_ref,
    here_grad_ref,
    below_grad_ref,
    above_grad_ref,
    text_grad_ref,
    grads,
):
    blocks = qg_ref.shape[0]
    text_count = text_ref.shape[0]
    scale = HEAD**-0.5
    near = (here_ref, below_ref, above_ref)
    grads[...] = jnp.zeros_like(grads)
    text_ok = lax.broadcasted_iota(jnp.int32, (text_count, CUBE), 0) < length_ref[0]
    blank = jnp.zeros((CUBE, HEAD), BF16)
    text_kv = text_ref[...]
    text_total = jnp.zeros((text_count, PAIR), F32)
    for block in range(blocks):
        start = window_start(block, blocks) * WIDE_H * TILE
        rows = slice(start, start + WINDOW)
        q = qg_ref[block, :, :HEAD]
        g = qg_ref[block, :, HEAD:]
        both = jnp.concatenate(
            [jnp.concatenate([q, blank], 1), jnp.concatenate([blank, g], 1)], 0
        )
        keys = [ref[rows, :] for ref in near] + [text_kv]
        masks = []
        for i in range(3):
            tiles = allow_ref[block, i * (WIDE_W * WIDE_H) : (i + 1) * (WIDE_W * WIDE_H), :]
            spread = jnp.broadcast_to(tiles[:, None, :], (WIDE_W * WIDE_H, TILE, CUBE))
            masks.append(spread.reshape(WINDOW, CUBE) > 0.5)
        masks.append(text_ok)
        scores = []
        dprobs = []
        for kv, ok in zip(keys, masks):
            mixed = lax.dot_general(
                kv, both, (((1,), (1,)), ((), ())), preferred_element_type=F32
            )
            scores.append(jnp.where(ok, mixed[:, :HEAD] * scale, NEGATIVE))
            dprobs.append(mixed[:, HEAD:])
        top = functools.reduce(jnp.maximum, [jnp.max(s, 0, keepdims=True) for s in scores])
        exps = [jnp.exp(s - top) for s in scores]
        total = functools.reduce(jnp.add, [jnp.sum(e, 0, keepdims=True) for e in exps])
        inverse = 1.0 / total
        soft = [e * inverse for e in exps]
        weights = [s.astype(BF16) for s in soft]
        attended = jnp.zeros((CUBE, HEAD), F32)
        for w, kv in zip(weights, keys):
            attended += lax.dot_general(
                w, kv[:, HEAD:], (((0,), (0,)), ((), ())), preferred_element_type=F32
            )
        attended = attended.astype(BF16)
        od_ref[block, :, :HEAD] = attended
        product = g.astype(F32) * attended.astype(F32)
        delta = jnp.sum(product.T, 0, keepdims=True)
        dscores = [(s * (d - delta)).astype(BF16) for s, d in zip(soft, dprobs)]
        query_grad = jnp.zeros((CUBE, HEAD), F32)
        for d, kv in zip(dscores, keys):
            query_grad += lax.dot_general(
                d, kv[:, :HEAD], (((0,), (0,)), ((), ())), preferred_element_type=F32
            )
        od_ref[block, :, HEAD:] = (query_grad * scale).astype(BF16)
        for i in range(4):
            change = jnp.dot(
                jnp.concatenate([dscores[i], weights[i]], 1), both, preferred_element_type=F32
            )
            if i < 3:
                grads[i, rows, :] += change
            else:
                text_total += change
    lane = lax.broadcasted_iota(jnp.int32, (1, PAIR), 1)
    factor = jnp.where(lane < HEAD, scale, 1.0).astype(F32)
    here_grad_ref[...] = grads[0] * factor
    below_grad_ref[...] = (grads[1] * factor).astype(BF16)
    above_grad_ref[...] = (grads[2] * factor).astype(BF16)
    text_grad_ref[...] = text_total * factor


def attention(length, allow, qg, here, below, above, text):
    blocks, _, width = qg.shape
    heads = width // PAIR
    tokens = here.shape[0]
    text_count = text.shape[0]
    wide = pl.BlockSpec((tokens, PAIR), lambda h: (0, h))
    part = pl.BlockSpec((blocks, CUBE, PAIR), lambda h: (0, 0, h))
    text_spec = pl.BlockSpec((text_count, PAIR), lambda h: (0, h))
    return pl.pallas_call(
        attention_kernel,
        grid=(heads,),
        in_specs=[
            pl.BlockSpec(memory_space=pltpu.SMEM),
            pl.BlockSpec(allow.shape, lambda h: (0, 0, 0)),
            part,
            wide,
            wide,
            wide,
            text_spec,
        ],
        out_specs=[part, wide, wide, wide, text_spec],
        out_shape=[
            jax.ShapeDtypeStruct(qg.shape, BF16),
            jax.ShapeDtypeStruct((tokens, width), F32),
            jax.ShapeDtypeStruct((tokens, width), BF16),
            jax.ShapeDtypeStruct((tokens, width), BF16),
            jax.ShapeDtypeStruct((text_count, width), F32),
        ],
        scratch_shapes=[pltpu.VMEM((3, tokens, PAIR), F32)],
        compiler_params=pltpu.CompilerParams(vmem_limit_bytes=VMEM),
    )(length, allow, qg, here, below, above, text)


def offset_table(blocks):
    table = np.full((blocks, 3, WIDE_W, WIDE_H, TILES_W, TILES_H), -1, np.int32)
    for block in range(blocks):
        start = window_start(block, blocks)
        for i, dt in enumerate((0, -1, 1)):
            for kw in range(WIDE_W):
                for kh in range(WIDE_H):
                    for qw in range(TILES_W):
                        for qh in range(TILES_H):
                            dw = start + kw - (block * TILES_W + qw)
                            dh = kh - (qh + 1)
                            if abs(dw) <= 1 and abs(dh) <= 1:
                                table[block, i, kw, kh, qw, qh] = 9 * dt + 3 * dh + dw + 13
    return table


def allowed_tiles(pattern, blocks):
    table = offset_table(blocks)
    hot = table[..., None] == np.arange(27)
    by_column = jnp.swapaxes(pattern, 1, 2)[:, None, None, None]
    picked = jnp.sum(jnp.where(hot, by_column, 0.0), -1)
    t = lax.axis_index("ta") + jnp.array([0, -1, 1])
    t_ok = (t >= 0) & (t < lax.axis_size("ta"))
    h = lax.axis_index("ha") * TILES_H + jnp.arange(WIDE_H) - 1
    h_ok = (h >= 0) & (h < TILES_H * lax.axis_size("ha"))
    inside = t_ok[:, None, None] & h_ok[None, None, :]
    picked = jnp.where(inside[None, :, :, :, None, None], picked, 0.0)
    picked = picked.reshape(blocks, 3 * WIDE_W * WIDE_H, TILES_W * TILES_H)
    return jnp.repeat(picked, TILE, axis=2)


def turned_height(value, step):
    count = lax.axis_size("ha")
    return lax.ppermute(value, "ha", [(i, (i + step) % count) for i in range(count)])


def turned_time(value, step):
    count_t, count_h = lax.axis_size("ta"), lax.axis_size("ha")
    pairs = []
    for t in range(count_t):
        for h in range(count_h):
            t_to = t + step
            h_to = h
            if not 0 <= t_to < count_t:
                h_to = (h + count_h // 2) % count_h
            pairs.append((t * count_h + h, t_to % count_t * count_h + h_to))
    return lax.ppermute(value, ("ta", "ha"), pairs)


def swapped(value, axis, bit):
    count = lax.axis_size(axis)
    return lax.ppermute(value, axis, [(i, i ^ bit) for i in range(count)])


def text_steps():
    steps = []
    bit = 1
    while bit < lax.axis_size("ha"):
        steps.append(("ha", bit, 0))
        bit *= 2
    bit = lax.axis_size("ta") // 2
    depth = 0
    while bit >= 1:
        steps.append(("ta", bit, depth))
        bit //= 2
        depth += 1
    return steps


def gathered_text(rows):
    width = rows.shape[-1]
    value = rows
    for axis, bit, depth in text_steps():
        other = swapped(value, axis, bit)
        high = (lax.axis_index(axis) & bit) > 0
        first = jnp.where(high, other, value)
        second = jnp.where(high, value, other)
        value = jnp.stack([first, second], axis=depth)
    return value.reshape(-1, width)


def scattered_text(total):
    width = total.shape[-1]
    steps = text_steps()
    value = total.reshape((2,) * len(steps) + (-1, width))
    for axis, bit, depth in reversed(steps):
        high = (lax.axis_index(axis) & bit) > 0
        first = lax.index_in_dim(value, 0, depth, keepdims=False)
        second = lax.index_in_dim(value, 1, depth, keepdims=False)
        mine = jnp.where(high, second, first)
        theirs = jnp.where(high, first, second)
        value = mine + swapped(theirs, axis, bit)
    return value


def local(query, key, value, d_out, text_key, text_value, block_pattern, text_length):
    blocks = lax.axis_size("wa")
    full = query.shape[-1]
    pattern = jnp.pad(block_pattern.reshape(8, 27).astype(F32), ((0, 0), (0, HEAD - 27)))
    kv_out = pack(
        key.reshape(CUBE, full),
        value.reshape(CUBE, full),
        blocks,
        (pattern, text_key, text_value),
    )
    qg_out = pack(query.reshape(CUBE, full), d_out.reshape(CUBE, full), blocks)
    kv_in = lax.all_to_all(kv_out, "wa", 0, 0)
    width = kv_in.shape[-1]
    own = kv_in[:, :CUBE].reshape(blocks * TILES_W, TILES_H, TILE, width)
    from_below = turned_height(own[:, TILES_H - 1 :], 1)
    from_above = turned_height(own[:, :1], -1)
    qg = lax.all_to_all(qg_out, "wa", 0, 0)
    text = gathered_text(kv_in[:, CUBE + 8])
    patterns = kv_in[:, CUBE : CUBE + 8, :27].reshape(blocks, TILES_H, TILES_W, 27)
    allow = allowed_tiles(patterns.astype(F32), blocks)
    here = jnp.concatenate([from_below, own, from_above], 1).reshape(-1, width)
    below = turned_time(here, 1)
    above = turned_time(here, -1)
    od, here_grad, below_grad, above_grad, text_grad = attention(
        text_length, allow, qg, here, below, above, text
    )
    back_above = turned_time(below_grad, -1)
    back_below = turned_time(above_grad, 1)
    od_in = lax.all_to_all(od, "wa", 0, 0)
    attended, query_grad = unpack(od_in, False)
    text_sum = scattered_text(text_grad)
    summed = here_grad + back_above.astype(F32) + back_below.astype(F32)
    summed = summed.reshape(blocks * TILES_W, WIDE_H, TILE, width)
    rim_above = turned_height(summed[:, :1].astype(BF16), -1)
    rim_below = turned_height(summed[:, WIDE_H - 1 :].astype(BF16), 1)
    low = summed[:, 1:2] + rim_below.astype(F32)
    high = summed[:, 2:3] + rim_above.astype(F32)
    folded = jnp.concatenate([low, high], 1).astype(BF16).reshape(blocks, CUBE, width)
    text_lines = jnp.broadcast_to(text_sum[:, None, :], (blocks, EXTRA, width)).astype(BF16)
    grads_in = lax.all_to_all(jnp.concatenate([folded, text_lines], 1), "wa", 0, 0)
    key_grad, value_grad, text_key_grad, text_value_grad = unpack(grads_in, True)
    return (
        attended.reshape(query.shape),
        query_grad.reshape(query.shape),
        key_grad.reshape(query.shape),
        value_grad.reshape(query.shape),
        text_key_grad,
        text_value_grad,
    )


def solution(mesh):
    cube = P("ta", "ha", "wa", None)
    text = P(("ta", "ha", "wa"), None)
    return jax.shard_map(
        local,
        mesh=mesh,
        in_specs=(cube, cube, cube, cube, text, text, cube, P()),
        out_specs=(cube, cube, cube, cube, text, text),
        check_vma=False,
    )
```

```python
import functools

import jax
import jax.numpy as jnp
import numpy as np
from jax import lax
from jax.experimental import pallas as pl
from jax.experimental.pallas import tpu as pltpu
from jax.sharding import PartitionSpec as P

HEAD = 128
PAIR = 2 * HEAD
TILE_T = 2
TILE_H = 2
TILE_W = 4
TILE = TILE_T * TILE_H * TILE_W
NEGATIVE = -1e30
LOG2E = 1.4426950408889634
EXTRA = 16
VMEM = 58 * 1024 * 1024
F32 = jnp.float32
BF16 = jnp.bfloat16

ROWS = 4
COLS = 16
TILES_H = ROWS // TILE_H
TILES_W = COLS // TILE_W
CUBE = TILE_T * ROWS * COLS
GROUP = 4
GROUP_H = GROUP * TILES_H
OWN = GROUP_H * TILES_W * TILE
SIDE = GROUP_H * TILE
RIM = (TILES_W + 2) * TILE
HALO = 2 * SIDE + RIM
SEEN = (TILES_H + 2) * (TILES_W + 2)


def natural_index(row):
    tile_h = row >> 6
    tile_w = (row >> 4) & 3
    t = (row >> 3) & 1
    h = (row >> 2) & 1
    w = row & 3
    return t * (ROWS * COLS) + (tile_h * TILE_H + h) * COLS + tile_w * TILE_W + w


def pack_kernel(first_ref, second_ref, *rest, extra):
    out_ref = rest[-1]
    row = lax.broadcasted_iota(jnp.int32, (CUBE, CUBE), 0)
    col = lax.broadcasted_iota(jnp.int32, (CUBE, CUBE), 1)
    order = jnp.where(natural_index(row) == col, 1.0, 0.0).astype(BF16)
    first = jnp.dot(order, first_ref[...], preferred_element_type=F32).astype(BF16)
    second = jnp.dot(order, second_ref[...], preferred_element_type=F32).astype(BF16)
    heads = first.shape[1] // HEAD
    for i in range(heads):
        out_ref[0, :CUBE, i * PAIR : i * PAIR + HEAD] = first[:, i * HEAD : (i + 1) * HEAD]
        out_ref[0, :CUBE, i * PAIR + HEAD : (i + 1) * PAIR] = second[:, i * HEAD : (i + 1) * HEAD]
    if extra:
        pattern_ref, text_key_ref, text_value_ref = rest[:3]
        text_key = text_key_ref[...].astype(F32)
        text_value = text_value_ref[...].astype(F32)
        for i in range(heads):
            for part, source in enumerate((text_key, text_value)):
                if i == 0 and part == 0:
                    top = pattern_ref[...]
                else:
                    top = jnp.zeros((8, HEAD), F32)
                line = jnp.broadcast_to(source[:, i * HEAD : (i + 1) * HEAD], (8, HEAD))
                place = (2 * i + part) * HEAD
                out_ref[0, CUBE:, place : place + HEAD] = jnp.concatenate([top, line], 0).astype(
                    BF16
                )


def pack(first, second, groups, extras=()):
    width = first.shape[1] // groups
    rows = CUBE + (EXTRA if extras else 0)
    specs = [pl.BlockSpec((CUBE, width), lambda g: (0, g))] * 2
    if extras:
        specs.append(pl.BlockSpec((8, HEAD), lambda g: (0, 0)))
        specs += [pl.BlockSpec((1, width), lambda g: (0, g))] * 2
    return pl.pallas_call(
        functools.partial(pack_kernel, extra=bool(extras)),
        grid=(groups,),
        in_specs=specs,
        out_specs=pl.BlockSpec((1, rows, 2 * width), lambda g: (g, 0, 0)),
        out_shape=jax.ShapeDtypeStruct((groups, rows, 2 * width), BF16),
        compiler_params=pltpu.CompilerParams(vmem_limit_bytes=VMEM),
    )(first, second, *extras)


def unpack_kernel(packed_ref, first_ref, second_ref, *rest):
    row = lax.broadcasted_iota(jnp.int32, (CUBE, CUBE), 0)
    col = lax.broadcasted_iota(jnp.int32, (CUBE, CUBE), 1)
    order = jnp.where(natural_index(col) == row, 1.0, 0.0).astype(BF16)
    both = jnp.dot(order, packed_ref[0, :CUBE, :], preferred_element_type=F32).astype(BF16)
    heads = both.shape[1] // PAIR
    for i in range(heads):
        first_ref[:, i * HEAD : (i + 1) * HEAD] = both[:, i * PAIR : i * PAIR + HEAD]
        second_ref[:, i * HEAD : (i + 1) * HEAD] = both[:, i * PAIR + HEAD : (i + 1) * PAIR]
    if rest:
        line = packed_ref[0, CUBE:, :].astype(F32)[:1]
        for i in range(heads):
            for part, target in enumerate(rest):
                place = (2 * i + part) * HEAD
                target[:, i * HEAD : (i + 1) * HEAD] = line[:, place : place + HEAD].astype(BF16)


def unpack(packed, with_text):
    groups, rows, width = packed.shape
    half = width // 2
    out_specs = [pl.BlockSpec((CUBE, half), lambda g: (0, g))] * 2
    out_shape = [jax.ShapeDtypeStruct((CUBE, groups * half), BF16)] * 2
    if with_text:
        out_specs += [pl.BlockSpec((1, half), lambda g: (0, g))] * 2
        out_shape += [jax.ShapeDtypeStruct((1, groups * half), BF16)] * 2
    return pl.pallas_call(
        unpack_kernel,
        grid=(groups,),
        in_specs=[pl.BlockSpec((1, rows, width), lambda g: (g, 0, 0))],
        out_specs=out_specs,
        out_shape=out_shape,
        compiler_params=pltpu.CompilerParams(vmem_limit_bytes=VMEM),
    )(packed)


def block_rows(block):
    low, high = block * TILES_H - 1, (block + 1) * TILES_H + 1
    outer = -1 if low < 0 else GROUP_H if high > GROUP_H else None
    return max(low, 0), min(high, GROUP_H), outer


def seen_tiles(block):
    low, high, outer = block_rows(block)
    tiles = [(h, w) for h in range(low, high) for w in range(TILES_W)]
    tiles += [(h, -1) for h in range(low, high)] + [(h, TILES_W) for h in range(low, high)]
    if outer is not None:
        tiles += [(outer, w) for w in (*range(TILES_W), -1, TILES_W)]
    return tiles


def attention_kernel(
    length_ref,
    allow_ref,
    qg_ref,
    own_ref,
    own_below_ref,
    own_above_ref,
    halo_ref,
    halo_below_ref,
    halo_above_ref,
    text_ref,
    od_ref,
    own_out,
    own_below_out,
    own_above_out,
    halo_out,
    halo_below_out,
    halo_above_out,
    text_out,
    own_below_sum,
    own_above_sum,
    halo_below_sum,
    halo_above_sum,
):
    text_count = text_ref.shape[0]
    scale = HEAD**-0.5
    owns = (own_ref, own_below_ref, own_above_ref)
    halos = (halo_ref, halo_below_ref, halo_above_ref)
    own_sums = (own_out, own_below_sum, own_above_sum)
    halo_sums = (halo_out, halo_below_sum, halo_above_sum)
    text_ok = lax.broadcasted_iota(jnp.int32, (text_count, CUBE), 0) < length_ref[0]
    blank = jnp.zeros((CUBE, HEAD), BF16)
    text_kv = text_ref[...]
    line = TILES_W * TILE
    for block in range(GROUP):
        low, high, outer = block_rows(block)
        count = high - low
        q = qg_ref[block, :, :HEAD]
        g = qg_ref[block, :, HEAD:]
        both = jnp.concatenate(
            [jnp.concatenate([q, blank], 1), jnp.concatenate([blank, g], 1)], 0
        )
        done = 0 if block == 0 else 2
        places = [(False, low * line, count * line, done * line)]
        for side in range(2):
            places.append((True, side * SIDE + low * TILE, count * TILE, done * TILE))
        if outer is not None:
            places.append((True, 2 * SIDE, RIM, 0 if block == 0 else RIM))
        keys = []
        masks = []
        for i in range(3):
            parts = [
                (halos if in_halo else owns)[i][first : first + size, :]
                for in_halo, first, size, _ in places
            ]
            keys.append(jnp.concatenate(parts, 0))
            tiles = allow_ref[block, i * SEEN : (i + 1) * SEEN, :]
            spread = jnp.broadcast_to(tiles[:, None, :], (SEEN, TILE, CUBE))
            masks.append(spread.reshape(SEEN * TILE, CUBE) > 0.5)
        keys.append(text_kv)
        masks.append(text_ok)
        scores = []
        dprobs = []
        for kv, ok in zip(keys, masks):
            mixed = lax.dot_general(
                kv, both, (((1,), (1,)), ((), ())), preferred_element_type=F32
            )
            scores.append(jnp.where(ok, mixed[:, :HEAD] * (scale * LOG2E), NEGATIVE))
            dprobs.append(mixed[:, HEAD:])
        top = functools.reduce(jnp.maximum, [jnp.max(s, 0, keepdims=True) for s in scores])
        exps = [jnp.exp2(s - top) for s in scores]
        total = functools.reduce(jnp.add, [jnp.sum(e, 0, keepdims=True) for e in exps])
        inverse = 1.0 / total
        weights = [(e * inverse).astype(BF16) for e in exps]
        attended = jnp.zeros((CUBE, HEAD), F32)
        for w, kv in zip(weights, keys):
            attended += lax.dot_general(
                w, kv[:, HEAD:], (((0,), (0,)), ((), ())), preferred_element_type=F32
            )
        attended = attended.astype(BF16)
        od_ref[block, :, :HEAD] = attended
        product = g.astype(F32) * attended.astype(F32)
        delta = jnp.sum(product.T, 0, keepdims=True)
        dscores = [(e * ((d - delta) * inverse)).astype(BF16) for e, d in zip(exps, dprobs)]
        query_grad = jnp.zeros((CUBE, HEAD), F32)
        for d, kv in zip(dscores, keys):
            query_grad += lax.dot_general(
                d, kv[:, :HEAD], (((0,), (0,)), ((), ())), preferred_element_type=F32
            )
        od_ref[block, :, HEAD:] = (query_grad * scale).astype(BF16)
        for i in range(4):
            change = jnp.dot(
                jnp.concatenate([dscores[i], weights[i]], 1), both, preferred_element_type=F32
            )
            if i == 3:
                if block == 0:
                    text_out[...] = change
                else:
                    text_out[...] += change
                continue
            taken = 0
            for in_halo, first, size, old in places:
                target = (halo_sums if in_halo else own_sums)[i]
                if old:
                    target[first : first + old, :] += change[taken : taken + old]
                if old < size:
                    target[first + old : first + size, :] = change[taken + old : taken + size]
                taken += size
    lane = lax.broadcasted_iota(jnp.int32, (1, PAIR), 1)
    factor = jnp.where(lane < HEAD, scale, 1.0).astype(F32)
    own_out[...] = own_out[...] * factor
    halo_out[...] = halo_out[...] * factor
    text_out[...] = text_out[...] * factor
    own_below_out[...] = (own_below_sum[...] * factor).astype(BF16)
    own_above_out[...] = (own_above_sum[...] * factor).astype(BF16)
    halo_below_out[...] = (halo_below_sum[...] * factor).astype(BF16)
    halo_above_out[...] = (halo_above_sum[...] * factor).astype(BF16)


def attention(length, allow, qg, owns, halos, text):
    width = qg.shape[-1]
    heads = width // PAIR
    text_count = text.shape[0]

    def spec(rows):
        return pl.BlockSpec((rows, PAIR), lambda h: (0, h))

    def shape(rows, dtype):
        return jax.ShapeDtypeStruct((rows, width), dtype)

    part = pl.BlockSpec((GROUP, CUBE, PAIR), lambda h: (0, 0, h))
    return pl.pallas_call(
        attention_kernel,
        grid=(heads,),
        in_specs=[
            pl.BlockSpec(memory_space=pltpu.SMEM),
            pl.BlockSpec(allow.shape, lambda h: (0, 0, 0)),
            part,
        ]
        + [spec(OWN)] * 3
        + [spec(HALO)] * 3
        + [spec(text_count)],
        out_specs=[part] + [spec(OWN)] * 3 + [spec(HALO)] * 3 + [spec(text_count)],
        out_shape=[
            jax.ShapeDtypeStruct(qg.shape, BF16),
            shape(OWN, F32),
            shape(OWN, BF16),
            shape(OWN, BF16),
            shape(HALO, F32),
            shape(HALO, BF16),
            shape(HALO, BF16),
            shape(text_count, F32),
        ],
        scratch_shapes=[pltpu.VMEM((rows, PAIR), F32) for rows in (OWN, OWN, HALO, HALO)],
        compiler_params=pltpu.CompilerParams(vmem_limit_bytes=VMEM),
    )(length, allow, qg, *owns, *halos, text)


def settle_kernel(half_ref, own_ref, first_ref, second_ref, rim_ref, left_ref, right_ref, text_ref, out_ref):
    block = pl.program_id(0)
    line = TILES_W * TILE
    total = own_ref[...] + first_ref[...].astype(F32) + second_ref[...].astype(F32)
    rim = rim_ref[:line, :].astype(F32)
    left = left_ref[...].astype(F32)
    right = right_ref[...].astype(F32)
    half = half_ref[0]
    for i in range(TILES_H):
        edge = (block == 0) & (half == 1) if i == 0 else (block == GROUP - 1) & (half == 0)
        part = total[i * line : (i + 1) * line]
        part += jnp.where(edge, rim, 0.0)
        here = slice(i * TILE, (i + 1) * TILE)
        pieces = [
            part[:TILE] + left[here],
            part[TILE : line - TILE],
            part[line - TILE :] + right[here],
        ]
        out_ref[0, i * line : (i + 1) * line, :] = jnp.concatenate(pieces, 0).astype(BF16)
    out_ref[0, CUBE:, :] = jnp.broadcast_to(text_ref[0], (EXTRA, out_ref.shape[2])).astype(BF16)


def settle(half, own, first, second, rim, left, right, text):
    width = own.shape[-1]

    def spec(rows):
        return pl.BlockSpec((rows, width), lambda b: (b, 0))

    return pl.pallas_call(
        settle_kernel,
        grid=(GROUP,),
        in_specs=[
            pl.BlockSpec(memory_space=pltpu.SMEM),
            spec(CUBE),
            spec(CUBE),
            spec(CUBE),
            pl.BlockSpec((RIM, width), lambda b: (0, 0)),
            spec(TILES_H * TILE),
            spec(TILES_H * TILE),
            pl.BlockSpec((1, 1, width), lambda b: (b, 0, 0)),
        ],
        out_specs=pl.BlockSpec((1, CUBE + EXTRA, width), lambda b: (b, 0, 0)),
        out_shape=jax.ShapeDtypeStruct((GROUP, CUBE + EXTRA, width), BF16),
        compiler_params=pltpu.CompilerParams(vmem_limit_bytes=VMEM),
    )(half, own, first, second, rim, left, right, text)


def offset_table():
    table = np.full((GROUP, 3, SEEN, TILES_H, TILES_W), -1, np.int32)
    for block in range(GROUP):
        for k, (kh, kw) in enumerate(seen_tiles(block)):
            for qh in range(TILES_H):
                for qw in range(TILES_W):
                    dh, dw = kh - (block * TILES_H + qh), kw - qw
                    if abs(dh) <= 1 and abs(dw) <= 1:
                        for i, dt in enumerate((0, -1, 1)):
                            table[block, i, k, qh, qw] = 9 * dt + 3 * dh + dw + 13
    return table


def allowed_tiles(pattern, half):
    hot = offset_table().reshape(GROUP, 3, SEEN, -1)[..., None] == np.arange(27)
    picked = jnp.sum(jnp.where(hot, pattern[:, None, None], 0.0), -1)
    places = np.array([seen_tiles(block) for block in range(GROUP)])
    t = lax.axis_index("ta") + jnp.array([0, -1, 1])
    t_ok = (t >= 0) & (t < lax.axis_size("ta"))
    w = lax.axis_index("wa") * TILES_W + places[..., 1]
    w_ok = (w >= 0) & (w < TILES_W * lax.axis_size("wa"))
    h = half * GROUP_H + places[..., 0]
    h_ok = (h >= 0) & (h < TILES_H * lax.axis_size("ha"))
    inside = t_ok[None, :, None] & (w_ok & h_ok)[:, None, :]
    picked = jnp.where(inside[..., None], picked, 0.0)
    return jnp.repeat(picked.reshape(GROUP, 3 * SEEN, -1), TILE, axis=2)


def turned_width(value, step):
    count = lax.axis_size("wa")
    return lax.ppermute(value, "wa", [(i, (i + step) % count) for i in range(count)])


def turned_time(value, step):
    count_t, count_h = lax.axis_size("ta"), lax.axis_size("ha")
    pairs = []
    for t in range(count_t):
        for h in range(count_h):
            t_to = t + step
            h_to = h
            if not 0 <= t_to < count_t:
                h_to = (h + count_h // 2) % count_h
            pairs.append((t * count_h + h, t_to % count_t * count_h + h_to))
    return lax.ppermute(value, ("ta", "ha"), pairs)


def swapped(value, axis, bit):
    count = lax.axis_size(axis)
    return lax.ppermute(value, axis, [(i, i ^ bit) for i in range(count)])


def regrouped(value):
    count = lax.axis_size("ha")
    groups = [list(range(i, i + GROUP)) for i in range(0, count, GROUP)]
    return lax.all_to_all(value, "ha", 0, 0, axis_index_groups=groups)


def text_steps():
    def bits(axis, start):
        bit = lax.axis_size(axis) // 2
        found = []
        while bit >= start:
            found.append((axis, bit))
            bit //= 2
        return found

    order = bits("ta", 1) + bits("ha", GROUP) + [None] + bits("wa", 1)
    taken = [step for step in bits("ta", 2)] + bits("ha", GROUP) + bits("wa", 1)[::-1] + [("ta", 1)]
    present = [None]
    steps = []
    for step in taken:
        place = sum(order.index(other) < order.index(step) for other in present)
        steps.append((*step, place))
        present.append(step)
    return steps


def text_shape():
    shape = [GROUP]
    for _, _, place in text_steps():
        shape.insert(place, 2)
    return tuple(shape)


def gathered_text(rows):
    width = rows.shape[-1]
    value = rows
    for axis, bit, place in text_steps():
        other = swapped(value, axis, bit)
        high = (lax.axis_index(axis) & bit) > 0
        first = jnp.where(high, other, value)
        second = jnp.where(high, value, other)
        value = jnp.stack([first, second], axis=place)
    return value.reshape(-1, width)


def halved_text(value, step):
    axis, bit, place = step
    high = (lax.axis_index(axis) & bit) > 0
    first = lax.index_in_dim(value, 0, place, keepdims=False)
    second = lax.index_in_dim(value, 1, place, keepdims=False)
    mine = jnp.where(high, second, first)
    theirs = jnp.where(high, first, second)
    return mine + swapped(theirs, axis, bit)


def after(value, *others):
    return lax.optimization_barrier((value, *others))[0]


def local(query, key, value, d_out, text_key, text_value, block_pattern, text_length):
    full = query.shape[-1]
    half = lax.axis_index("ha") // GROUP
    pattern = jnp.pad(block_pattern.reshape(8, 27).astype(F32), ((0, 0), (0, HEAD - 27)))
    kv_out = pack(
        key.reshape(CUBE, full),
        value.reshape(CUBE, full),
        GROUP,
        (pattern, text_key, text_value),
    )
    qg_out = pack(query.reshape(CUBE, full), d_out.reshape(CUBE, full), GROUP)
    kv_in = regrouped(kv_out)
    width = kv_in.shape[-1]
    own = kv_in[:, :CUBE].reshape(GROUP_H, TILES_W, TILE, width)
    from_left = turned_width(own[:, TILES_W - 1].reshape(SIDE, width), 1)
    from_right = turned_width(own[:, 0].reshape(SIDE, width), -1)
    flat = own.reshape(OWN, width)
    owns = [flat, turned_time(flat, 1), turned_time(flat, -1)]
    qg = regrouped(qg_out)
    text = gathered_text(kv_in[:, CUBE + 8])
    allow = allowed_tiles(kv_in[:, CUBE : CUBE + 8, :27].astype(F32), half)

    line = TILES_W * TILE

    def edge(rows, size):
        return jnp.where(half == 0, rows[(GROUP_H - 1) * size :], rows[:size])

    rim = jnp.concatenate([edge(flat, line), edge(from_left, TILE), edge(from_right, TILE)], 0)
    rim = swapped(rim, "ha", GROUP)
    halo = jnp.concatenate([from_left, from_right, rim], 0)
    halos = [halo, turned_time(halo, 1), turned_time(halo, -1)]
    (
        od,
        own_grad,
        own_below,
        own_above,
        halo_grad,
        halo_below,
        halo_above,
        text_grad,
    ) = attention(text_length, allow, qg, owns, halos, text)

    halo_first = turned_time(halo_below, -1)
    halo_second = turned_time(halo_above, 1)
    steps = text_steps()
    text_sum = text_grad.reshape(text_shape() + (width,))
    text_sum = halved_text(text_sum, steps[-1])
    text_sum = halved_text(text_sum, steps[-2])
    own_first = turned_time(after(own_below, halo_first, halo_second), -1)
    own_second = turned_time(after(own_above, halo_first, halo_second), 1)
    od_in = regrouped(od)
    attended, query_grad = unpack(od_in, False)
    halo_sum = halo_grad + halo_first.astype(F32) + halo_second.astype(F32)
    rim_in = swapped(halo_sum[2 * SIDE :].astype(BF16), "ha", GROUP)
    text_sum = after(text_sum, halo_first, halo_second)
    for step in steps[-3::-1]:
        text_sum = halved_text(text_sum, step)
    sides = halo_sum[: 2 * SIDE].reshape(2, GROUP_H, TILE, width)
    row = lax.broadcasted_iota(jnp.int32, (1, GROUP_H, 1, 1), 1)
    at_edge = row == jnp.where(half == 0, GROUP_H - 1, 0)
    extra = rim_in[line:].astype(F32).reshape(2, 1, TILE, width)
    sides = (sides + jnp.where(at_edge, extra, 0.0)).astype(BF16).reshape(2, SIDE, width)
    right = turned_width(sides[0], -1)
    left = turned_width(sides[1], 1)
    grads = settle(
        half.reshape(1),
        own_grad,
        own_first,
        own_second,
        rim_in,
        left,
        right,
        text_sum.reshape(GROUP, 1, width),
    )
    key_grad, value_grad, text_key_grad, text_value_grad = unpack(regrouped(grads), True)
    return (
        attended.reshape(query.shape),
        query_grad.reshape(query.shape),
        key_grad.reshape(query.shape),
        value_grad.reshape(query.shape),
        text_key_grad,
        text_value_grad,
    )


def solution(mesh):
    cube = P("ta", "ha", "wa", None)
    text = P(("ta", "ha", "wa"), None)
    return jax.shard_map(
        local,
        mesh=mesh,
        in_specs=(cube, cube, cube, cube, text, text, cube, P()),
        out_specs=(cube, cube, cube, cube, text, text),
        check_vma=False,
    )
```

```python
import functools

import jax
import jax.numpy as jnp
import numpy as np
from jax import lax
from jax.experimental import pallas as pl
from jax.experimental.pallas import tpu as pltpu
from jax.sharding import PartitionSpec as P

HEAD = 128
PAIR = 2 * HEAD
TILE_T = 2
TILE_H = 2
TILE_W = 4
TILE = TILE_T * TILE_H * TILE_W
NEGATIVE = -1e30
LOG2E = 1.4426950408889634
EXTRA = 16
PACKS = 2
VMEM = 58 * 1024 * 1024
F32 = jnp.float32
BF16 = jnp.bfloat16

ROWS = 4
COLS = 16
TILES_H = ROWS // TILE_H
TILES_W = COLS // TILE_W
CUBE = TILE_T * ROWS * COLS
GROUP = 4
GROUP_H = GROUP * TILES_H
OWN = GROUP_H * TILES_W * TILE
SIDE = GROUP_H * TILE
RIM = (TILES_W + 2) * TILE
HALO = 2 * SIDE + RIM
SEEN = (TILES_H + 2) * (TILES_W + 2)


def natural_index(row):
    tile_h = row >> 6
    tile_w = (row >> 4) & 3
    t = (row >> 3) & 1
    h = (row >> 2) & 1
    w = row & 3
    return t * (ROWS * COLS) + (tile_h * TILE_H + h) * COLS + tile_w * TILE_W + w


def pack_kernel(first_ref, second_ref, *rest):
    out_ref = rest[-1]
    row = lax.broadcasted_iota(jnp.int32, (CUBE, CUBE), 0)
    col = lax.broadcasted_iota(jnp.int32, (CUBE, CUBE), 1)
    order = jnp.where(natural_index(row) == col, 1.0, 0.0).astype(BF16)
    first = jnp.dot(order, first_ref[...], preferred_element_type=F32).astype(BF16)
    second = jnp.dot(order, second_ref[...], preferred_element_type=F32).astype(BF16)
    groups, _, width = out_ref.shape
    heads = width // PAIR
    for group in range(groups):
        for i in range(heads):
            source = slice((group * heads + i) * HEAD, (group * heads + i + 1) * HEAD)
            out_ref[group, :CUBE, i * PAIR : i * PAIR + HEAD] = first[:, source]
            out_ref[group, :CUBE, i * PAIR + HEAD : (i + 1) * PAIR] = second[:, source]
        if len(rest) > 1:
            pattern = rest[0][...].astype(F32)
            lines = jnp.concatenate([pattern, jnp.zeros_like(pattern)], 0).astype(BF16)
            out_ref[group, CUBE:, :] = jnp.zeros((EXTRA, width), BF16)
            out_ref[group, CUBE:, : pattern.shape[1]] = lines


def pack(first, second, pattern=None):
    width = first.shape[1] // GROUP
    step = GROUP // PACKS
    rows = CUBE + (0 if pattern is None else EXTRA)
    specs = [pl.BlockSpec((CUBE, width * step), lambda g: (0, g))] * 2
    extras = ()
    if pattern is not None:
        specs.append(pl.BlockSpec(pattern.shape, lambda g: (0, 0)))
        extras = (pattern,)
    return pl.pallas_call(
        pack_kernel,
        grid=(PACKS,),
        in_specs=specs,
        out_specs=pl.BlockSpec((step, rows, 2 * width), lambda g: (g, 0, 0)),
        out_shape=jax.ShapeDtypeStruct((GROUP, rows, 2 * width), BF16),
        compiler_params=pltpu.CompilerParams(vmem_limit_bytes=VMEM),
    )(first, second, *extras)


def unpack_kernel(packed_ref, first_ref, second_ref):
    row = lax.broadcasted_iota(jnp.int32, (CUBE, CUBE), 0)
    col = lax.broadcasted_iota(jnp.int32, (CUBE, CUBE), 1)
    order = jnp.where(natural_index(col) == row, 1.0, 0.0).astype(BF16)
    groups, _, width = packed_ref.shape
    heads = width // PAIR
    for group in range(groups):
        both = jnp.dot(order, packed_ref[group], preferred_element_type=F32).astype(BF16)
        for i in range(heads):
            target = slice((group * heads + i) * HEAD, (group * heads + i + 1) * HEAD)
            first_ref[:, target] = both[:, i * PAIR : i * PAIR + HEAD]
            second_ref[:, target] = both[:, i * PAIR + HEAD : (i + 1) * PAIR]


def unpack(packed):
    _, rows, width = packed.shape
    step = GROUP // PACKS
    half = width // 2
    return pl.pallas_call(
        unpack_kernel,
        grid=(PACKS,),
        in_specs=[pl.BlockSpec((step, rows, width), lambda g: (g, 0, 0))],
        out_specs=[pl.BlockSpec((CUBE, half * step), lambda g: (0, g))] * 2,
        out_shape=[jax.ShapeDtypeStruct((CUBE, GROUP * half), BF16)] * 2,
        compiler_params=pltpu.CompilerParams(vmem_limit_bytes=VMEM),
    )(packed)


def block_rows(block):
    low, high = block * TILES_H - 1, (block + 1) * TILES_H + 1
    outer = -1 if low < 0 else GROUP_H if high > GROUP_H else None
    return max(low, 0), min(high, GROUP_H), outer


def seen_tiles(block):
    low, high, outer = block_rows(block)
    tiles = [(h, w) for h in range(low, high) for w in range(TILES_W)]
    tiles += [(h, -1) for h in range(low, high)] + [(h, TILES_W) for h in range(low, high)]
    if outer is not None:
        tiles += [(outer, w) for w in (*range(TILES_W), -1, TILES_W)]
    return tiles


def attention_kernel(
    text_bits,
    length_ref,
    allow_ref,
    qg_ref,
    own_ref,
    own_below_ref,
    own_above_ref,
    halo_ref,
    halo_below_ref,
    halo_above_ref,
    text_ref,
    od_ref,
    own_out,
    own_below_out,
    own_above_out,
    halo_out,
    halo_below_out,
    halo_above_out,
    text_out,
    own_below_sum,
    own_above_sum,
    halo_below_sum,
    halo_above_sum,
):
    text_count = text_ref.shape[0]
    scale = HEAD**-0.5
    owns = (own_ref, own_below_ref, own_above_ref)
    halos = (halo_ref, halo_below_ref, halo_above_ref)
    own_sums = (own_out, own_below_sum, own_above_sum)
    halo_sums = (halo_out, halo_below_sum, halo_above_sum)
    text_row = lax.broadcasted_iota(jnp.int32, (text_count, CUBE), 0)
    text_place = jnp.zeros_like(text_row)
    for bit, place in enumerate(text_bits):
        text_place += ((text_row >> bit) & 1) << place
    text_ok = text_place < length_ref[0]
    blank = jnp.zeros((CUBE, HEAD), BF16)
    text_kv = text_ref[...]
    line = TILES_W * TILE
    for block in range(GROUP):
        low, high, outer = block_rows(block)
        count = high - low
        q = qg_ref[block, :, :HEAD]
        g = qg_ref[block, :, HEAD:]
        both = jnp.concatenate(
            [jnp.concatenate([q, blank], 1), jnp.concatenate([blank, g], 1)], 0
        )
        done = 0 if block == 0 else 2
        places = [(False, low * line, count * line, done * line)]
        for side in range(2):
            places.append((True, side * SIDE + low * TILE, count * TILE, done * TILE))
        if outer is not None:
            places.append((True, 2 * SIDE, RIM, 0 if block == 0 else RIM))
        keys = []
        masks = []
        for i in range(3):
            parts = [
                (halos if in_halo else owns)[i][first : first + size, :]
                for in_halo, first, size, _ in places
            ]
            keys.append(jnp.concatenate(parts, 0))
            tiles = allow_ref[block, i * SEEN : (i + 1) * SEEN, :]
            spread = jnp.broadcast_to(tiles[:, None, :], (SEEN, TILE, CUBE))
            masks.append(spread.reshape(SEEN * TILE, CUBE) > 0.5)
        keys.append(text_kv)
        masks.append(text_ok)
        scores = []
        dprobs = []
        for kv, ok in zip(keys, masks):
            mixed = lax.dot_general(
                kv, both, (((1,), (1,)), ((), ())), preferred_element_type=F32
            )
            scores.append(jnp.where(ok, mixed[:, :HEAD] * (scale * LOG2E), NEGATIVE))
            dprobs.append(mixed[:, HEAD:])
        top = functools.reduce(jnp.maximum, [jnp.max(s, 0, keepdims=True) for s in scores])
        exps = [jnp.exp2(s - top) for s in scores]
        total = functools.reduce(jnp.add, [jnp.sum(e, 0, keepdims=True) for e in exps])
        inverse = 1.0 / total
        weights = [(e * inverse).astype(BF16) for e in exps]
        attended = jnp.zeros((CUBE, HEAD), F32)
        for w, kv in zip(weights, keys):
            attended += lax.dot_general(
                w, kv[:, HEAD:], (((0,), (0,)), ((), ())), preferred_element_type=F32
            )
        attended = attended.astype(BF16)
        od_ref[block, :, :HEAD] = attended
        product = g.astype(F32) * attended.astype(F32)
        delta = jnp.sum(product.T, 0, keepdims=True)
        dscores = [(e * ((d - delta) * inverse)).astype(BF16) for e, d in zip(exps, dprobs)]
        query_grad = jnp.zeros((CUBE, HEAD), F32)
        for d, kv in zip(dscores, keys):
            query_grad += lax.dot_general(
                d, kv[:, :HEAD], (((0,), (0,)), ((), ())), preferred_element_type=F32
            )
        od_ref[block, :, HEAD:] = (query_grad * scale).astype(BF16)
        for i in range(4):
            change = jnp.dot(
                jnp.concatenate([dscores[i], weights[i]], 1), both, preferred_element_type=F32
            )
            if i == 3:
                if block == 0:
                    text_out[...] = change
                else:
                    text_out[...] += change
                continue
            taken = 0
            for in_halo, first, size, old in places:
                target = (halo_sums if in_halo else own_sums)[i]
                if old:
                    target[first : first + old, :] += change[taken : taken + old]
                if old < size:
                    target[first + old : first + size, :] = change[taken + old : taken + size]
                taken += size
    lane = lax.broadcasted_iota(jnp.int32, (1, PAIR), 1)
    factor = jnp.where(lane < HEAD, scale, 1.0).astype(F32)
    own_out[...] = own_out[...] * factor
    halo_out[...] = halo_out[...] * factor
    text_out[...] = text_out[...] * factor
    own_below_out[...] = (own_below_sum[...] * factor).astype(BF16)
    own_above_out[...] = (own_above_sum[...] * factor).astype(BF16)
    halo_below_out[...] = (halo_below_sum[...] * factor).astype(BF16)
    halo_above_out[...] = (halo_above_sum[...] * factor).astype(BF16)


def attention(length, allow, qg, owns, halos, text, text_bits):
    width = qg.shape[-1]
    heads = width // PAIR
    text_count = text.shape[0]

    def spec(rows):
        return pl.BlockSpec((rows, PAIR), lambda h: (0, h))

    def shape(rows, dtype):
        return jax.ShapeDtypeStruct((rows, width), dtype)

    part = pl.BlockSpec((GROUP, CUBE, PAIR), lambda h: (0, 0, h))
    return pl.pallas_call(
        functools.partial(attention_kernel, text_bits),
        grid=(heads,),
        in_specs=[
            pl.BlockSpec(memory_space=pltpu.SMEM),
            pl.BlockSpec(allow.shape, lambda h: (0, 0, 0)),
            part,
        ]
        + [spec(OWN)] * 3
        + [spec(HALO)] * 3
        + [spec(text_count)],
        out_specs=[part] + [spec(OWN)] * 3 + [spec(HALO)] * 3 + [spec(text_count)],
        out_shape=[
            jax.ShapeDtypeStruct(qg.shape, BF16),
            shape(OWN, F32),
            shape(OWN, BF16),
            shape(OWN, BF16),
            shape(HALO, F32),
            shape(HALO, BF16),
            shape(HALO, BF16),
            shape(text_count, F32),
        ],
        scratch_shapes=[pltpu.VMEM((rows, PAIR), F32) for rows in (OWN, OWN, HALO, HALO)],
        compiler_params=pltpu.CompilerParams(vmem_limit_bytes=VMEM),
    )(length, allow, qg, *owns, *halos, text)


def settle_kernel(half_ref, own_ref, first_ref, second_ref, rim_ref, left_ref, right_ref, out_ref):
    block = pl.program_id(0)
    line = TILES_W * TILE
    total = own_ref[...] + first_ref[...].astype(F32) + second_ref[...].astype(F32)
    rim = rim_ref[:line, :].astype(F32)
    left = left_ref[...].astype(F32)
    right = right_ref[...].astype(F32)
    half = half_ref[0]
    for i in range(TILES_H):
        edge = (block == 0) & (half == 1) if i == 0 else (block == GROUP - 1) & (half == 0)
        part = total[i * line : (i + 1) * line]
        part += jnp.where(edge, rim, 0.0)
        here = slice(i * TILE, (i + 1) * TILE)
        pieces = [
            part[:TILE] + left[here],
            part[TILE : line - TILE],
            part[line - TILE :] + right[here],
        ]
        out_ref[0, i * line : (i + 1) * line, :] = jnp.concatenate(pieces, 0).astype(BF16)


def settle(half, own, first, second, rim, left, right):
    width = own.shape[-1]

    def spec(rows):
        return pl.BlockSpec((rows, width), lambda b: (b, 0))

    return pl.pallas_call(
        settle_kernel,
        grid=(GROUP,),
        in_specs=[
            pl.BlockSpec(memory_space=pltpu.SMEM),
            spec(CUBE),
            spec(CUBE),
            spec(CUBE),
            pl.BlockSpec((RIM, width), lambda b: (0, 0)),
            spec(TILES_H * TILE),
            spec(TILES_H * TILE),
        ],
        out_specs=pl.BlockSpec((1, CUBE, width), lambda b: (b, 0, 0)),
        out_shape=jax.ShapeDtypeStruct((GROUP, CUBE, width), BF16),
        compiler_params=pltpu.CompilerParams(vmem_limit_bytes=VMEM),
    )(half, own, first, second, rim, left, right)


def offset_table():
    table = np.full((GROUP, 3, SEEN, TILES_H, TILES_W), -1, np.int32)
    for block in range(GROUP):
        for k, (kh, kw) in enumerate(seen_tiles(block)):
            for qh in range(TILES_H):
                for qw in range(TILES_W):
                    dh, dw = kh - (block * TILES_H + qh), kw - qw
                    if abs(dh) <= 1 and abs(dw) <= 1:
                        for i, dt in enumerate((0, -1, 1)):
                            table[block, i, k, qh, qw] = 9 * dt + 3 * dh + dw + 13
    return table


def allowed_tiles(pattern, half):
    hot = offset_table().reshape(GROUP, 3, SEEN, -1)[..., None] == np.arange(27)
    picked = jnp.sum(jnp.where(hot, pattern[:, None, None], 0.0), -1)
    places = np.array([seen_tiles(block) for block in range(GROUP)])
    t = lax.axis_index("ta") + jnp.array([0, -1, 1])
    t_ok = (t >= 0) & (t < lax.axis_size("ta"))
    w = lax.axis_index("wa") * TILES_W + places[..., 1]
    w_ok = (w >= 0) & (w < TILES_W * lax.axis_size("wa"))
    h = half * GROUP_H + places[..., 0]
    h_ok = (h >= 0) & (h < TILES_H * lax.axis_size("ha"))
    inside = t_ok[None, :, None] & (w_ok & h_ok)[:, None, :]
    picked = jnp.where(inside[..., None], picked, 0.0)
    return jnp.repeat(picked.reshape(GROUP, 3 * SEEN, -1), TILE, axis=2)


def turned_width(value, step):
    count = lax.axis_size("wa")
    return lax.ppermute(value, "wa", [(i, (i + step) % count) for i in range(count)])


def turned_time(value, step):
    count_t, count_h = lax.axis_size("ta"), lax.axis_size("ha")
    pairs = []
    for t in range(count_t):
        for h in range(count_h):
            t_to = t + step
            h_to = h
            if not 0 <= t_to < count_t:
                h_to = (h + count_h // 2) % count_h
            pairs.append((t * count_h + h, t_to % count_t * count_h + h_to))
    return lax.ppermute(value, ("ta", "ha"), pairs)


def swapped(value, axis, bit):
    count = lax.axis_size(axis)
    return lax.ppermute(value, axis, [(i, i ^ bit) for i in range(count)])


def regrouped(value):
    count = lax.axis_size("ha")
    groups = [list(range(i, i + GROUP)) for i in range(0, count, GROUP)]
    return lax.all_to_all(value, "ha", 0, 0, axis_index_groups=groups)


def log2(count):
    return count.bit_length() - 1


def text_steps():
    ta, ha, wa = (lax.axis_size(axis) for axis in ("ta", "ha", "wa"))
    steps = [("ta", ta >> i) for i in range(1, log2(ta))]
    steps += [("ha", ha >> i) for i in range(1, log2(ha) + 1)]
    steps += [("wa", wa >> i) for i in range(1, log2(wa) + 1)]
    return steps + [("ta", 1)]


def text_bits():
    start = {"wa": 0, "ha": log2(lax.axis_size("wa"))}
    start["ta"] = start["ha"] + log2(lax.axis_size("ha"))
    return tuple(start[axis] + log2(bit) for axis, bit in text_steps())


def is_high(axis, bit):
    return (lax.axis_index(axis) & bit) > 0


def gather_text(value, axis, bit):
    high = is_high(axis, bit)
    if axis == "ha" and bit < GROUP:
        middle = value.shape[0] // 2
        mine = jnp.where(high, value[middle:], value[:middle])
        theirs = jnp.where(high, value[:middle], value[middle:])
    else:
        mine = theirs = value
    other = swapped(theirs, axis, bit)
    first = jnp.where(high, other, mine)
    second = jnp.where(high, mine, other)
    return jnp.concatenate([first, second], 1)


def scatter_text(value, axis, bit):
    high = is_high(axis, bit)
    middle = value.shape[1] // 2
    mine = jnp.where(high, value[:, middle:], value[:, :middle])
    theirs = jnp.where(high, value[:, :middle], value[:, middle:])
    other = swapped(theirs, axis, bit)
    if axis == "ha" and bit < GROUP:
        first = jnp.where(high, other, mine)
        second = jnp.where(high, mine, other)
        return jnp.concatenate([first, second], 0)
    return mine + other


def after(value, *others):
    return lax.optimization_barrier((value, *others))[0]


def local(query, key, value, d_out, text_key, text_value, block_pattern, text_length):
    full = query.shape[-1]
    half = lax.axis_index("ha") // GROUP
    steps = text_steps()
    line = TILES_W * TILE

    def edge(rows, size):
        return jnp.where(half == 0, rows[(GROUP_H - 1) * size :], rows[:size])

    text = jnp.stack([text_key.reshape(-1, HEAD), text_value.reshape(-1, HEAD)], 1)
    text = gather_text(text.reshape(GROUP, 1, -1), *steps[0])
    kv_out = pack(
        key.reshape(CUBE, full), value.reshape(CUBE, full), block_pattern.reshape(-1, 27)
    )
    qg_out = pack(query.reshape(CUBE, full), d_out.reshape(CUBE, full))
    kv_out = after(kv_out, text)
    text = gather_text(after(text, kv_out), *steps[1])
    text = gather_text(after(text, qg_out), *steps[2])
    kv_in = after(regrouped(kv_out), text)
    width = kv_in.shape[-1]

    own = kv_in[:, :CUBE].reshape(GROUP_H, TILES_W, TILE, width)
    from_left = turned_width(own[:, TILES_W - 1].reshape(SIDE, width), 1)
    from_right = turned_width(own[:, 0].reshape(SIDE, width), -1)
    flat = own.reshape(OWN, width)
    owns = [flat, turned_time(flat, 1), turned_time(flat, -1)]
    qg = regrouped(qg_out)
    text = gather_text(after(text, kv_in), *steps[3])
    rim = jnp.concatenate([edge(flat, line), edge(from_left, TILE), edge(from_right, TILE)], 0)
    rim = swapped(rim, "ha", GROUP)
    text = gather_text(after(text, from_left, from_right), *steps[4])
    halo = jnp.concatenate([from_left, from_right, rim], 0)
    halos = [halo, turned_time(halo, 1), turned_time(halo, -1)]
    text = after(text, rim)
    for step in steps[5:]:
        text = gather_text(text, *step)
    allow = allowed_tiles(kv_in[:, CUBE : CUBE + 8, :27].astype(F32), half)

    (
        od,
        own_grad,
        own_below,
        own_above,
        halo_grad,
        halo_below,
        halo_above,
        text_grad,
    ) = attention(text_length, allow, qg, owns, halos, text[0], text_bits())

    halo_first = turned_time(halo_below, -1)
    halo_second = turned_time(halo_above, 1)
    back = steps[::-1]
    text_grad = scatter_text(text_grad[None], *back[0])
    text_grad = scatter_text(text_grad, *back[1])
    od_in = regrouped(od)
    own_first = turned_time(after(own_below, halo_first, halo_second), -1)
    own_second = turned_time(after(own_above, halo_first, halo_second), 1)
    halo_sum = halo_grad + halo_first.astype(F32) + halo_second.astype(F32)
    rim_in = swapped(halo_sum[2 * SIDE :].astype(BF16), "ha", GROUP)
    text_grad = scatter_text(after(text_grad, halo_first, halo_second), *back[2])
    sides = halo_sum[: 2 * SIDE].reshape(2, GROUP_H, TILE, width)
    row = lax.broadcasted_iota(jnp.int32, (1, GROUP_H, 1, 1), 1)
    at_edge = row == jnp.where(half == 0, GROUP_H - 1, 0)
    extra = rim_in[line:].astype(F32).reshape(2, 1, TILE, width)
    sides = (sides + jnp.where(at_edge, extra, 0.0)).astype(BF16).reshape(2, SIDE, width)
    right = turned_width(sides[0], -1)
    left = turned_width(sides[1], 1)
    text_grad = scatter_text(after(text_grad, rim_in, od_in), *back[3])
    grads = settle(half.reshape(1), own_grad, own_first, own_second, rim_in, left, right)
    text_grad = after(text_grad, own_first, own_second)
    for step in back[4:]:
        text_grad = scatter_text(text_grad, *step)
    attended, query_grad = unpack(od_in)
    key_grad, value_grad = unpack(regrouped(grads))
    text_grad = text_grad.astype(BF16).reshape(-1, 2, HEAD)
    return (
        attended.reshape(query.shape),
        query_grad.reshape(query.shape),
        key_grad.reshape(query.shape),
        value_grad.reshape(query.shape),
        text_grad[:, 0].reshape(1, full),
        text_grad[:, 1].reshape(1, full),
    )


def solution(mesh):
    cube = P("ta", "ha", "wa", None)
    text = P(("ta", "ha", "wa"), None)
    return jax.shard_map(
        local,
        mesh=mesh,
        in_specs=(cube, cube, cube, cube, text, text, cube, P()),
        out_specs=(cube, cube, cube, cube, text, text),
        check_vma=False,
    )
```

```python
import functools

import jax
import jax.numpy as jnp
import numpy as np
from jax import lax
from jax.experimental import pallas as pl
from jax.experimental.pallas import tpu as pltpu
from jax.sharding import PartitionSpec as P

HEAD = 128
PAIR = 2 * HEAD
TILE_T = 2
TILE_H = 2
TILE_W = 4
TILE = TILE_T * TILE_H * TILE_W
NEGATIVE = -1e30
LOG2E = 1.4426950408889634
EXTRA = 16
PACKS = 2
VMEM = 58 * 1024 * 1024
F32 = jnp.float32
BF16 = jnp.bfloat16

ROWS = 4
COLS = 16
TILES_H = ROWS // TILE_H
TILES_W = COLS // TILE_W
CUBE = TILE_T * ROWS * COLS
GROUP = 4
GROUP_H = GROUP * TILES_H
OWN = GROUP_H * TILES_W * TILE
SIDE = GROUP_H * TILE
RIM = (TILES_W + 2) * TILE
HALO = 2 * SIDE + RIM
SEEN = (TILES_H + 2) * (TILES_W + 2)


def natural_index(row):
    tile_h = row >> 6
    tile_w = (row >> 4) & 3
    t = (row >> 3) & 1
    h = (row >> 2) & 1
    w = row & 3
    return t * (ROWS * COLS) + (tile_h * TILE_H + h) * COLS + tile_w * TILE_W + w


def pack_kernel(first_ref, second_ref, *rest):
    out_ref = rest[-1]
    row = lax.broadcasted_iota(jnp.int32, (CUBE, CUBE), 0)
    col = lax.broadcasted_iota(jnp.int32, (CUBE, CUBE), 1)
    order = jnp.where(natural_index(row) == col, 1.0, 0.0).astype(BF16)
    first = jnp.dot(order, first_ref[...], preferred_element_type=F32).astype(BF16)
    second = jnp.dot(order, second_ref[...], preferred_element_type=F32).astype(BF16)
    groups, _, width = out_ref.shape
    heads = width // PAIR
    for group in range(groups):
        for i in range(heads):
            source = slice((group * heads + i) * HEAD, (group * heads + i + 1) * HEAD)
            out_ref[group, :CUBE, i * PAIR : i * PAIR + HEAD] = first[:, source]
            out_ref[group, :CUBE, i * PAIR + HEAD : (i + 1) * PAIR] = second[:, source]
        if len(rest) > 1:
            pattern = rest[0][...].astype(F32)
            lines = jnp.concatenate([pattern, jnp.zeros_like(pattern)], 0).astype(BF16)
            out_ref[group, CUBE:, :] = jnp.zeros((EXTRA, width), BF16)
            out_ref[group, CUBE:, : pattern.shape[1]] = lines


def pack(first, second, pattern=None):
    width = first.shape[1] // GROUP
    step = GROUP // PACKS
    rows = CUBE + (0 if pattern is None else EXTRA)
    specs = [pl.BlockSpec((CUBE, width * step), lambda g: (0, g))] * 2
    extras = ()
    if pattern is not None:
        specs.append(pl.BlockSpec(pattern.shape, lambda g: (0, 0)))
        extras = (pattern,)
    return pl.pallas_call(
        pack_kernel,
        grid=(PACKS,),
        in_specs=specs,
        out_specs=pl.BlockSpec((step, rows, 2 * width), lambda g: (g, 0, 0)),
        out_shape=jax.ShapeDtypeStruct((GROUP, rows, 2 * width), BF16),
        compiler_params=pltpu.CompilerParams(vmem_limit_bytes=VMEM),
    )(first, second, *extras)


def unpack_kernel(packed_ref, first_ref, second_ref):
    row = lax.broadcasted_iota(jnp.int32, (CUBE, CUBE), 0)
    col = lax.broadcasted_iota(jnp.int32, (CUBE, CUBE), 1)
    order = jnp.where(natural_index(col) == row, 1.0, 0.0).astype(BF16)
    groups, _, width = packed_ref.shape
    heads = width // PAIR
    for group in range(groups):
        both = jnp.dot(order, packed_ref[group], preferred_element_type=F32).astype(BF16)
        for i in range(heads):
            target = slice((group * heads + i) * HEAD, (group * heads + i + 1) * HEAD)
            first_ref[:, target] = both[:, i * PAIR : i * PAIR + HEAD]
            second_ref[:, target] = both[:, i * PAIR + HEAD : (i + 1) * PAIR]


def unpack(packed):
    _, rows, width = packed.shape
    step = GROUP // PACKS
    half = width // 2
    return pl.pallas_call(
        unpack_kernel,
        grid=(PACKS,),
        in_specs=[pl.BlockSpec((step, rows, width), lambda g: (g, 0, 0))],
        out_specs=[pl.BlockSpec((CUBE, half * step), lambda g: (0, g))] * 2,
        out_shape=[jax.ShapeDtypeStruct((CUBE, GROUP * half), BF16)] * 2,
        compiler_params=pltpu.CompilerParams(vmem_limit_bytes=VMEM),
    )(packed)


def block_rows(block):
    low, high = block * TILES_H - 1, (block + 1) * TILES_H + 1
    outer = -1 if low < 0 else GROUP_H if high > GROUP_H else None
    return max(low, 0), min(high, GROUP_H), outer


def seen_tiles(block):
    low, high, outer = block_rows(block)
    tiles = [(h, w) for h in range(low, high) for w in range(TILES_W)]
    tiles += [(h, -1) for h in range(low, high)] + [(h, TILES_W) for h in range(low, high)]
    if outer is not None:
        tiles += [(outer, w) for w in (*range(TILES_W), -1, TILES_W)]
    return tiles


def attention_kernel(
    text_bits,
    length_ref,
    allow_ref,
    qg_ref,
    own_ref,
    own_below_ref,
    own_above_ref,
    halo_ref,
    halo_below_ref,
    halo_above_ref,
    text_ref,
    od_ref,
    own_out,
    own_below_out,
    own_above_out,
    halo_out,
    halo_below_out,
    halo_above_out,
    text_out,
    text_away_out,
    own_below_sum,
    own_above_sum,
    halo_below_sum,
    halo_above_sum,
):
    text_count = text_ref.shape[0]
    scale = HEAD**-0.5
    owns = (own_ref, own_below_ref, own_above_ref)
    halos = (halo_ref, halo_below_ref, halo_above_ref)
    own_sums = (own_out, own_below_sum, own_above_sum)
    halo_sums = (halo_out, halo_below_sum, halo_above_sum)
    text_row = lax.broadcasted_iota(jnp.int32, (text_count, CUBE), 0)
    text_place = jnp.zeros_like(text_row)
    for bit, place in enumerate(text_bits):
        text_place += ((text_row >> bit) & 1) << place
    text_ok = (text_place ^ length_ref[1]) < length_ref[0]
    blank = jnp.zeros((CUBE, HEAD), BF16)
    text_kv = text_ref[...]
    line = TILES_W * TILE
    def look(block):
        low, high, outer = block_rows(block)
        count = high - low
        q = qg_ref[block, :, :HEAD]
        g = qg_ref[block, :, HEAD:]
        both = jnp.concatenate(
            [jnp.concatenate([q, blank], 1), jnp.concatenate([blank, g], 1)], 0
        )
        done = 0 if block == 0 else 2
        places = [(False, low * line, count * line, done * line)]
        for side in range(2):
            places.append((True, side * SIDE + low * TILE, count * TILE, done * TILE))
        if outer is not None:
            places.append((True, 2 * SIDE, RIM, 0 if block == 0 else RIM))
        keys = []
        masks = []
        for i in range(3):
            parts = [
                (halos if in_halo else owns)[i][first : first + size, :]
                for in_halo, first, size, _ in places
            ]
            keys.append(jnp.concatenate(parts, 0))
            tiles = allow_ref[block, i * SEEN : (i + 1) * SEEN, :]
            spread = jnp.broadcast_to(tiles[:, None, :], (SEEN, TILE, CUBE))
            masks.append(spread.reshape(SEEN * TILE, CUBE) > 0.5)
        keys.append(text_kv)
        masks.append(text_ok)
        scores = []
        dprobs = []
        for kv, ok in zip(keys, masks):
            mixed = lax.dot_general(
                kv, both, (((1,), (1,)), ((), ())), preferred_element_type=F32
            )
            scores.append(jnp.where(ok, mixed[:, :HEAD] * (scale * LOG2E), NEGATIVE))
            dprobs.append(mixed[:, HEAD:])
        top = functools.reduce(jnp.maximum, [jnp.max(s, 0, keepdims=True) for s in scores])
        return g, both, places, keys, scores, dprobs, top

    def finish(block, found):
        g, both, places, keys, scores, dprobs, top = found
        exps = [jnp.exp2(s - top) for s in scores]
        total = functools.reduce(jnp.add, [jnp.sum(e, 0, keepdims=True) for e in exps])
        inverse = 1.0 / total
        weights = [(e * inverse).astype(BF16) for e in exps]
        attended = jnp.zeros((CUBE, HEAD), F32)
        for w, kv in zip(weights, keys):
            attended += lax.dot_general(
                w, kv[:, HEAD:], (((0,), (0,)), ((), ())), preferred_element_type=F32
            )
        attended = attended.astype(BF16)
        od_ref[block, :, :HEAD] = attended
        product = g.astype(F32) * attended.astype(F32)
        delta = jnp.sum(product.T, 0, keepdims=True)
        dscores = [(e * ((d - delta) * inverse)).astype(BF16) for e, d in zip(exps, dprobs)]
        return both, places, keys, weights, dscores

    def settle_block(block, state):
        both, places, keys, weights, dscores = state
        query_grad = jnp.zeros((CUBE, HEAD), F32)
        for d, kv in zip(dscores, keys):
            query_grad += lax.dot_general(
                d, kv[:, :HEAD], (((0,), (0,)), ((), ())), preferred_element_type=F32
            )
        od_ref[block, :, HEAD:] = (query_grad * scale).astype(BF16)
        for i in range(4):
            change = jnp.dot(
                jnp.concatenate([dscores[i], weights[i]], 1), both, preferred_element_type=F32
            )
            if i == 3:
                middle = text_count // 2
                for target, piece in (
                    (text_out, change[:middle]),
                    (text_away_out, change[middle:]),
                ):
                    if block == 0:
                        target[...] = piece
                    else:
                        target[...] += piece
                continue
            taken = 0
            for in_halo, first, size, old in places:
                target = (halo_sums if in_halo else own_sums)[i]
                if old:
                    target[first : first + old, :] += change[taken : taken + old]
                if old < size:
                    target[first + old : first + size, :] = change[taken + old : taken + size]
                taken += size
    found = look(0)
    before = None
    for block in range(GROUP):
        following = look(block + 1) if block + 1 < GROUP else None
        now = finish(block, found)
        if before is not None:
            settle_block(block - 1, before)
        before = now
        found = following
    settle_block(GROUP - 1, before)
    lane = lax.broadcasted_iota(jnp.int32, (1, PAIR), 1)
    factor = jnp.where(lane < HEAD, scale, 1.0).astype(F32)
    own_out[...] = own_out[...] * factor
    halo_out[...] = halo_out[...] * factor
    text_out[...] = text_out[...] * factor
    text_away_out[...] = text_away_out[...] * factor
    own_below_out[...] = (own_below_sum[...] * factor).astype(BF16)
    own_above_out[...] = (own_above_sum[...] * factor).astype(BF16)
    halo_below_out[...] = (halo_below_sum[...] * factor).astype(BF16)
    halo_above_out[...] = (halo_above_sum[...] * factor).astype(BF16)


def attention(length, allow, qg, owns, halos, text, text_bits):
    width = qg.shape[-1]
    heads = width // PAIR
    text_count = text.shape[0]

    def spec(rows):
        return pl.BlockSpec((rows, PAIR), lambda h: (0, h))

    def shape(rows, dtype):
        return jax.ShapeDtypeStruct((rows, width), dtype)

    part = pl.BlockSpec((GROUP, CUBE, PAIR), lambda h: (0, 0, h))
    return pl.pallas_call(
        functools.partial(attention_kernel, text_bits),
        grid=(heads,),
        in_specs=[
            pl.BlockSpec(memory_space=pltpu.SMEM),
            pl.BlockSpec(allow.shape, lambda h: (0, 0, 0)),
            part,
        ]
        + [spec(OWN)] * 3
        + [spec(HALO)] * 3
        + [spec(text_count)],
        out_specs=[part] + [spec(OWN)] * 3 + [spec(HALO)] * 3 + [spec(text_count // 2)] * 2,
        out_shape=[
            jax.ShapeDtypeStruct(qg.shape, BF16),
            shape(OWN, F32),
            shape(OWN, BF16),
            shape(OWN, BF16),
            shape(HALO, F32),
            shape(HALO, BF16),
            shape(HALO, BF16),
            shape(text_count // 2, F32),
            shape(text_count // 2, F32),
        ],
        scratch_shapes=[pltpu.VMEM((rows, PAIR), F32) for rows in (OWN, OWN, HALO, HALO)],
        compiler_params=pltpu.CompilerParams(vmem_limit_bytes=VMEM),
    )(length, allow, qg, *owns, *halos, text)


def settle_kernel(half_ref, own_ref, first_ref, second_ref, rim_ref, left_ref, right_ref, out_ref):
    line = TILES_W * TILE
    rim = rim_ref[:line, :].astype(F32)
    half = half_ref[0]
    groups = out_ref.shape[0]
    for group in range(groups):
        block = pl.program_id(0) * groups + group
        cube = slice(group * CUBE, (group + 1) * CUBE)
        total = own_ref[cube] + first_ref[cube].astype(F32) + second_ref[cube].astype(F32)
        for i in range(TILES_H):
            edge = (block == 0) & (half == 1) if i == 0 else (block == GROUP - 1) & (half == 0)
            part = total[i * line : (i + 1) * line]
            part += jnp.where(edge, rim, 0.0)
            here = slice((group * TILES_H + i) * TILE, (group * TILES_H + i + 1) * TILE)
            pieces = [
                part[:TILE] + left_ref[here].astype(F32),
                part[TILE : line - TILE],
                part[line - TILE :] + right_ref[here].astype(F32),
            ]
            out_ref[group, i * line : (i + 1) * line, :] = jnp.concatenate(pieces, 0).astype(BF16)


def settle(half, own, first, second, rim, left, right):
    width = own.shape[-1]
    step = GROUP // PACKS

    def spec(rows):
        return pl.BlockSpec((rows * step, width), lambda b: (b, 0))

    return pl.pallas_call(
        settle_kernel,
        grid=(PACKS,),
        in_specs=[
            pl.BlockSpec(memory_space=pltpu.SMEM),
            spec(CUBE),
            spec(CUBE),
            spec(CUBE),
            pl.BlockSpec((RIM, width), lambda b: (0, 0)),
            spec(TILES_H * TILE),
            spec(TILES_H * TILE),
        ],
        out_specs=pl.BlockSpec((step, CUBE, width), lambda b: (b, 0, 0)),
        out_shape=jax.ShapeDtypeStruct((GROUP, CUBE, width), BF16),
        compiler_params=pltpu.CompilerParams(vmem_limit_bytes=VMEM),
    )(half, own, first, second, rim, left, right)


def offset_table():
    table = np.full((GROUP, 3, SEEN, TILES_H, TILES_W), -1, np.int32)
    for block in range(GROUP):
        for k, (kh, kw) in enumerate(seen_tiles(block)):
            for qh in range(TILES_H):
                for qw in range(TILES_W):
                    dh, dw = kh - (block * TILES_H + qh), kw - qw
                    if abs(dh) <= 1 and abs(dw) <= 1:
                        for i, dt in enumerate((0, -1, 1)):
                            table[block, i, k, qh, qw] = 9 * dt + 3 * dh + dw + 13
    return table


def allowed_tiles(pattern, half):
    hot = offset_table().reshape(GROUP, 3, SEEN, -1)[..., None] == np.arange(27)
    picked = jnp.sum(jnp.where(hot, pattern[:, None, None], 0.0), -1)
    places = np.array([seen_tiles(block) for block in range(GROUP)])
    t = lax.axis_index("ta") + jnp.array([0, -1, 1])
    t_ok = (t >= 0) & (t < lax.axis_size("ta"))
    w = lax.axis_index("wa") * TILES_W + places[..., 1]
    w_ok = (w >= 0) & (w < TILES_W * lax.axis_size("wa"))
    h = half * GROUP_H + places[..., 0]
    h_ok = (h >= 0) & (h < TILES_H * lax.axis_size("ha"))
    inside = t_ok[None, :, None] & (w_ok & h_ok)[:, None, :]
    picked = jnp.where(inside[..., None], picked, 0.0)
    return jnp.repeat(picked.reshape(GROUP, 3 * SEEN, -1), TILE, axis=2)


def turned_width(value, step):
    count = lax.axis_size("wa")
    return lax.ppermute(value, "wa", [(i, (i + step) % count) for i in range(count)])


def turned_time(value, step):
    count_t, count_h = lax.axis_size("ta"), lax.axis_size("ha")
    pairs = []
    for t in range(count_t):
        for h in range(count_h):
            t_to = t + step
            h_to = h
            if not 0 <= t_to < count_t:
                h_to = (h + count_h // 2) % count_h
            pairs.append((t * count_h + h, t_to % count_t * count_h + h_to))
    return lax.ppermute(value, ("ta", "ha"), pairs)


def swapped(value, axis, bit):
    count = lax.axis_size(axis)
    return lax.ppermute(value, axis, [(i, i ^ bit) for i in range(count)])


def regrouped(value):
    count = lax.axis_size("ha")
    groups = [list(range(i, i + GROUP)) for i in range(0, count, GROUP)]
    return lax.all_to_all(value, "ha", 0, 0, axis_index_groups=groups)


def log2(count):
    return count.bit_length() - 1


def text_steps():
    ta, ha, wa = (lax.axis_size(axis) for axis in ("ta", "ha", "wa"))
    steps = [("ta", ta >> i) for i in range(1, log2(ta))]
    steps += [("ha", ha >> i) for i in range(1, log2(ha) + 1)]
    steps += [("wa", wa >> i) for i in range(1, log2(wa) + 1)]
    return steps + [("ta", 1)]


def text_bits():
    start = {"wa": 0, "ha": log2(lax.axis_size("wa"))}
    start["ta"] = start["ha"] + log2(lax.axis_size("ha"))
    return tuple(start[axis] + log2(bit) for axis, bit in text_steps())


def is_high(axis, bit):
    return (lax.axis_index(axis) & bit) > 0


def gather_text(value, axis, bit):
    high = is_high(axis, bit)
    mine = theirs = value
    if axis == "ha" and bit < GROUP:
        middle = value.shape[0] // 2
        mine = jnp.where(high, value[middle:], value[:middle])
        theirs = jnp.where(high, value[:middle], value[middle:])
    return jnp.concatenate([mine, swapped(theirs, axis, bit)], 1)


def scatter_text(mine, theirs, axis, bit):
    high = is_high(axis, bit)
    other = swapped(theirs, axis, bit)
    if axis == "ha" and bit < GROUP:
        first = jnp.where(high, other, mine)
        second = jnp.where(high, mine, other)
        return jnp.concatenate([first, second], 0)
    return mine + other


def scatter_halves(value, axis, bit):
    middle = value.shape[1] // 2
    return scatter_text(value[:, :middle], value[:, middle:], axis, bit)


def after(value, *others):
    return lax.optimization_barrier((value, *others))[0]


def local(query, key, value, d_out, text_key, text_value, block_pattern, text_length):
    full = query.shape[-1]
    half = lax.axis_index("ha") // GROUP
    steps = text_steps()
    line = TILES_W * TILE

    def edge(rows, size):
        return jnp.where(half == 0, rows[(GROUP_H - 1) * size :], rows[:size])

    kv_out = pack(
        key.reshape(CUBE, full), value.reshape(CUBE, full), block_pattern.reshape(-1, 27)
    )
    text = jnp.stack([text_key.reshape(-1, HEAD), text_value.reshape(-1, HEAD)], 1)
    text = after(text.reshape(GROUP, 1, -1), kv_out)
    for step in steps[:3]:
        text = gather_text(text, *step)
    qg_out = pack(query.reshape(CUBE, full), d_out.reshape(CUBE, full))
    kv_in = regrouped(kv_out)
    width = kv_in.shape[-1]

    own = kv_in[:, :CUBE].reshape(GROUP_H, TILES_W, TILE, width)
    from_left = turned_width(own[:, TILES_W - 1].reshape(SIDE, width), 1)
    from_right = turned_width(own[:, 0].reshape(SIDE, width), -1)
    flat = own.reshape(OWN, width)
    owns = [flat, turned_time(flat, 1), turned_time(flat, -1)]
    text = gather_text(after(text, kv_in), *steps[3])
    qg = regrouped(after(qg_out, from_left, from_right))
    text = gather_text(after(text, from_left, from_right), *steps[4])
    text = gather_text(text, *steps[5])
    rim = jnp.concatenate([edge(flat, line), edge(from_left, TILE), edge(from_right, TILE)], 0)
    rim = swapped(rim, "ha", GROUP)
    halo = jnp.concatenate([from_left, from_right, rim], 0)
    halos = [halo, turned_time(halo, 1), turned_time(halo, -1)]
    text = after(text, halo)
    for step in steps[6:]:
        text = gather_text(text, *step)
    allow = allowed_tiles(kv_in[:, CUBE : CUBE + 8, :27].astype(F32), half)

    me = (lax.axis_index("ta") * lax.axis_size("ha") + lax.axis_index("ha")) * lax.axis_size("wa")
    me = me + lax.axis_index("wa")
    (
        od,
        own_grad,
        own_below,
        own_above,
        halo_grad,
        halo_below,
        halo_above,
        text_grad,
        text_away,
    ) = attention(
        jnp.concatenate([text_length, me.reshape(1)]),
        allow,
        qg,
        owns,
        halos,
        text[0],
        text_bits(),
    )

    halo_first = turned_time(halo_below, -1)
    halo_second = turned_time(halo_above, 1)
    own_first = turned_time(own_below, -1)
    own_second = turned_time(own_above, 1)
    back = steps[::-1]
    text_grad = scatter_text(text_grad[None], text_away[None], *back[0])
    text_grad = scatter_halves(text_grad, *back[1])
    od_in = regrouped(od)
    halo_sum = halo_grad + halo_first.astype(F32) + halo_second.astype(F32)
    rim_out = halo_sum[2 * SIDE :].astype(BF16)
    rim_in = swapped(rim_out, "ha", GROUP)
    text_grad = scatter_halves(after(text_grad, rim_out), *back[2])
    sides = halo_sum[: 2 * SIDE].reshape(2, GROUP_H, TILE, width)
    row = lax.broadcasted_iota(jnp.int32, (1, GROUP_H, 1, 1), 1)
    at_edge = row == jnp.where(half == 0, GROUP_H - 1, 0)
    extra = rim_in[line:].astype(F32).reshape(2, 1, TILE, width)
    sides = (sides + jnp.where(at_edge, extra, 0.0)).astype(BF16).reshape(2, SIDE, width)
    right = turned_width(sides[0], -1)
    left = turned_width(sides[1], 1)
    text_grad = scatter_halves(after(text_grad, rim_in, od_in), *back[3])
    grads = settle(half.reshape(1), own_grad, own_first, own_second, rim_in, left, right)
    text_grad = after(text_grad, left, right)
    for step in back[4:]:
        text_grad = scatter_halves(text_grad, *step)
    attended, query_grad = unpack(od_in)
    key_grad, value_grad = unpack(regrouped(grads))
    text_grad = text_grad.astype(BF16).reshape(-1, 2, HEAD)
    return (
        attended.reshape(query.shape),
        query_grad.reshape(query.shape),
        key_grad.reshape(query.shape),
        value_grad.reshape(query.shape),
        text_grad[:, 0].reshape(1, full),
        text_grad[:, 1].reshape(1, full),
    )


def solution(mesh):
    cube = P("ta", "ha", "wa", None)
    text = P(("ta", "ha", "wa"), None)
    return jax.shard_map(
        local,
        mesh=mesh,
        in_specs=(cube, cube, cube, cube, text, text, cube, P()),
        out_specs=(cube, cube, cube, cube, text, text),
        check_vma=False,
    )
```

```python
import functools

import jax
import jax.numpy as jnp
import numpy as np
from jax import lax
from jax.experimental import pallas as pl
from jax.experimental.pallas import tpu as pltpu
from jax.sharding import PartitionSpec as P

HEAD = 128
PAIR = 2 * HEAD
TILE_T = 2
TILE_H = 2
TILE_W = 4
TILE = TILE_T * TILE_H * TILE_W
NEGATIVE = -1e30
LOG2E = 1.4426950408889634
EXTRA = 16
PACKS = 2
VMEM = 58 * 1024 * 1024
F32 = jnp.float32
BF16 = jnp.bfloat16

ROWS = 4
COLS = 16
TILES_H = ROWS // TILE_H
TILES_W = COLS // TILE_W
CUBE = TILE_T * ROWS * COLS
GROUP = 4
GROUP_H = GROUP * TILES_H
OWN = GROUP_H * TILES_W * TILE
SIDE = GROUP_H * TILE
RIM = (TILES_W + 2) * TILE
HALO = 2 * SIDE + RIM
SEEN = (TILES_H + 2) * (TILES_W + 2)


def natural_index(row):
    tile_h = row >> 6
    tile_w = (row >> 4) & 3
    t = (row >> 3) & 1
    h = (row >> 2) & 1
    w = row & 3
    return t * (ROWS * COLS) + (tile_h * TILE_H + h) * COLS + tile_w * TILE_W + w


def pack_kernel(first_ref, second_ref, *rest):
    out_ref = rest[-1]
    row = lax.broadcasted_iota(jnp.int32, (CUBE, CUBE), 0)
    col = lax.broadcasted_iota(jnp.int32, (CUBE, CUBE), 1)
    order = jnp.where(natural_index(row) == col, 1.0, 0.0).astype(BF16)
    first = jnp.dot(order, first_ref[...], preferred_element_type=F32).astype(BF16)
    second = jnp.dot(order, second_ref[...], preferred_element_type=F32).astype(BF16)
    groups, _, width = out_ref.shape
    heads = width // PAIR
    for group in range(groups):
        for i in range(heads):
            source = slice((group * heads + i) * HEAD, (group * heads + i + 1) * HEAD)
            out_ref[group, :CUBE, i * PAIR : i * PAIR + HEAD] = first[:, source]
            out_ref[group, :CUBE, i * PAIR + HEAD : (i + 1) * PAIR] = second[:, source]
        if len(rest) > 1:
            pattern = rest[0][...].astype(F32)
            lines = jnp.concatenate([pattern, jnp.zeros_like(pattern)], 0).astype(BF16)
            out_ref[group, CUBE:, :] = jnp.zeros((EXTRA, width), BF16)
            out_ref[group, CUBE:, : pattern.shape[1]] = lines


def pack(first, second, pattern=None):
    width = first.shape[1] // GROUP
    step = GROUP // PACKS
    rows = CUBE + (0 if pattern is None else EXTRA)
    specs = [pl.BlockSpec((CUBE, width * step), lambda g: (0, g))] * 2
    extras = ()
    if pattern is not None:
        specs.append(pl.BlockSpec(pattern.shape, lambda g: (0, 0)))
        extras = (pattern,)
    return pl.pallas_call(
        pack_kernel,
        grid=(PACKS,),
        in_specs=specs,
        out_specs=pl.BlockSpec((step, rows, 2 * width), lambda g: (g, 0, 0)),
        out_shape=jax.ShapeDtypeStruct((GROUP, rows, 2 * width), BF16),
        compiler_params=pltpu.CompilerParams(vmem_limit_bytes=VMEM),
    )(first, second, *extras)


def unpack_kernel(packed_ref, first_ref, second_ref):
    row = lax.broadcasted_iota(jnp.int32, (CUBE, CUBE), 0)
    col = lax.broadcasted_iota(jnp.int32, (CUBE, CUBE), 1)
    order = jnp.where(natural_index(col) == row, 1.0, 0.0).astype(BF16)
    groups, _, width = packed_ref.shape
    heads = width // PAIR
    for group in range(groups):
        both = jnp.dot(order, packed_ref[group], preferred_element_type=F32).astype(BF16)
        for i in range(heads):
            target = slice((group * heads + i) * HEAD, (group * heads + i + 1) * HEAD)
            first_ref[:, target] = both[:, i * PAIR : i * PAIR + HEAD]
            second_ref[:, target] = both[:, i * PAIR + HEAD : (i + 1) * PAIR]


def unpack(packed):
    _, rows, width = packed.shape
    step = GROUP // PACKS
    half = width // 2
    return pl.pallas_call(
        unpack_kernel,
        grid=(PACKS,),
        in_specs=[pl.BlockSpec((step, rows, width), lambda g: (g, 0, 0))],
        out_specs=[pl.BlockSpec((CUBE, half * step), lambda g: (0, g))] * 2,
        out_shape=[jax.ShapeDtypeStruct((CUBE, GROUP * half), BF16)] * 2,
        compiler_params=pltpu.CompilerParams(vmem_limit_bytes=VMEM),
    )(packed)


def block_rows(block):
    low, high = block * TILES_H - 1, (block + 1) * TILES_H + 1
    outer = -1 if low < 0 else GROUP_H if high > GROUP_H else None
    return max(low, 0), min(high, GROUP_H), outer


def seen_tiles(block):
    low, high, outer = block_rows(block)
    tiles = [(h, w) for h in range(low, high) for w in range(TILES_W)]
    tiles += [(h, -1) for h in range(low, high)] + [(h, TILES_W) for h in range(low, high)]
    if outer is not None:
        tiles += [(outer, w) for w in (*range(TILES_W), -1, TILES_W)]
    return tiles


def attention_kernel(
    length_ref,
    allow_ref,
    qg_ref,
    own_ref,
    own_below_ref,
    own_above_ref,
    halo_ref,
    halo_below_ref,
    halo_above_ref,
    text_ref,
    od_ref,
    own_out,
    own_below_out,
    own_above_out,
    halo_out,
    halo_below_out,
    halo_above_out,
    text_out,
    own_below_sum,
    own_above_sum,
    halo_below_sum,
    halo_above_sum,
    text_sum,
):
    text_count = text_ref.shape[0]
    scale = HEAD**-0.5
    owns = (own_ref, own_below_ref, own_above_ref)
    halos = (halo_ref, halo_below_ref, halo_above_ref)
    own_sums = (own_out, own_below_sum, own_above_sum)
    halo_sums = (halo_out, halo_below_sum, halo_above_sum)
    text_row = lax.broadcasted_iota(jnp.int32, (text_count, CUBE), 0)
    text_ok = text_row < length_ref[0]
    blank = jnp.zeros((CUBE, HEAD), BF16)
    text_kv = text_ref[...]
    line = TILES_W * TILE
    def look(block):
        low, high, outer = block_rows(block)
        count = high - low
        q = qg_ref[block, :, :HEAD]
        g = qg_ref[block, :, HEAD:]
        both = jnp.concatenate(
            [jnp.concatenate([q, blank], 1), jnp.concatenate([blank, g], 1)], 0
        )
        done = 0 if block == 0 else 2
        places = [(False, low * line, count * line, done * line)]
        for side in range(2):
            places.append((True, side * SIDE + low * TILE, count * TILE, done * TILE))
        if outer is not None:
            places.append((True, 2 * SIDE, RIM, 0 if block == 0 else RIM))
        keys = []
        masks = []
        for i in range(3):
            parts = [
                (halos if in_halo else owns)[i][first : first + size, :]
                for in_halo, first, size, _ in places
            ]
            keys.append(jnp.concatenate(parts, 0))
            tiles = allow_ref[block, i * SEEN : (i + 1) * SEEN, :]
            spread = jnp.broadcast_to(tiles[:, None, :], (SEEN, TILE, CUBE))
            masks.append(spread.reshape(SEEN * TILE, CUBE) > 0.5)
        keys.append(text_kv)
        masks.append(text_ok)
        scores = []
        dprobs = []
        for kv, ok in zip(keys, masks):
            mixed = lax.dot_general(
                kv, both, (((1,), (1,)), ((), ())), preferred_element_type=F32
            )
            scores.append(jnp.where(ok, mixed[:, :HEAD] * (scale * LOG2E), NEGATIVE))
            dprobs.append(mixed[:, HEAD:])
        top = functools.reduce(jnp.maximum, [jnp.max(s, 0, keepdims=True) for s in scores])
        return g, both, places, keys, scores, dprobs, top

    def finish(block, found):
        g, both, places, keys, scores, dprobs, top = found
        exps = [jnp.exp2(s - top) for s in scores]
        total = functools.reduce(jnp.add, [jnp.sum(e, 0, keepdims=True) for e in exps])
        inverse = 1.0 / total
        weights = [(e * inverse).astype(BF16) for e in exps]
        attended = jnp.zeros((CUBE, HEAD), F32)
        for w, kv in zip(weights, keys):
            attended += lax.dot_general(
                w, kv[:, HEAD:], (((0,), (0,)), ((), ())), preferred_element_type=F32
            )
        attended = attended.astype(BF16)
        od_ref[block, :, :HEAD] = attended
        product = g.astype(F32) * attended.astype(F32)
        delta = jnp.sum(product.T, 0, keepdims=True)
        dscores = [(e * ((d - delta) * inverse)).astype(BF16) for e, d in zip(exps, dprobs)]
        return both, places, keys, weights, dscores

    def settle_block(block, state):
        both, places, keys, weights, dscores = state
        query_grad = jnp.zeros((CUBE, HEAD), F32)
        for d, kv in zip(dscores, keys):
            query_grad += lax.dot_general(
                d, kv[:, :HEAD], (((0,), (0,)), ((), ())), preferred_element_type=F32
            )
        od_ref[block, :, HEAD:] = (query_grad * scale).astype(BF16)
        for i in range(4):
            change = jnp.dot(
                jnp.concatenate([dscores[i], weights[i]], 1), both, preferred_element_type=F32
            )
            if i == 3:
                if block == 0:
                    text_sum[...] = change
                else:
                    text_sum[...] += change
                continue
            taken = 0
            for in_halo, first, size, old in places:
                target = (halo_sums if in_halo else own_sums)[i]
                if old:
                    target[first : first + old, :] += change[taken : taken + old]
                if old < size:
                    target[first + old : first + size, :] = change[taken + old : taken + size]
                taken += size
    found = look(0)
    before = None
    for block in range(GROUP):
        following = look(block + 1) if block + 1 < GROUP else None
        now = finish(block, found)
        if before is not None:
            settle_block(block - 1, before)
        before = now
        found = following
    settle_block(GROUP - 1, before)
    lane = lax.broadcasted_iota(jnp.int32, (1, PAIR), 1)
    factor = jnp.where(lane < HEAD, scale, 1.0).astype(F32)
    own_out[...] = own_out[...] * factor
    halo_out[...] = halo_out[...] * factor
    text_out[...] = (text_sum[...] * factor).astype(BF16)
    own_below_out[...] = (own_below_sum[...] * factor).astype(BF16)
    own_above_out[...] = (own_above_sum[...] * factor).astype(BF16)
    halo_below_out[...] = (halo_below_sum[...] * factor).astype(BF16)
    halo_above_out[...] = (halo_above_sum[...] * factor).astype(BF16)


def attention(length, allow, qg, owns, halos, text):
    width = qg.shape[-1]
    heads = width // PAIR
    text_count = text.shape[0]

    def spec(rows):
        return pl.BlockSpec((rows, PAIR), lambda h: (0, h))

    def shape(rows, dtype):
        return jax.ShapeDtypeStruct((rows, width), dtype)

    part = pl.BlockSpec((GROUP, CUBE, PAIR), lambda h: (0, 0, h))
    return pl.pallas_call(
        attention_kernel,
        grid=(heads,),
        in_specs=[
            pl.BlockSpec(memory_space=pltpu.SMEM),
            pl.BlockSpec(allow.shape, lambda h: (0, 0, 0)),
            part,
        ]
        + [spec(OWN)] * 3
        + [spec(HALO)] * 3
        + [spec(text_count)],
        out_specs=[part] + [spec(OWN)] * 3 + [spec(HALO)] * 3 + [spec(text_count)],
        out_shape=[
            jax.ShapeDtypeStruct(qg.shape, BF16),
            shape(OWN, F32),
            shape(OWN, BF16),
            shape(OWN, BF16),
            shape(HALO, F32),
            shape(HALO, BF16),
            shape(HALO, BF16),
            shape(text_count, BF16),
        ],
        scratch_shapes=[pltpu.VMEM((rows, PAIR), F32) for rows in (OWN, OWN, HALO, HALO, text_count)],
        compiler_params=pltpu.CompilerParams(vmem_limit_bytes=VMEM),
    )(length, allow, qg, *owns, *halos, text)


def settle_kernel(
    half_ref,
    own_ref,
    first_ref,
    second_ref,
    rim_ref,
    corner_left_ref,
    corner_right_ref,
    left_ref,
    right_ref,
    out_ref,
):
    line = TILES_W * TILE
    rim = rim_ref[...].astype(F32)
    rim = jnp.concatenate(
        [
            rim[:TILE] + corner_left_ref[...].astype(F32),
            rim[TILE : line - TILE],
            rim[line - TILE :] + corner_right_ref[...].astype(F32),
        ],
        0,
    )
    half = half_ref[0]
    groups = out_ref.shape[0]
    for group in range(groups):
        block = pl.program_id(0) * groups + group
        cube = slice(group * CUBE, (group + 1) * CUBE)
        total = own_ref[cube] + first_ref[cube].astype(F32) + second_ref[cube].astype(F32)
        for i in range(TILES_H):
            edge = (block == 0) & (half == 1) if i == 0 else (block == GROUP - 1) & (half == 0)
            part = total[i * line : (i + 1) * line]
            part += jnp.where(edge, rim, 0.0)
            here = slice((group * TILES_H + i) * TILE, (group * TILES_H + i + 1) * TILE)
            pieces = [
                part[:TILE] + left_ref[here].astype(F32),
                part[TILE : line - TILE],
                part[line - TILE :] + right_ref[here].astype(F32),
            ]
            out_ref[group, i * line : (i + 1) * line, :] = jnp.concatenate(pieces, 0).astype(BF16)


def settle(half, own, first, second, rim, corners, left, right):
    width = own.shape[-1]
    step = GROUP // PACKS

    def spec(rows):
        return pl.BlockSpec((rows * step, width), lambda b: (b, 0))

    return pl.pallas_call(
        settle_kernel,
        grid=(PACKS,),
        in_specs=[
            pl.BlockSpec(memory_space=pltpu.SMEM),
            spec(CUBE),
            spec(CUBE),
            spec(CUBE),
            pl.BlockSpec((TILES_W * TILE, width), lambda b: (0, 0)),
            pl.BlockSpec((TILE, width), lambda b: (0, 0)),
            pl.BlockSpec((TILE, width), lambda b: (0, 0)),
            spec(TILES_H * TILE),
            spec(TILES_H * TILE),
        ],
        out_specs=pl.BlockSpec((step, CUBE, width), lambda b: (b, 0, 0)),
        out_shape=jax.ShapeDtypeStruct((GROUP, CUBE, width), BF16),
        compiler_params=pltpu.CompilerParams(vmem_limit_bytes=VMEM),
    )(half, own, first, second, rim, *corners, left, right)


def offset_table():
    table = np.full((GROUP, 3, SEEN, TILES_H, TILES_W), -1, np.int32)
    for block in range(GROUP):
        for k, (kh, kw) in enumerate(seen_tiles(block)):
            for qh in range(TILES_H):
                for qw in range(TILES_W):
                    dh, dw = kh - (block * TILES_H + qh), kw - qw
                    if abs(dh) <= 1 and abs(dw) <= 1:
                        for i, dt in enumerate((0, -1, 1)):
                            table[block, i, k, qh, qw] = 9 * dt + 3 * dh + dw + 13
    return table


def allowed_tiles(pattern, half):
    hot = offset_table().reshape(GROUP, 3, SEEN, -1)[..., None] == np.arange(27)
    picked = jnp.sum(jnp.where(hot, pattern[:, None, None], 0.0), -1)
    places = np.array([seen_tiles(block) for block in range(GROUP)])
    t = lax.axis_index("ta") + jnp.array([0, -1, 1])
    t_ok = (t >= 0) & (t < lax.axis_size("ta"))
    w = lax.axis_index("wa") * TILES_W + places[..., 1]
    w_ok = (w >= 0) & (w < TILES_W * lax.axis_size("wa"))
    h = half * GROUP_H + places[..., 0]
    h_ok = (h >= 0) & (h < TILES_H * lax.axis_size("ha"))
    inside = t_ok[None, :, None] & (w_ok & h_ok)[:, None, :]
    picked = jnp.where(inside[..., None], picked, 0.0)
    return jnp.repeat(picked.reshape(GROUP, 3 * SEEN, -1), TILE, axis=2)


def turned_width(value, step):
    count = lax.axis_size("wa")
    return lax.ppermute(value, "wa", [(i, (i + step) % count) for i in range(count)])


def turned_time(value, step):
    count_t, count_h = lax.axis_size("ta"), lax.axis_size("ha")
    pairs = []
    for t in range(count_t):
        for h in range(count_h):
            t_to = t + step
            h_to = h
            if not 0 <= t_to < count_t:
                h_to = (h + count_h // 2) % count_h
            pairs.append((t * count_h + h, t_to % count_t * count_h + h_to))
    return lax.ppermute(value, ("ta", "ha"), pairs)


def turned_corner(value, step):
    count_h, count_w = lax.axis_size("ha"), lax.axis_size("wa")
    pairs = []
    for h in range(count_h):
        for w in range(count_w):
            h_to = (h + count_h // 2) % count_h
            pairs.append((h * count_w + w, h_to * count_w + (w + step) % count_w))
    return lax.ppermute(value, ("ha", "wa"), pairs)


def swapped(value):
    count = lax.axis_size("ha")
    return lax.ppermute(value, "ha", [(i, (i + count // 2) % count) for i in range(count)])


def regrouped(value):
    count = lax.axis_size("ha")
    groups = [list(range(i, i + GROUP)) for i in range(0, count, GROUP)]
    return lax.all_to_all(value, "ha", 0, 0, axis_index_groups=groups)


def crossed(value):
    lines = lax.all_to_all(value[:, None], ("ta", "ha", "wa"), 0, 0)
    return lines[:, 0]


def after(value, *others):
    return lax.optimization_barrier((value, *others))[0]


def local(query, key, value, d_out, text_key, text_value, block_pattern, text_length):
    full = query.shape[-1]
    half = lax.axis_index("ha") // GROUP
    devices = [lax.axis_size(axis) for axis in ("ta", "ha", "wa")]
    split = (devices[0] * devices[1] // GROUP, GROUP, devices[2], -1)
    line = TILES_W * TILE

    kv_out = pack(
        key.reshape(CUBE, full), value.reshape(CUBE, full), block_pattern.reshape(-1, 27)
    )
    kv_in = regrouped(kv_out)
    width = kv_in.shape[-1]
    qg_out = pack(query.reshape(CUBE, full), d_out.reshape(CUBE, full))
    text = jnp.stack([text_key.reshape(-1, HEAD), text_value.reshape(-1, HEAD)], 1)
    text = jnp.broadcast_to(text.reshape(1, GROUP, 1, width), split[:3] + (width,))
    text = crossed(after(text.reshape(-1, width), kv_out))

    own = kv_in[:, :CUBE].reshape(GROUP_H, TILES_W, TILE, width)
    flat = own.reshape(OWN, width)
    edge = jnp.where(half == 0, own[GROUP_H - 1], own[0])
    from_left = turned_width(own[:, TILES_W - 1].reshape(SIDE, width), 1)
    from_right = turned_width(own[:, 0].reshape(SIDE, width), -1)
    rim = swapped(edge.reshape(line, width))
    corner_left = turned_corner(edge[TILES_W - 1], 1)
    corner_right = turned_corner(edge[0], -1)
    owns = [flat, turned_time(flat, 1), turned_time(flat, -1)]
    qg = regrouped(after(qg_out, kv_in))
    halo = jnp.concatenate([from_left, from_right, rim, corner_left, corner_right], 0)
    halos = [halo, turned_time(halo, 1), turned_time(halo, -1)]
    allow = allowed_tiles(kv_in[:, CUBE : CUBE + 8, :27].astype(F32), half)
    (
        od,
        own_grad,
        own_below,
        own_above,
        halo_grad,
        halo_below,
        halo_above,
        text_grad,
    ) = attention(text_length, allow, qg, owns, halos, text)

    halo_first = turned_time(halo_below, -1)
    halo_second = turned_time(halo_above, 1)
    own_first = turned_time(own_below, -1)
    own_second = turned_time(own_above, 1)
    od_in = regrouped(od)
    text_in = crossed(text_grad)
    halo_sum = halo_grad + halo_first.astype(F32) + halo_second.astype(F32)
    halo_sum = halo_sum.astype(BF16)
    right = turned_width(halo_sum[:SIDE], -1)
    left = turned_width(halo_sum[SIDE : 2 * SIDE], 1)
    rim_in = swapped(halo_sum[2 * SIDE : 2 * SIDE + line])
    right_corner = turned_corner(halo_sum[HALO - 2 * TILE : HALO - TILE], -1)
    left_corner = turned_corner(halo_sum[HALO - TILE :], 1)
    grads = settle(
        half.reshape(1),
        own_grad,
        own_first,
        own_second,
        rim_in,
        (left_corner, right_corner),
        left,
        right,
    )
    attended, query_grad = unpack(od_in)
    key_grad, value_grad = unpack(regrouped(grads))
    text_sum = jnp.sum(text_in.astype(F32).reshape(split), (0, 2)).astype(BF16)
    text_sum = text_sum.reshape(-1, 2, HEAD)
    return (
        attended.reshape(query.shape),
        query_grad.reshape(query.shape),
        key_grad.reshape(query.shape),
        value_grad.reshape(query.shape),
        text_sum[:, 0].reshape(1, full),
        text_sum[:, 1].reshape(1, full),
    )


def solution(mesh):
    cube = P("ta", "ha", "wa", None)
    text = P(("ta", "ha", "wa"), None)
    return jax.shard_map(
        local,
        mesh=mesh,
        in_specs=(cube, cube, cube, cube, text, text, cube, P()),
        out_specs=(cube, cube, cube, cube, text, text),
        check_vma=False,
    )
```

```python
import functools

import jax
import jax.numpy as jnp
import numpy as np
from jax import lax
from jax.experimental import pallas as pl
from jax.experimental.pallas import tpu as pltpu
from jax.sharding import PartitionSpec as P

HEAD = 128
PAIR = 2 * HEAD
TILE_T = 2
TILE_H = 2
TILE_W = 4
TILE = TILE_T * TILE_H * TILE_W
NEGATIVE = -1e30
LOG2E = 1.4426950408889634
EXTRA = 16
PACKS = 2
VMEM = 58 * 1024 * 1024
F32 = jnp.float32
BF16 = jnp.bfloat16

ROWS = 4
COLS = 16
TILES_H = ROWS // TILE_H
TILES_W = COLS // TILE_W
CUBE = TILE_T * ROWS * COLS
GROUP = 4
GROUP_H = GROUP * TILES_H
OWN = GROUP_H * TILES_W * TILE
SIDE = GROUP_H * TILE
RIM = (TILES_W + 2) * TILE
ALL = OWN + 2 * SIDE + RIM
SEEN = (TILES_H + 2) * (TILES_W + 2)


def natural_index(row):
    tile_h = row >> 6
    tile_w = (row >> 4) & 3
    t = (row >> 3) & 1
    h = (row >> 2) & 1
    w = row & 3
    return t * (ROWS * COLS) + (tile_h * TILE_H + h) * COLS + tile_w * TILE_W + w


def pack_kernel(first_ref, second_ref, *rest):
    out_ref = rest[-1]
    row = lax.broadcasted_iota(jnp.int32, (CUBE, CUBE), 0)
    col = lax.broadcasted_iota(jnp.int32, (CUBE, CUBE), 1)
    order = jnp.where(natural_index(row) == col, 1.0, 0.0).astype(BF16)
    first = jnp.dot(order, first_ref[...], preferred_element_type=F32).astype(BF16)
    second = jnp.dot(order, second_ref[...], preferred_element_type=F32).astype(BF16)
    groups, _, width = out_ref.shape
    heads = width // PAIR
    for group in range(groups):
        for i in range(heads):
            source = slice((group * heads + i) * HEAD, (group * heads + i + 1) * HEAD)
            out_ref[group, :CUBE, i * PAIR : i * PAIR + HEAD] = first[:, source]
            out_ref[group, :CUBE, i * PAIR + HEAD : (i + 1) * PAIR] = second[:, source]
        if len(rest) > 1:
            pattern = rest[0][...].astype(F32)
            lines = jnp.concatenate([pattern, jnp.zeros_like(pattern)], 0).astype(BF16)
            out_ref[group, CUBE:, :] = jnp.zeros((EXTRA, width), BF16)
            out_ref[group, CUBE:, : pattern.shape[1]] = lines


def pack(first, second, pattern=None):
    width = first.shape[1] // GROUP
    step = GROUP // PACKS
    rows = CUBE + (0 if pattern is None else EXTRA)
    specs = [pl.BlockSpec((CUBE, width * step), lambda g: (0, g))] * 2
    extras = ()
    if pattern is not None:
        specs.append(pl.BlockSpec(pattern.shape, lambda g: (0, 0)))
        extras = (pattern,)
    return pl.pallas_call(
        pack_kernel,
        grid=(PACKS,),
        in_specs=specs,
        out_specs=pl.BlockSpec((step, rows, 2 * width), lambda g: (g, 0, 0)),
        out_shape=jax.ShapeDtypeStruct((GROUP, rows, 2 * width), BF16),
        compiler_params=pltpu.CompilerParams(vmem_limit_bytes=VMEM),
    )(first, second, *extras)


def unpack_kernel(packed_ref, first_ref, second_ref):
    row = lax.broadcasted_iota(jnp.int32, (CUBE, CUBE), 0)
    col = lax.broadcasted_iota(jnp.int32, (CUBE, CUBE), 1)
    order = jnp.where(natural_index(col) == row, 1.0, 0.0).astype(BF16)
    groups, _, width = packed_ref.shape
    heads = width // PAIR
    for group in range(groups):
        both = jnp.dot(order, packed_ref[group], preferred_element_type=F32).astype(BF16)
        for i in range(heads):
            target = slice((group * heads + i) * HEAD, (group * heads + i + 1) * HEAD)
            first_ref[:, target] = both[:, i * PAIR : i * PAIR + HEAD]
            second_ref[:, target] = both[:, i * PAIR + HEAD : (i + 1) * PAIR]


def unpack(packed):
    _, rows, width = packed.shape
    step = GROUP // PACKS
    half = width // 2
    return pl.pallas_call(
        unpack_kernel,
        grid=(PACKS,),
        in_specs=[pl.BlockSpec((step, rows, width), lambda g: (g, 0, 0))],
        out_specs=[pl.BlockSpec((CUBE, half * step), lambda g: (0, g))] * 2,
        out_shape=[jax.ShapeDtypeStruct((CUBE, GROUP * half), BF16)] * 2,
        compiler_params=pltpu.CompilerParams(vmem_limit_bytes=VMEM),
    )(packed)


def block_rows(block):
    low, high = block * TILES_H - 1, (block + 1) * TILES_H + 1
    outer = -1 if low < 0 else GROUP_H if high > GROUP_H else None
    return max(low, 0), min(high, GROUP_H), outer


def seen_tiles(block):
    low, high, outer = block_rows(block)
    tiles = [(h, w) for h in range(low, high) for w in range(TILES_W)]
    tiles += [(h, -1) for h in range(low, high)] + [(h, TILES_W) for h in range(low, high)]
    if outer is not None:
        tiles += [(outer, w) for w in (*range(TILES_W), -1, TILES_W)]
    return tiles


def attention_kernel(
    text_bits,
    length_ref,
    allow_ref,
    qg_ref,
    here_ref,
    below_ref,
    above_ref,
    text_ref,
    od_ref,
    here_out,
    below_out,
    above_out,
    text_out,
    text_away_out,
    below_sum,
    above_sum,
):
    text_count = text_ref.shape[0]
    scale = HEAD**-0.5
    near = (here_ref, below_ref, above_ref)
    sums = (here_out, below_sum, above_sum)
    text_row = lax.broadcasted_iota(jnp.int32, (text_count, CUBE), 0)
    text_place = jnp.zeros_like(text_row)
    for bit, place in enumerate(text_bits):
        text_place += ((text_row >> bit) & 1) << place
    text_ok = (text_place ^ length_ref[1]) < length_ref[0]
    blank = jnp.zeros((CUBE, HEAD), BF16)
    text_kv = text_ref[...]
    line = TILES_W * TILE
    def look(block):
        low, high, outer = block_rows(block)
        count = high - low
        q = qg_ref[block, :, :HEAD]
        g = qg_ref[block, :, HEAD:]
        both = jnp.concatenate(
            [jnp.concatenate([q, blank], 1), jnp.concatenate([blank, g], 1)], 0
        )
        done = 0 if block == 0 else 2
        places = [(low * line, count * line, done * line)]
        for side in range(2):
            places.append((OWN + side * SIDE + low * TILE, count * TILE, done * TILE))
        if outer is not None:
            places.append((OWN + 2 * SIDE, RIM, 0 if block == 0 else RIM))
        keys = []
        masks = []
        for i in range(3):
            parts = [near[i][first : first + size, :] for first, size, _ in places]
            keys.append(jnp.concatenate(parts, 0))
            tiles = allow_ref[block, i * SEEN : (i + 1) * SEEN, :]
            spread = jnp.broadcast_to(tiles[:, None, :], (SEEN, TILE, CUBE))
            masks.append(spread.reshape(SEEN * TILE, CUBE) > 0.5)
        keys.append(text_kv)
        masks.append(text_ok)
        scores = []
        dprobs = []
        for kv, ok in zip(keys, masks):
            mixed = lax.dot_general(
                kv, both, (((1,), (1,)), ((), ())), preferred_element_type=F32
            )
            scores.append(jnp.where(ok, mixed[:, :HEAD] * (scale * LOG2E), NEGATIVE))
            dprobs.append(mixed[:, HEAD:])
        top = functools.reduce(jnp.maximum, [jnp.max(s, 0, keepdims=True) for s in scores])
        return g, both, places, keys, scores, dprobs, top

    def finish(block, found):
        g, both, places, keys, scores, dprobs, top = found
        exps = [jnp.exp2(s - top) for s in scores]
        total = functools.reduce(jnp.add, [jnp.sum(e, 0, keepdims=True) for e in exps])
        inverse = 1.0 / total
        weights = [(e * inverse).astype(BF16) for e in exps]
        attended = jnp.zeros((CUBE, HEAD), F32)
        for w, kv in zip(weights, keys):
            attended += lax.dot_general(
                w, kv[:, HEAD:], (((0,), (0,)), ((), ())), preferred_element_type=F32
            )
        attended = attended.astype(BF16)
        od_ref[block, :, :HEAD] = attended
        product = g.astype(F32) * attended.astype(F32)
        delta = jnp.sum(product.T, 0, keepdims=True)
        dscores = [(e * ((d - delta) * inverse)).astype(BF16) for e, d in zip(exps, dprobs)]
        return both, places, keys, weights, dscores

    def settle_block(block, state):
        both, places, keys, weights, dscores = state
        query_grad = jnp.zeros((CUBE, HEAD), F32)
        for d, kv in zip(dscores, keys):
            query_grad += lax.dot_general(
                d, kv[:, :HEAD], (((0,), (0,)), ((), ())), preferred_element_type=F32
            )
        od_ref[block, :, HEAD:] = (query_grad * scale).astype(BF16)
        for i in range(4):
            change = jnp.dot(
                jnp.concatenate([dscores[i], weights[i]], 1), both, preferred_element_type=F32
            )
            if i == 3:
                middle = text_count // 2
                for target, piece in (
                    (text_out, change[:middle]),
                    (text_away_out, change[middle:]),
                ):
                    if block == 0:
                        target[...] = piece
                    else:
                        target[...] += piece
                continue
            taken = 0
            target = sums[i]
            for first, size, old in places:
                if old:
                    target[first : first + old, :] += change[taken : taken + old]
                if old < size:
                    target[first + old : first + size, :] = change[taken + old : taken + size]
                taken += size
    found = look(0)
    before = None
    for block in range(GROUP):
        following = look(block + 1) if block + 1 < GROUP else None
        now = finish(block, found)
        if before is not None:
            settle_block(block - 1, before)
        before = now
        found = following
    settle_block(GROUP - 1, before)
    lane = lax.broadcasted_iota(jnp.int32, (1, PAIR), 1)
    factor = jnp.where(lane < HEAD, scale, 1.0).astype(F32)
    here_out[...] = here_out[...] * factor
    below_out[...] = (below_sum[...] * factor).astype(BF16)
    above_out[...] = (above_sum[...] * factor).astype(BF16)
    text_out[...] = text_out[...] * factor
    text_away_out[...] = text_away_out[...] * factor


def attention(length, allow, qg, here, below, above, text, text_bits):
    width = qg.shape[-1]
    heads = width // PAIR
    text_count = text.shape[0]

    def spec(rows):
        return pl.BlockSpec((rows, PAIR), lambda h: (0, h))

    def shape(rows, dtype):
        return jax.ShapeDtypeStruct((rows, width), dtype)

    part = pl.BlockSpec((GROUP, CUBE, PAIR), lambda h: (0, 0, h))
    return pl.pallas_call(
        functools.partial(attention_kernel, text_bits),
        grid=(heads,),
        in_specs=[
            pl.BlockSpec(memory_space=pltpu.SMEM),
            pl.BlockSpec(allow.shape, lambda h: (0, 0, 0)),
            part,
        ]
        + [spec(ALL)] * 3
        + [spec(text_count)],
        out_specs=[part] + [spec(ALL)] * 3 + [spec(text_count // 2)] * 2,
        out_shape=[
            jax.ShapeDtypeStruct(qg.shape, BF16),
            shape(ALL, F32),
            shape(ALL, BF16),
            shape(ALL, BF16),
            shape(text_count // 2, F32),
            shape(text_count // 2, F32),
        ],
        scratch_shapes=[pltpu.VMEM((rows, PAIR), F32) for rows in (ALL, ALL)],
        compiler_params=pltpu.CompilerParams(vmem_limit_bytes=VMEM),
    )(length, allow, qg, here, below, above, text)


def settle_kernel(half_ref, own_ref, first_ref, second_ref, rim_ref, left_ref, right_ref, out_ref):
    line = TILES_W * TILE
    rim = rim_ref[:line, :].astype(F32)
    half = half_ref[0]
    groups = out_ref.shape[0]
    for group in range(groups):
        block = pl.program_id(0) * groups + group
        cube = slice(group * CUBE, (group + 1) * CUBE)
        total = own_ref[cube] + first_ref[cube].astype(F32) + second_ref[cube].astype(F32)
        for i in range(TILES_H):
            edge = (block == 0) & (half == 1) if i == 0 else (block == GROUP - 1) & (half == 0)
            part = total[i * line : (i + 1) * line]
            part += jnp.where(edge, rim, 0.0)
            here = slice((group * TILES_H + i) * TILE, (group * TILES_H + i + 1) * TILE)
            pieces = [
                part[:TILE] + left_ref[here].astype(F32),
                part[TILE : line - TILE],
                part[line - TILE :] + right_ref[here].astype(F32),
            ]
            out_ref[group, i * line : (i + 1) * line, :] = jnp.concatenate(pieces, 0).astype(BF16)


def settle(half, own, first, second, rim, left, right):
    width = own.shape[-1]
    step = GROUP // PACKS

    def spec(rows):
        return pl.BlockSpec((rows * step, width), lambda b: (b, 0))

    return pl.pallas_call(
        settle_kernel,
        grid=(PACKS,),
        in_specs=[
            pl.BlockSpec(memory_space=pltpu.SMEM),
            spec(CUBE),
            spec(CUBE),
            spec(CUBE),
            pl.BlockSpec((RIM, width), lambda b: (0, 0)),
            spec(TILES_H * TILE),
            spec(TILES_H * TILE),
        ],
        out_specs=pl.BlockSpec((step, CUBE, width), lambda b: (b, 0, 0)),
        out_shape=jax.ShapeDtypeStruct((GROUP, CUBE, width), BF16),
        compiler_params=pltpu.CompilerParams(vmem_limit_bytes=VMEM),
    )(half, own, first, second, rim, left, right)


def offset_table():
    table = np.full((GROUP, 3, SEEN, TILES_H, TILES_W), -1, np.int32)
    for block in range(GROUP):
        for k, (kh, kw) in enumerate(seen_tiles(block)):
            for qh in range(TILES_H):
                for qw in range(TILES_W):
                    dh, dw = kh - (block * TILES_H + qh), kw - qw
                    if abs(dh) <= 1 and abs(dw) <= 1:
                        for i, dt in enumerate((0, -1, 1)):
                            table[block, i, k, qh, qw] = 9 * dt + 3 * dh + dw + 13
    return table


def allowed_tiles(pattern, half):
    hot = offset_table().reshape(GROUP, 3, SEEN, -1)[..., None] == np.arange(27)
    picked = jnp.sum(jnp.where(hot, pattern[:, None, None], 0.0), -1)
    places = np.array([seen_tiles(block) for block in range(GROUP)])
    t = lax.axis_index("ta") + jnp.array([0, -1, 1])
    t_ok = (t >= 0) & (t < lax.axis_size("ta"))
    w = lax.axis_index("wa") * TILES_W + places[..., 1]
    w_ok = (w >= 0) & (w < TILES_W * lax.axis_size("wa"))
    h = half * GROUP_H + places[..., 0]
    h_ok = (h >= 0) & (h < TILES_H * lax.axis_size("ha"))
    inside = t_ok[None, :, None] & (w_ok & h_ok)[:, None, :]
    picked = jnp.where(inside[..., None], picked, 0.0)
    return jnp.repeat(picked.reshape(GROUP, 3 * SEEN, -1), TILE, axis=2)


def turned_width(value, step):
    count = lax.axis_size("wa")
    return lax.ppermute(value, "wa", [(i, (i + step) % count) for i in range(count)])


def turned_time(value, step):
    count_t, count_h = lax.axis_size("ta"), lax.axis_size("ha")
    pairs = []
    for t in range(count_t):
        for h in range(count_h):
            t_to = t + step
            h_to = h
            if not 0 <= t_to < count_t:
                h_to = (h + count_h // 2) % count_h
            pairs.append((t * count_h + h, t_to % count_t * count_h + h_to))
    return lax.ppermute(value, ("ta", "ha"), pairs)


def swapped(value, axis, bit):
    count = lax.axis_size(axis)
    return lax.ppermute(value, axis, [(i, i ^ bit) for i in range(count)])


def regrouped(value):
    count = lax.axis_size("ha")
    groups = [list(range(i, i + GROUP)) for i in range(0, count, GROUP)]
    return lax.all_to_all(value, "ha", 0, 0, axis_index_groups=groups)


def log2(count):
    return count.bit_length() - 1


def text_steps():
    ta, ha, wa = (lax.axis_size(axis) for axis in ("ta", "ha", "wa"))
    steps = [("ta", ta >> i) for i in range(1, log2(ta))]
    steps += [("ha", ha >> i) for i in range(1, log2(ha) + 1)]
    steps += [("wa", wa >> i) for i in range(1, log2(wa) + 1)]
    return steps + [("ta", 1)]


def text_bits():
    start = {"wa": 0, "ha": log2(lax.axis_size("wa"))}
    start["ta"] = start["ha"] + log2(lax.axis_size("ha"))
    return tuple(start[axis] + log2(bit) for axis, bit in text_steps())


def is_high(axis, bit):
    return (lax.axis_index(axis) & bit) > 0


def gather_text(value, axis, bit):
    high = is_high(axis, bit)
    mine = theirs = value
    if axis == "ha" and bit < GROUP:
        middle = value.shape[0] // 2
        mine = jnp.where(high, value[middle:], value[:middle])
        theirs = jnp.where(high, value[:middle], value[middle:])
    return jnp.concatenate([mine, swapped(theirs, axis, bit)], 1)


def scatter_text(mine, theirs, axis, bit):
    high = is_high(axis, bit)
    other = swapped(theirs, axis, bit)
    if axis == "ha" and bit < GROUP:
        first = jnp.where(high, other, mine)
        second = jnp.where(high, mine, other)
        return jnp.concatenate([first, second], 0)
    return mine + other


def scatter_halves(value, axis, bit):
    middle = value.shape[1] // 2
    return scatter_text(value[:, :middle], value[:, middle:], axis, bit)


def after(value, *others):
    return lax.optimization_barrier((value, *others))[0]


def local(query, key, value, d_out, text_key, text_value, block_pattern, text_length):
    full = query.shape[-1]
    half = lax.axis_index("ha") // GROUP
    steps = text_steps()
    line = TILES_W * TILE

    def edge(rows, size):
        return jnp.where(half == 0, rows[(GROUP_H - 1) * size :], rows[:size])

    kv_out = pack(
        key.reshape(CUBE, full), value.reshape(CUBE, full), block_pattern.reshape(-1, 27)
    )
    text = jnp.stack([text_key.reshape(-1, HEAD), text_value.reshape(-1, HEAD)], 1)
    text = after(text.reshape(GROUP, 1, -1), kv_out)
    for step in steps[:2]:
        text = gather_text(text, *step)
    qg_out = pack(query.reshape(CUBE, full), d_out.reshape(CUBE, full))
    kv_in = regrouped(kv_out)
    width = kv_in.shape[-1]

    own = kv_in[:, :CUBE].reshape(GROUP_H, TILES_W, TILE, width)
    flat = own.reshape(OWN, width)
    from_left = turned_width(own[:, TILES_W - 1].reshape(SIDE, width), 1)
    from_right = turned_width(own[:, 0].reshape(SIDE, width), -1)
    text = gather_text(after(text, kv_in), *steps[2])
    rim = jnp.concatenate([edge(flat, line), edge(from_left, TILE), edge(from_right, TILE)], 0)
    rim = swapped(rim, "ha", GROUP)
    text = gather_text(after(text, from_left, from_right), *steps[3])
    here = jnp.concatenate([flat, from_left, from_right, rim], 0)
    below = turned_time(here, 1)
    above = turned_time(here, -1)
    qg = regrouped(after(qg_out, here))
    text = after(text, here)
    for step in steps[4:]:
        text = gather_text(text, *step)
    allow = allowed_tiles(kv_in[:, CUBE : CUBE + 8, :27].astype(F32), half)

    me = (lax.axis_index("ta") * lax.axis_size("ha") + lax.axis_index("ha")) * lax.axis_size("wa")
    me = me + lax.axis_index("wa")
    od, here_grad, below_grad, above_grad, text_grad, text_away = attention(
        jnp.concatenate([text_length, me.reshape(1)]),
        allow,
        qg,
        here,
        below,
        above,
        text[0],
        text_bits(),
    )

    first = turned_time(below_grad, -1)
    second = turned_time(above_grad, 1)
    back = steps[::-1]
    text_grad = scatter_text(text_grad[None], text_away[None], *back[0])
    for step in back[1:3]:
        text_grad = scatter_halves(text_grad, *step)
    od_in = regrouped(od)
    halo_sum = here_grad[OWN:] + first[OWN:].astype(F32) + second[OWN:].astype(F32)
    rim_in = swapped(halo_sum[2 * SIDE :].astype(BF16), "ha", GROUP)
    sides = halo_sum[: 2 * SIDE].reshape(2, GROUP_H, TILE, width)
    row = lax.broadcasted_iota(jnp.int32, (1, GROUP_H, 1, 1), 1)
    at_edge = row == jnp.where(half == 0, GROUP_H - 1, 0)
    extra = rim_in[line:].astype(F32).reshape(2, 1, TILE, width)
    sides = (sides + jnp.where(at_edge, extra, 0.0)).astype(BF16).reshape(2, SIDE, width)
    right = turned_width(sides[0], -1)
    left = turned_width(sides[1], 1)
    text_grad = scatter_halves(after(text_grad, rim_in, od_in), *back[3])
    grads = settle(half.reshape(1), here_grad, first, second, rim_in, left, right)
    text_grad = after(text_grad, grads)
    for step in back[4:]:
        text_grad = scatter_halves(text_grad, *step)
    attended, query_grad = unpack(od_in)
    key_grad, value_grad = unpack(regrouped(grads))
    text_grad = text_grad.astype(BF16).reshape(-1, 2, HEAD)
    return (
        attended.reshape(query.shape),
        query_grad.reshape(query.shape),
        key_grad.reshape(query.shape),
        value_grad.reshape(query.shape),
        text_grad[:, 0].reshape(1, full),
        text_grad[:, 1].reshape(1, full),
    )


def solution(mesh):
    cube = P("ta", "ha", "wa", None)
    text = P(("ta", "ha", "wa"), None)
    return jax.shard_map(
        local,
        mesh=mesh,
        in_specs=(cube, cube, cube, cube, text, text, cube, P()),
        out_specs=(cube, cube, cube, cube, text, text),
        check_vma=False,
    )
```

```python
import functools

import jax
import jax.numpy as jnp
import numpy as np
from jax import lax
from jax.experimental import pallas as pl
from jax.experimental.pallas import tpu as pltpu
from jax.sharding import PartitionSpec as P

HEAD = 128
PAIR = 2 * HEAD
TILE_T = 2
TILE_H = 2
TILE_W = 4
TILE = TILE_T * TILE_H * TILE_W
NEGATIVE = -1e30
LOG2E = 1.4426950408889634
EXTRA = 16
PACKS = 2
VMEM = 58 * 1024 * 1024
F32 = jnp.float32
BF16 = jnp.bfloat16

ROWS = 4
COLS = 16
TILES_H = ROWS // TILE_H
TILES_W = COLS // TILE_W
CUBE = TILE_T * ROWS * COLS
GROUP = 4
GROUP_H = GROUP * TILES_H
OWN = GROUP_H * TILES_W * TILE
SIDE = GROUP_H * TILE
RIM = (TILES_W + 2) * TILE
ALL = OWN + 2 * SIDE + RIM
SEEN = (TILES_H + 2) * (TILES_W + 2)


def natural_index(row):
    tile_h = row >> 6
    tile_w = (row >> 4) & 3
    t = (row >> 3) & 1
    h = (row >> 2) & 1
    w = row & 3
    return t * (ROWS * COLS) + (tile_h * TILE_H + h) * COLS + tile_w * TILE_W + w


def pack_kernel(first_ref, second_ref, *rest):
    out_ref = rest[-1]
    row = lax.broadcasted_iota(jnp.int32, (CUBE, CUBE), 0)
    col = lax.broadcasted_iota(jnp.int32, (CUBE, CUBE), 1)
    order = jnp.where(natural_index(row) == col, 1.0, 0.0).astype(BF16)
    first = jnp.dot(order, first_ref[...], preferred_element_type=F32).astype(BF16)
    second = jnp.dot(order, second_ref[...], preferred_element_type=F32).astype(BF16)
    groups, _, width = out_ref.shape
    heads = width // PAIR
    for group in range(groups):
        for i in range(heads):
            source = slice((group * heads + i) * HEAD, (group * heads + i + 1) * HEAD)
            out_ref[group, :CUBE, i * PAIR : i * PAIR + HEAD] = first[:, source]
            out_ref[group, :CUBE, i * PAIR + HEAD : (i + 1) * PAIR] = second[:, source]
        if len(rest) > 1:
            pattern = rest[0][...].astype(F32)
            lines = jnp.concatenate([pattern, jnp.zeros_like(pattern)], 0).astype(BF16)
            out_ref[group, CUBE:, :] = jnp.zeros((EXTRA, width), BF16)
            out_ref[group, CUBE:, : pattern.shape[1]] = lines


def pack(first, second, pattern=None):
    width = first.shape[1] // GROUP
    step = GROUP // PACKS
    rows = CUBE + (0 if pattern is None else EXTRA)
    specs = [pl.BlockSpec((CUBE, width * step), lambda g: (0, g))] * 2
    extras = ()
    if pattern is not None:
        specs.append(pl.BlockSpec(pattern.shape, lambda g: (0, 0)))
        extras = (pattern,)
    return pl.pallas_call(
        pack_kernel,
        grid=(PACKS,),
        in_specs=specs,
        out_specs=pl.BlockSpec((step, rows, 2 * width), lambda g: (g, 0, 0)),
        out_shape=jax.ShapeDtypeStruct((GROUP, rows, 2 * width), BF16),
        compiler_params=pltpu.CompilerParams(vmem_limit_bytes=VMEM),
    )(first, second, *extras)


def unpack_kernel(packed_ref, first_ref, second_ref):
    row = lax.broadcasted_iota(jnp.int32, (CUBE, CUBE), 0)
    col = lax.broadcasted_iota(jnp.int32, (CUBE, CUBE), 1)
    order = jnp.where(natural_index(col) == row, 1.0, 0.0).astype(BF16)
    groups, _, width = packed_ref.shape
    heads = width // PAIR
    for group in range(groups):
        both = jnp.dot(order, packed_ref[group], preferred_element_type=F32).astype(BF16)
        for i in range(heads):
            target = slice((group * heads + i) * HEAD, (group * heads + i + 1) * HEAD)
            first_ref[:, target] = both[:, i * PAIR : i * PAIR + HEAD]
            second_ref[:, target] = both[:, i * PAIR + HEAD : (i + 1) * PAIR]


def unpack(packed):
    _, rows, width = packed.shape
    step = GROUP // PACKS
    half = width // 2
    return pl.pallas_call(
        unpack_kernel,
        grid=(PACKS,),
        in_specs=[pl.BlockSpec((step, rows, width), lambda g: (g, 0, 0))],
        out_specs=[pl.BlockSpec((CUBE, half * step), lambda g: (0, g))] * 2,
        out_shape=[jax.ShapeDtypeStruct((CUBE, GROUP * half), BF16)] * 2,
        compiler_params=pltpu.CompilerParams(vmem_limit_bytes=VMEM),
    )(packed)


def block_rows(block):
    low, high = block * TILES_H - 1, (block + 1) * TILES_H + 1
    outer = -1 if low < 0 else GROUP_H if high > GROUP_H else None
    return max(low, 0), min(high, GROUP_H), outer


def seen_tiles(block):
    low, high, outer = block_rows(block)
    tiles = [(h, w) for h in range(low, high) for w in range(TILES_W)]
    tiles += [(h, -1) for h in range(low, high)] + [(h, TILES_W) for h in range(low, high)]
    if outer is not None:
        tiles += [(outer, w) for w in (*range(TILES_W), -1, TILES_W)]
    return tiles


def attention_kernel(
    text_bits,
    length_ref,
    allow_ref,
    qg_ref,
    here_ref,
    below_ref,
    above_ref,
    text_ref,
    od_ref,
    here_out,
    below_out,
    above_out,
    text_out,
    text_away_out,
    below_sum,
    above_sum,
):
    text_count = text_ref.shape[0]
    scale = HEAD**-0.5
    near = (here_ref, below_ref, above_ref)
    sums = (here_out, below_sum, above_sum)
    text_row = lax.broadcasted_iota(jnp.int32, (text_count, CUBE), 0)
    text_place = jnp.zeros_like(text_row)
    for bit, place in enumerate(text_bits):
        text_place += ((text_row >> bit) & 1) << place
    text_ok = (text_place ^ length_ref[1]) < length_ref[0]
    blank = jnp.zeros((CUBE, HEAD), BF16)
    text_kv = text_ref[...]
    line = TILES_W * TILE
    def look(block):
        low, high, outer = block_rows(block)
        count = high - low
        q = qg_ref[block, :, :HEAD]
        g = qg_ref[block, :, HEAD:]
        both = jnp.concatenate(
            [jnp.concatenate([q, blank], 1), jnp.concatenate([blank, g], 1)], 0
        )
        done = 0 if block == 0 else 2
        places = [(low * line, count * line, done * line)]
        for side in range(2):
            places.append((OWN + side * SIDE + low * TILE, count * TILE, done * TILE))
        if outer is not None:
            places.append((OWN + 2 * SIDE, RIM, 0 if block == 0 else RIM))
        keys = []
        masks = []
        for i in range(3):
            parts = [near[i][first : first + size, :] for first, size, _ in places]
            keys.append(jnp.concatenate(parts, 0))
            tiles = allow_ref[block, i * SEEN : (i + 1) * SEEN, :]
            spread = jnp.broadcast_to(tiles[:, None, :], (SEEN, TILE, CUBE))
            masks.append(spread.reshape(SEEN * TILE, CUBE) > 0.5)
        keys.append(text_kv)
        masks.append(text_ok)
        scores = []
        dprobs = []
        for kv, ok in zip(keys, masks):
            mixed = lax.dot_general(
                kv, both, (((1,), (1,)), ((), ())), preferred_element_type=F32
            )
            scores.append(jnp.where(ok, mixed[:, :HEAD] * (scale * LOG2E), NEGATIVE))
            dprobs.append(mixed[:, HEAD:])
        top = functools.reduce(jnp.maximum, [jnp.max(s, 0, keepdims=True) for s in scores])
        return g, both, places, keys, scores, dprobs, top

    def finish(block, found):
        g, both, places, keys, scores, dprobs, top = found
        exps = [jnp.exp2(s - top) for s in scores]
        total = functools.reduce(jnp.add, [jnp.sum(e, 0, keepdims=True) for e in exps])
        inverse = 1.0 / total
        weights = [(e * inverse).astype(BF16) for e in exps]
        attended = jnp.zeros((CUBE, HEAD), F32)
        for w, kv in zip(weights, keys):
            attended += lax.dot_general(
                w, kv[:, HEAD:], (((0,), (0,)), ((), ())), preferred_element_type=F32
            )
        attended = attended.astype(BF16)
        od_ref[block, :, :HEAD] = attended
        product = g.astype(F32) * attended.astype(F32)
        delta = jnp.sum(product.T, 0, keepdims=True)
        dscores = [(e * ((d - delta) * inverse)).astype(BF16) for e, d in zip(exps, dprobs)]
        return both, places, keys, weights, dscores

    def settle_block(block, state):
        both, places, keys, weights, dscores = state
        query_grad = jnp.zeros((CUBE, HEAD), F32)
        for d, kv in zip(dscores, keys):
            query_grad += lax.dot_general(
                d, kv[:, :HEAD], (((0,), (0,)), ((), ())), preferred_element_type=F32
            )
        od_ref[block, :, HEAD:] = (query_grad * scale).astype(BF16)
        for i in range(4):
            change = jnp.dot(
                jnp.concatenate([dscores[i], weights[i]], 1), both, preferred_element_type=F32
            )
            if i == 3:
                middle = text_count // 2
                for target, piece in (
                    (text_out, change[:middle]),
                    (text_away_out, change[middle:]),
                ):
                    if block == 0:
                        target[...] = piece
                    else:
                        target[...] += piece
                continue
            taken = 0
            target = sums[i]
            for first, size, old in places:
                if old:
                    target[first : first + old, :] += change[taken : taken + old]
                if old < size:
                    target[first + old : first + size, :] = change[taken + old : taken + size]
                taken += size
    found = look(0)
    before = None
    for block in range(GROUP):
        following = look(block + 1) if block + 1 < GROUP else None
        now = finish(block, found)
        if before is not None:
            settle_block(block - 1, before)
        before = now
        found = following
    settle_block(GROUP - 1, before)
    lane = lax.broadcasted_iota(jnp.int32, (1, PAIR), 1)
    factor = jnp.where(lane < HEAD, scale, 1.0).astype(F32)
    here_out[...] = here_out[...] * factor
    below_out[...] = (below_sum[...] * factor).astype(BF16)
    above_out[...] = (above_sum[...] * factor).astype(BF16)
    text_out[...] = text_out[...] * factor
    text_away_out[...] = text_away_out[...] * factor


def attention(length, allow, qg, here, below, above, text, text_bits):
    width = qg.shape[-1]
    heads = width // PAIR
    text_count = text.shape[0]

    def spec(rows):
        return pl.BlockSpec((rows, PAIR), lambda h: (0, h))

    def shape(rows, dtype):
        return jax.ShapeDtypeStruct((rows, width), dtype)

    part = pl.BlockSpec((GROUP, CUBE, PAIR), lambda h: (0, 0, h))
    return pl.pallas_call(
        functools.partial(attention_kernel, text_bits),
        grid=(heads,),
        in_specs=[
            pl.BlockSpec(memory_space=pltpu.SMEM),
            pl.BlockSpec(allow.shape, lambda h: (0, 0, 0)),
            part,
        ]
        + [spec(ALL)] * 3
        + [spec(text_count)],
        out_specs=[part] + [spec(ALL)] * 3 + [spec(text_count // 2)] * 2,
        out_shape=[
            jax.ShapeDtypeStruct(qg.shape, BF16),
            shape(ALL, F32),
            shape(ALL, BF16),
            shape(ALL, BF16),
            shape(text_count // 2, F32),
            shape(text_count // 2, F32),
        ],
        scratch_shapes=[pltpu.VMEM((rows, PAIR), F32) for rows in (ALL, ALL)],
        compiler_params=pltpu.CompilerParams(vmem_limit_bytes=VMEM),
    )(length, allow, qg, here, below, above, text)


def settle_kernel(half_ref, own_ref, first_ref, second_ref, rim_ref, left_ref, right_ref, out_ref):
    line = TILES_W * TILE
    rim = rim_ref[...].astype(F32)
    half = half_ref[0]
    groups = out_ref.shape[0]
    for group in range(groups):
        block = pl.program_id(0) * groups + group
        cube = slice(group * CUBE, (group + 1) * CUBE)
        total = own_ref[cube] + first_ref[cube].astype(F32) + second_ref[cube].astype(F32)
        for i in range(TILES_H):
            edge = (block == 0) & (half == 1) if i == 0 else (block == GROUP - 1) & (half == 0)
            part = total[i * line : (i + 1) * line]
            part += jnp.where(edge, rim, 0.0)
            here = slice((group * TILES_H + i) * TILE, (group * TILES_H + i + 1) * TILE)
            pieces = [
                part[:TILE] + left_ref[here].astype(F32),
                part[TILE : line - TILE],
                part[line - TILE :] + right_ref[here].astype(F32),
            ]
            out_ref[group, i * line : (i + 1) * line, :] = jnp.concatenate(pieces, 0).astype(BF16)


def settle(half, own, first, second, rim, left, right):
    width = own.shape[-1]
    step = GROUP // PACKS

    def spec(rows):
        return pl.BlockSpec((rows * step, width), lambda b: (b, 0))

    return pl.pallas_call(
        settle_kernel,
        grid=(PACKS,),
        in_specs=[
            pl.BlockSpec(memory_space=pltpu.SMEM),
            spec(CUBE),
            spec(CUBE),
            spec(CUBE),
            pl.BlockSpec((TILES_W * TILE, width), lambda b: (0, 0)),
            spec(TILES_H * TILE),
            spec(TILES_H * TILE),
        ],
        out_specs=pl.BlockSpec((step, CUBE, width), lambda b: (b, 0, 0)),
        out_shape=jax.ShapeDtypeStruct((GROUP, CUBE, width), BF16),
        compiler_params=pltpu.CompilerParams(vmem_limit_bytes=VMEM),
    )(half, own, first, second, rim, left, right)


def offset_table():
    table = np.full((GROUP, 3, SEEN, TILES_H, TILES_W), -1, np.int32)
    for block in range(GROUP):
        for k, (kh, kw) in enumerate(seen_tiles(block)):
            for qh in range(TILES_H):
                for qw in range(TILES_W):
                    dh, dw = kh - (block * TILES_H + qh), kw - qw
                    if abs(dh) <= 1 and abs(dw) <= 1:
                        for i, dt in enumerate((0, -1, 1)):
                            table[block, i, k, qh, qw] = 9 * dt + 3 * dh + dw + 13
    return table


def allowed_tiles(pattern, half):
    hot = offset_table().reshape(GROUP, 3, SEEN, -1)[..., None] == np.arange(27)
    picked = jnp.sum(jnp.where(hot, pattern[:, None, None], 0.0), -1)
    places = np.array([seen_tiles(block) for block in range(GROUP)])
    t = lax.axis_index("ta") + jnp.array([0, -1, 1])
    t_ok = (t >= 0) & (t < lax.axis_size("ta"))
    w = lax.axis_index("wa") * TILES_W + places[..., 1]
    w_ok = (w >= 0) & (w < TILES_W * lax.axis_size("wa"))
    h = half * GROUP_H + places[..., 0]
    h_ok = (h >= 0) & (h < TILES_H * lax.axis_size("ha"))
    inside = t_ok[None, :, None] & (w_ok & h_ok)[:, None, :]
    picked = jnp.where(inside[..., None], picked, 0.0)
    return jnp.repeat(picked.reshape(GROUP, 3 * SEEN, -1), TILE, axis=2)


def turned_width(value, step):
    count = lax.axis_size("wa")
    return lax.ppermute(value, "wa", [(i, (i + step) % count) for i in range(count)])


def turned_time(value, step):
    count_t, count_h = lax.axis_size("ta"), lax.axis_size("ha")
    pairs = []
    for t in range(count_t):
        for h in range(count_h):
            t_to = t + step
            h_to = h
            if not 0 <= t_to < count_t:
                h_to = (h + count_h // 2) % count_h
            pairs.append((t * count_h + h, t_to % count_t * count_h + h_to))
    return lax.ppermute(value, ("ta", "ha"), pairs)


def swapped(value, axis, bit):
    count = lax.axis_size(axis)
    return lax.ppermute(value, axis, [(i, i ^ bit) for i in range(count)])


def regrouped(value):
    count = lax.axis_size("ha")
    groups = [list(range(i, i + GROUP)) for i in range(0, count, GROUP)]
    return lax.all_to_all(value, "ha", 0, 0, axis_index_groups=groups)


def log2(count):
    return count.bit_length() - 1


def text_steps():
    ta, ha, wa = (lax.axis_size(axis) for axis in ("ta", "ha", "wa"))
    halves = [("ha", ha >> i) for i in range(1, log2(ha) + 1)]
    steps = halves[:-2] + [("ta", ta >> i) for i in range(1, log2(ta))] + halves[-2:]
    steps += [("wa", wa >> i) for i in range(1, log2(wa) + 1)]
    return steps + [("ta", 1)]


def text_bits():
    start = {"wa": 0, "ha": log2(lax.axis_size("wa"))}
    start["ta"] = start["ha"] + log2(lax.axis_size("ha"))
    return tuple(start[axis] + log2(bit) for axis, bit in text_steps())


def is_high(axis, bit):
    return (lax.axis_index(axis) & bit) > 0


def gather_text(value, axis, bit):
    high = is_high(axis, bit)
    mine = theirs = value
    if axis == "ha" and bit < GROUP:
        middle = value.shape[0] // 2
        mine = jnp.where(high, value[middle:], value[:middle])
        theirs = jnp.where(high, value[:middle], value[middle:])
    return jnp.concatenate([mine, swapped(theirs, axis, bit)], 1)


def scatter_text(mine, theirs, axis, bit):
    high = is_high(axis, bit)
    other = swapped(theirs, axis, bit)
    if axis == "ha" and bit < GROUP:
        first = jnp.where(high, other, mine)
        second = jnp.where(high, mine, other)
        return jnp.concatenate([first, second], 0)
    return mine + other


def scatter_halves(value, axis, bit):
    middle = value.shape[1] // 2
    return scatter_text(value[:, :middle], value[:, middle:], axis, bit)


def after(value, *others):
    return lax.optimization_barrier((value, *others))[0]


def local(query, key, value, d_out, text_key, text_value, block_pattern, text_length):
    full = query.shape[-1]
    half = lax.axis_index("ha") // GROUP
    steps = text_steps()
    line = TILES_W * TILE

    kv_out = pack(
        key.reshape(CUBE, full), value.reshape(CUBE, full), block_pattern.reshape(-1, 27)
    )
    text = jnp.stack([text_key.reshape(-1, HEAD), text_value.reshape(-1, HEAD)], 1)
    text = after(text.reshape(GROUP, 1, -1), kv_out)
    for step in steps[:3]:
        text = gather_text(text, *step)
    qg_out = pack(query.reshape(CUBE, full), d_out.reshape(CUBE, full))
    kv_in = regrouped(kv_out)
    width = kv_in.shape[-1]

    own = kv_in[:, :CUBE].reshape(GROUP_H, TILES_W, TILE, width)
    flat = own.reshape(OWN, width)
    edge = jnp.where(half == 0, own[GROUP_H - 1], own[0])
    rim = swapped(edge.reshape(line, width), "ha", GROUP)
    text = gather_text(after(text, kv_in), *steps[3])
    to_right = jnp.concatenate([own[:, TILES_W - 1].reshape(SIDE, width), rim[line - TILE :]], 0)
    to_left = jnp.concatenate([own[:, 0].reshape(SIDE, width), rim[:TILE]], 0)
    left = turned_width(to_right, 1)
    right = turned_width(to_left, -1)
    text = after(text, rim)
    for step in steps[4:6]:
        text = gather_text(text, *step)
    here = jnp.concatenate([flat, left[:SIDE], right[:SIDE], rim, left[SIDE:], right[SIDE:]], 0)
    below = turned_time(here, 1)
    above = turned_time(here, -1)
    qg = regrouped(after(qg_out, here))
    text = after(text, here)
    for step in steps[6:]:
        text = gather_text(text, *step)
    allow = allowed_tiles(kv_in[:, CUBE : CUBE + 8, :27].astype(F32), half)

    me = (lax.axis_index("ta") * lax.axis_size("ha") + lax.axis_index("ha")) * lax.axis_size("wa")
    me = me + lax.axis_index("wa")
    od, here_grad, below_grad, above_grad, text_grad, text_away = attention(
        jnp.concatenate([text_length, me.reshape(1)]),
        allow,
        qg,
        here,
        below,
        above,
        text[0],
        text_bits(),
    )

    first = turned_time(below_grad, -1)
    second = turned_time(above_grad, 1)
    back = steps[::-1]
    text_grad = scatter_text(text_grad[None], text_away[None], *back[0])
    for step in back[1:4]:
        text_grad = scatter_halves(text_grad, *step)
    od_in = regrouped(od)
    halo = here_grad[OWN:] + first[OWN:].astype(F32) + second[OWN:].astype(F32)
    rim_grad = halo[2 * SIDE : 2 * SIDE + line]
    corner = 2 * SIDE + line
    to_left = jnp.concatenate([halo[:SIDE], halo[corner : corner + TILE]], 0).astype(BF16)
    to_right = jnp.concatenate([halo[SIDE : 2 * SIDE], halo[corner + TILE :]], 0).astype(BF16)
    right = turned_width(to_left, -1)
    left = turned_width(to_right, 1)
    text_grad = scatter_halves(after(text_grad, to_left, to_right, od_in), *back[4])
    rim_out = jnp.concatenate(
        [
            rim_grad[:TILE] + left[SIDE:].astype(F32),
            rim_grad[TILE : line - TILE],
            rim_grad[line - TILE :] + right[SIDE:].astype(F32),
        ],
        0,
    ).astype(BF16)
    rim_in = swapped(rim_out, "ha", GROUP)
    text_grad = scatter_halves(after(text_grad, rim_out), *back[5])
    grads = settle(half.reshape(1), here_grad, first, second, rim_in, left, right)
    text_grad = after(text_grad, grads)
    for step in back[6:]:
        text_grad = scatter_halves(text_grad, *step)
    attended, query_grad = unpack(od_in)
    key_grad, value_grad = unpack(regrouped(grads))
    text_grad = text_grad.astype(BF16).reshape(-1, 2, HEAD)
    return (
        attended.reshape(query.shape),
        query_grad.reshape(query.shape),
        key_grad.reshape(query.shape),
        value_grad.reshape(query.shape),
        text_grad[:, 0].reshape(1, full),
        text_grad[:, 1].reshape(1, full),
    )


def solution(mesh):
    cube = P("ta", "ha", "wa", None)
    text = P(("ta", "ha", "wa"), None)
    return jax.shard_map(
        local,
        mesh=mesh,
        in_specs=(cube, cube, cube, cube, text, text, cube, P()),
        out_specs=(cube, cube, cube, cube, text, text),
        check_vma=False,
    )
```

```python
import functools

import jax
import jax.numpy as jnp
import numpy as np
from jax import lax
from jax.experimental import pallas as pl
from jax.experimental.pallas import tpu as pltpu
from jax.sharding import PartitionSpec as P

HEAD = 128
PAIR = 2 * HEAD
TILE_T = 2
TILE_H = 2
TILE_W = 4
TILE = TILE_T * TILE_H * TILE_W
NEGATIVE = -1e30
LOG2E = 1.4426950408889634
EXTRA = 16
PACKS = 2
VMEM = 58 * 1024 * 1024
F32 = jnp.float32
BF16 = jnp.bfloat16

ROWS = 4
COLS = 16
TILES_H = ROWS // TILE_H
TILES_W = COLS // TILE_W
CUBE = TILE_T * ROWS * COLS
GROUP = 4
GROUP_H = GROUP * TILES_H
OWN = GROUP_H * TILES_W * TILE
SIDE = GROUP_H * TILE
RIM = (TILES_W + 2) * TILE
ALL = OWN + 2 * SIDE + RIM
SEEN = (TILES_H + 2) * (TILES_W + 2)


def natural_index(row):
    tile_h = row >> 6
    tile_w = (row >> 4) & 3
    t = (row >> 3) & 1
    h = (row >> 2) & 1
    w = row & 3
    return t * (ROWS * COLS) + (tile_h * TILE_H + h) * COLS + tile_w * TILE_W + w


def pack_kernel(first_ref, second_ref, *rest):
    out_ref = rest[-1]
    row = lax.broadcasted_iota(jnp.int32, (CUBE, CUBE), 0)
    col = lax.broadcasted_iota(jnp.int32, (CUBE, CUBE), 1)
    order = jnp.where(natural_index(row) == col, 1.0, 0.0).astype(BF16)
    first = jnp.dot(order, first_ref[...], preferred_element_type=F32).astype(BF16)
    second = jnp.dot(order, second_ref[...], preferred_element_type=F32).astype(BF16)
    groups, _, width = out_ref.shape
    heads = width // PAIR
    for group in range(groups):
        for i in range(heads):
            source = slice((group * heads + i) * HEAD, (group * heads + i + 1) * HEAD)
            out_ref[group, :CUBE, i * PAIR : i * PAIR + HEAD] = first[:, source]
            out_ref[group, :CUBE, i * PAIR + HEAD : (i + 1) * PAIR] = second[:, source]
        if len(rest) > 1:
            pattern = rest[0][...].astype(F32)
            lines = jnp.concatenate([pattern, jnp.zeros_like(pattern)], 0).astype(BF16)
            out_ref[group, CUBE:, :] = jnp.zeros((EXTRA, width), BF16)
            out_ref[group, CUBE:, : pattern.shape[1]] = lines


def pack(first, second, pattern=None):
    width = first.shape[1] // GROUP
    step = GROUP // PACKS
    rows = CUBE + (0 if pattern is None else EXTRA)
    specs = [pl.BlockSpec((CUBE, width * step), lambda g: (0, g))] * 2
    extras = ()
    if pattern is not None:
        specs.append(pl.BlockSpec(pattern.shape, lambda g: (0, 0)))
        extras = (pattern,)
    return pl.pallas_call(
        pack_kernel,
        grid=(PACKS,),
        in_specs=specs,
        out_specs=pl.BlockSpec((step, rows, 2 * width), lambda g: (g, 0, 0)),
        out_shape=jax.ShapeDtypeStruct((GROUP, rows, 2 * width), BF16),
        compiler_params=pltpu.CompilerParams(vmem_limit_bytes=VMEM),
    )(first, second, *extras)


def unpack_kernel(packed_ref, first_ref, second_ref):
    row = lax.broadcasted_iota(jnp.int32, (CUBE, CUBE), 0)
    col = lax.broadcasted_iota(jnp.int32, (CUBE, CUBE), 1)
    order = jnp.where(natural_index(col) == row, 1.0, 0.0).astype(BF16)
    groups, _, width = packed_ref.shape
    heads = width // PAIR
    for group in range(groups):
        both = jnp.dot(order, packed_ref[group], preferred_element_type=F32).astype(BF16)
        for i in range(heads):
            target = slice((group * heads + i) * HEAD, (group * heads + i + 1) * HEAD)
            first_ref[:, target] = both[:, i * PAIR : i * PAIR + HEAD]
            second_ref[:, target] = both[:, i * PAIR + HEAD : (i + 1) * PAIR]


def unpack(packed):
    _, rows, width = packed.shape
    step = GROUP // PACKS
    half = width // 2
    return pl.pallas_call(
        unpack_kernel,
        grid=(PACKS,),
        in_specs=[pl.BlockSpec((step, rows, width), lambda g: (g, 0, 0))],
        out_specs=[pl.BlockSpec((CUBE, half * step), lambda g: (0, g))] * 2,
        out_shape=[jax.ShapeDtypeStruct((CUBE, GROUP * half), BF16)] * 2,
        compiler_params=pltpu.CompilerParams(vmem_limit_bytes=VMEM),
    )(packed)


def block_rows(block):
    low, high = block * TILES_H - 1, (block + 1) * TILES_H + 1
    outer = -1 if low < 0 else GROUP_H if high > GROUP_H else None
    return max(low, 0), min(high, GROUP_H), outer


def seen_tiles(block):
    low, high, outer = block_rows(block)
    tiles = [(h, w) for h in range(low, high) for w in range(TILES_W)]
    tiles += [(h, -1) for h in range(low, high)] + [(h, TILES_W) for h in range(low, high)]
    if outer is not None:
        tiles += [(outer, w) for w in (*range(TILES_W), -1, TILES_W)]
    return tiles


def attention_kernel(
    text_bits,
    length_ref,
    allow_ref,
    qg_ref,
    here_ref,
    below_ref,
    above_ref,
    text_ref,
    od_ref,
    here_out,
    below_out,
    above_out,
    text_out,
    text_away_out,
    below_sum,
    above_sum,
):
    text_count = text_ref.shape[0]
    scale = HEAD**-0.5
    near = (here_ref, below_ref, above_ref)
    sums = (here_out, below_sum, above_sum)
    text_row = lax.broadcasted_iota(jnp.int32, (text_count, CUBE), 0)
    text_place = jnp.zeros_like(text_row)
    for bit, place in enumerate(text_bits):
        text_place += ((text_row >> bit) & 1) << place
    text_ok = (text_place ^ length_ref[1]) < length_ref[0]
    blank = jnp.zeros((CUBE, HEAD), BF16)
    text_kv = text_ref[...]
    line = TILES_W * TILE
    def look(block):
        low, high, outer = block_rows(block)
        count = high - low
        q = qg_ref[block, :, :HEAD]
        g = qg_ref[block, :, HEAD:]
        both = jnp.concatenate(
            [jnp.concatenate([q, blank], 1), jnp.concatenate([blank, g], 1)], 0
        )
        done = 0 if block == 0 else 2
        places = [(low * line, count * line, done * line)]
        for side in range(2):
            places.append((OWN + side * (SIDE + TILE) + low * TILE, count * TILE, done * TILE))
        if outer is not None:
            rim = (OWN + 2 * (SIDE + TILE), OWN + SIDE, OWN + 2 * SIDE + TILE)
            for first, size in zip(rim, (line, TILE, TILE)):
                places.append((first, size, 0 if block == 0 else size))
        keys = []
        masks = []
        for i in range(3):
            parts = [near[i][first : first + size, :] for first, size, _ in places]
            keys.append(jnp.concatenate(parts, 0))
            tiles = allow_ref[block, i * SEEN : (i + 1) * SEEN, :]
            spread = jnp.broadcast_to(tiles[:, None, :], (SEEN, TILE, CUBE))
            masks.append(spread.reshape(SEEN * TILE, CUBE) > 0.5)
        keys.append(text_kv)
        masks.append(text_ok)
        scores = []
        dprobs = []
        for kv, ok in zip(keys, masks):
            mixed = lax.dot_general(
                kv, both, (((1,), (1,)), ((), ())), preferred_element_type=F32
            )
            scores.append(jnp.where(ok, mixed[:, :HEAD] * (scale * LOG2E), NEGATIVE))
            dprobs.append(mixed[:, HEAD:])
        top = functools.reduce(jnp.maximum, [jnp.max(s, 0, keepdims=True) for s in scores])
        return g, both, places, keys, scores, dprobs, top

    def finish(block, found):
        g, both, places, keys, scores, dprobs, top = found
        exps = [jnp.exp2(s - top) for s in scores]
        total = functools.reduce(jnp.add, [jnp.sum(e, 0, keepdims=True) for e in exps])
        inverse = 1.0 / total
        weights = [(e * inverse).astype(BF16) for e in exps]
        attended = jnp.zeros((CUBE, HEAD), F32)
        for w, kv in zip(weights, keys):
            attended += lax.dot_general(
                w, kv[:, HEAD:], (((0,), (0,)), ((), ())), preferred_element_type=F32
            )
        attended = attended.astype(BF16)
        od_ref[block, :, :HEAD] = attended
        product = g.astype(F32) * attended.astype(F32)
        delta = jnp.sum(product.T, 0, keepdims=True)
        dscores = [(e * ((d - delta) * inverse)).astype(BF16) for e, d in zip(exps, dprobs)]
        return both, places, keys, weights, dscores

    def settle_block(block, state):
        both, places, keys, weights, dscores = state
        query_grad = jnp.zeros((CUBE, HEAD), F32)
        for d, kv in zip(dscores, keys):
            query_grad += lax.dot_general(
                d, kv[:, :HEAD], (((0,), (0,)), ((), ())), preferred_element_type=F32
            )
        od_ref[block, :, HEAD:] = (query_grad * scale).astype(BF16)
        for i in range(4):
            change = jnp.dot(
                jnp.concatenate([dscores[i], weights[i]], 1), both, preferred_element_type=F32
            )
            if i == 3:
                middle = text_count // 2
                for target, piece in (
                    (text_out, change[:middle]),
                    (text_away_out, change[middle:]),
                ):
                    if block == 0:
                        target[...] = piece
                    else:
                        target[...] += piece
                continue
            taken = 0
            target = sums[i]
            for first, size, old in places:
                if old:
                    target[first : first + old, :] += change[taken : taken + old]
                if old < size:
                    target[first + old : first + size, :] = change[taken + old : taken + size]
                taken += size
    found = look(0)
    before = None
    for block in range(GROUP):
        following = look(block + 1) if block + 1 < GROUP else None
        now = finish(block, found)
        if before is not None:
            settle_block(block - 1, before)
        before = now
        found = following
    settle_block(GROUP - 1, before)
    lane = lax.broadcasted_iota(jnp.int32, (1, PAIR), 1)
    factor = jnp.where(lane < HEAD, scale, 1.0).astype(F32)
    here_out[...] = here_out[...] * factor
    below_out[...] = (below_sum[...] * factor).astype(BF16)
    above_out[...] = (above_sum[...] * factor).astype(BF16)
    text_out[...] = text_out[...] * factor
    text_away_out[...] = text_away_out[...] * factor


def attention(length, allow, qg, here, below, above, text, text_bits):
    width = qg.shape[-1]
    heads = width // PAIR
    text_count = text.shape[0]

    def spec(rows):
        return pl.BlockSpec((rows, PAIR), lambda h: (0, h))

    def shape(rows, dtype):
        return jax.ShapeDtypeStruct((rows, width), dtype)

    part = pl.BlockSpec((GROUP, CUBE, PAIR), lambda h: (0, 0, h))
    return pl.pallas_call(
        functools.partial(attention_kernel, text_bits),
        grid=(heads,),
        in_specs=[
            pl.BlockSpec(memory_space=pltpu.SMEM),
            pl.BlockSpec(allow.shape, lambda h: (0, 0, 0)),
            part,
        ]
        + [spec(ALL)] * 3
        + [spec(text_count)],
        out_specs=[part] + [spec(ALL)] * 3 + [spec(text_count // 2)] * 2,
        out_shape=[
            jax.ShapeDtypeStruct(qg.shape, BF16),
            shape(ALL, F32),
            shape(ALL, BF16),
            shape(ALL, BF16),
            shape(text_count // 2, F32),
            shape(text_count // 2, F32),
        ],
        scratch_shapes=[pltpu.VMEM((rows, PAIR), F32) for rows in (ALL, ALL)],
        compiler_params=pltpu.CompilerParams(vmem_limit_bytes=VMEM),
    )(length, allow, qg, here, below, above, text)


def settle_kernel(half_ref, own_ref, first_ref, second_ref, rim_ref, left_ref, right_ref, out_ref):
    line = TILES_W * TILE
    rim = rim_ref[...].astype(F32)
    half = half_ref[0]
    groups = out_ref.shape[0]
    for group in range(groups):
        block = pl.program_id(0) * groups + group
        cube = slice(group * CUBE, (group + 1) * CUBE)
        total = own_ref[cube] + first_ref[cube].astype(F32) + second_ref[cube].astype(F32)
        for i in range(TILES_H):
            edge = (block == 0) & (half == 1) if i == 0 else (block == GROUP - 1) & (half == 0)
            part = total[i * line : (i + 1) * line]
            part += jnp.where(edge, rim, 0.0)
            here = slice((group * TILES_H + i) * TILE, (group * TILES_H + i + 1) * TILE)
            pieces = [
                part[:TILE] + left_ref[here].astype(F32),
                part[TILE : line - TILE],
                part[line - TILE :] + right_ref[here].astype(F32),
            ]
            out_ref[group, i * line : (i + 1) * line, :] = jnp.concatenate(pieces, 0).astype(BF16)


def settle(half, own, first, second, rim, left, right):
    width = own.shape[-1]
    step = GROUP // PACKS

    def spec(rows):
        return pl.BlockSpec((rows * step, width), lambda b: (b, 0))

    return pl.pallas_call(
        settle_kernel,
        grid=(PACKS,),
        in_specs=[
            pl.BlockSpec(memory_space=pltpu.SMEM),
            spec(CUBE),
            spec(CUBE),
            spec(CUBE),
            pl.BlockSpec((TILES_W * TILE, width), lambda b: (0, 0)),
            spec(TILES_H * TILE),
            spec(TILES_H * TILE),
        ],
        out_specs=pl.BlockSpec((step, CUBE, width), lambda b: (b, 0, 0)),
        out_shape=jax.ShapeDtypeStruct((GROUP, CUBE, width), BF16),
        compiler_params=pltpu.CompilerParams(vmem_limit_bytes=VMEM),
    )(half, own, first, second, rim, left, right)


def offset_table():
    table = np.full((GROUP, 3, SEEN, TILES_H, TILES_W), -1, np.int32)
    for block in range(GROUP):
        for k, (kh, kw) in enumerate(seen_tiles(block)):
            for qh in range(TILES_H):
                for qw in range(TILES_W):
                    dh, dw = kh - (block * TILES_H + qh), kw - qw
                    if abs(dh) <= 1 and abs(dw) <= 1:
                        for i, dt in enumerate((0, -1, 1)):
                            table[block, i, k, qh, qw] = 9 * dt + 3 * dh + dw + 13
    return table


def allowed_tiles(pattern, half):
    hot = offset_table().reshape(GROUP, 3, SEEN, -1)[..., None] == np.arange(27)
    picked = jnp.sum(jnp.where(hot, pattern[:, None, None], 0.0), -1)
    places = np.array([seen_tiles(block) for block in range(GROUP)])
    t = lax.axis_index("ta") + jnp.array([0, -1, 1])
    t_ok = (t >= 0) & (t < lax.axis_size("ta"))
    w = lax.axis_index("wa") * TILES_W + places[..., 1]
    w_ok = (w >= 0) & (w < TILES_W * lax.axis_size("wa"))
    h = half * GROUP_H + places[..., 0]
    h_ok = (h >= 0) & (h < TILES_H * lax.axis_size("ha"))
    inside = t_ok[None, :, None] & (w_ok & h_ok)[:, None, :]
    picked = jnp.where(inside[..., None], picked, 0.0)
    return jnp.repeat(picked.reshape(GROUP, 3 * SEEN, -1), TILE, axis=2)


def turned_width(value, step):
    count = lax.axis_size("wa")
    return lax.ppermute(value, "wa", [(i, (i + step) % count) for i in range(count)])


def turned_time(value, step):
    count_t, count_h = lax.axis_size("ta"), lax.axis_size("ha")
    pairs = []
    for t in range(count_t):
        for h in range(count_h):
            t_to = t + step
            h_to = h
            if not 0 <= t_to < count_t:
                h_to = (h + count_h // 2) % count_h
            pairs.append((t * count_h + h, t_to % count_t * count_h + h_to))
    return lax.ppermute(value, ("ta", "ha"), pairs)


def swapped(value, axis, bit):
    count = lax.axis_size(axis)
    return lax.ppermute(value, axis, [(i, i ^ bit) for i in range(count)])


def regrouped(value):
    count = lax.axis_size("ha")
    groups = [list(range(i, i + GROUP)) for i in range(0, count, GROUP)]
    return lax.all_to_all(value, "ha", 0, 0, axis_index_groups=groups)


def log2(count):
    return count.bit_length() - 1


def text_steps():
    ta, ha, wa = (lax.axis_size(axis) for axis in ("ta", "ha", "wa"))
    halves = [("ha", ha >> i) for i in range(1, log2(ha) + 1)]
    steps = halves[:-2] + [("ta", ta >> i) for i in range(1, log2(ta))] + halves[-2:]
    steps += [("wa", wa >> i) for i in range(1, log2(wa) + 1)]
    return steps + [("ta", 1)]


def text_bits():
    start = {"wa": 0, "ha": log2(lax.axis_size("wa"))}
    start["ta"] = start["ha"] + log2(lax.axis_size("ha"))
    return tuple(start[axis] + log2(bit) for axis, bit in text_steps())


def is_high(axis, bit):
    return (lax.axis_index(axis) & bit) > 0


def gather_text(value, axis, bit):
    high = is_high(axis, bit)
    mine = theirs = value
    if axis == "ha" and bit < GROUP:
        middle = value.shape[0] // 2
        mine = jnp.where(high, value[middle:], value[:middle])
        theirs = jnp.where(high, value[:middle], value[middle:])
    return jnp.concatenate([mine, swapped(theirs, axis, bit)], 1)


def scatter_text(mine, theirs, axis, bit):
    high = is_high(axis, bit)
    other = swapped(theirs, axis, bit)
    if axis == "ha" and bit < GROUP:
        first = jnp.where(high, other, mine)
        second = jnp.where(high, mine, other)
        return jnp.concatenate([first, second], 0)
    return mine + other


def scatter_halves(value, axis, bit):
    middle = value.shape[1] // 2
    return scatter_text(value[:, :middle], value[:, middle:], axis, bit)


def after(value, *others):
    return lax.optimization_barrier((value, *others))[0]


def local(query, key, value, d_out, text_key, text_value, block_pattern, text_length):
    full = query.shape[-1]
    half = lax.axis_index("ha") // GROUP
    steps = text_steps()
    line = TILES_W * TILE

    kv_out = pack(
        key.reshape(CUBE, full), value.reshape(CUBE, full), block_pattern.reshape(-1, 27)
    )
    text = jnp.stack([text_key.reshape(-1, HEAD), text_value.reshape(-1, HEAD)], 1)
    text = after(text.reshape(GROUP, 1, -1), kv_out)
    for step in steps[:2]:
        text = gather_text(text, *step)
    qg_out = pack(query.reshape(CUBE, full), d_out.reshape(CUBE, full))
    kv_in = regrouped(kv_out)
    width = kv_in.shape[-1]

    own = kv_in[:, :CUBE].reshape(GROUP_H, TILES_W, TILE, width)
    flat = own.reshape(OWN, width)
    edge = jnp.where(half == 0, own[GROUP_H - 1], own[0])
    rim = swapped(edge.reshape(line, width), "ha", GROUP)
    text = gather_text(after(text, kv_in), *steps[2])
    to_right = jnp.concatenate([own[:, TILES_W - 1].reshape(SIDE, width), rim[line - TILE :]], 0)
    to_left = jnp.concatenate([own[:, 0].reshape(SIDE, width), rim[:TILE]], 0)
    left = turned_width(to_right, 1)
    right = turned_width(to_left, -1)
    text = after(text, rim)
    for step in steps[3:5]:
        text = gather_text(text, *step)
    here = after(jnp.concatenate([flat, left, right, rim], 0), text)
    below = turned_time(here, 1)
    above = turned_time(here, -1)
    qg = regrouped(after(qg_out, here))
    text = after(text, here)
    for step in steps[5:-1]:
        text = gather_text(text, *step)
    text = gather_text(after(text, qg), *steps[-1])
    allow = allowed_tiles(kv_in[:, CUBE : CUBE + 8, :27].astype(F32), half)

    me = (lax.axis_index("ta") * lax.axis_size("ha") + lax.axis_index("ha")) * lax.axis_size("wa")
    me = me + lax.axis_index("wa")
    od, here_grad, below_grad, above_grad, text_grad, text_away = attention(
        jnp.concatenate([text_length, me.reshape(1)]),
        allow,
        qg,
        here,
        below,
        above,
        text[0],
        text_bits(),
    )

    first = turned_time(below_grad, -1)
    second = turned_time(above_grad, 1)
    back = steps[::-1]
    text_grad = scatter_text(text_grad[None], text_away[None], *back[0])
    for step in back[1:3]:
        text_grad = scatter_halves(text_grad, *step)
    od_in = regrouped(od)
    halo = here_grad[OWN:] + first[OWN:].astype(F32) + second[OWN:].astype(F32)
    side = SIDE + TILE
    to_left = halo[:side].astype(BF16)
    to_right = halo[side : 2 * side].astype(BF16)
    rim_grad = halo[2 * side :]
    right = turned_width(to_left, -1)
    left = turned_width(to_right, 1)
    text_grad = scatter_halves(after(text_grad, to_left, to_right), *back[3])
    rim_out = jnp.concatenate(
        [
            rim_grad[:TILE] + left[SIDE:].astype(F32),
            rim_grad[TILE : line - TILE],
            rim_grad[line - TILE :] + right[SIDE:].astype(F32),
        ],
        0,
    ).astype(BF16)
    rim_in = swapped(rim_out, "ha", GROUP)
    text_grad = after(text_grad, rim_out)
    for step in back[4:6]:
        text_grad = scatter_halves(text_grad, *step)
    grads = settle(after(half.reshape(1), od_in), here_grad, first, second, rim_in, left, right)
    text_grad = after(text_grad, grads)
    for step in back[6:]:
        text_grad = scatter_halves(text_grad, *step)
    attended, query_grad = unpack(od_in)
    key_grad, value_grad = unpack(regrouped(grads))
    text_grad = text_grad.astype(BF16).reshape(-1, 2, HEAD)
    return (
        attended.reshape(query.shape),
        query_grad.reshape(query.shape),
        key_grad.reshape(query.shape),
        value_grad.reshape(query.shape),
        text_grad[:, 0].reshape(1, full),
        text_grad[:, 1].reshape(1, full),
    )


def solution(mesh):
    cube = P("ta", "ha", "wa", None)
    text = P(("ta", "ha", "wa"), None)
    return jax.shard_map(
        local,
        mesh=mesh,
        in_specs=(cube, cube, cube, cube, text, text, cube, P()),
        out_specs=(cube, cube, cube, cube, text, text),
        check_vma=False,
    )
```

```python
import functools

import jax
import jax.numpy as jnp
import numpy as np
from jax import lax
from jax.experimental import pallas as pl
from jax.experimental.pallas import tpu as pltpu
from jax.sharding import PartitionSpec as P

HEAD = 128
PAIR = 2 * HEAD
TILE_T = 2
TILE_H = 2
TILE_W = 4
TILE = TILE_T * TILE_H * TILE_W
NEGATIVE = -1e30
LOG2E = 1.4426950408889634
EXTRA = 16
PACKS = 2
VMEM = 58 * 1024 * 1024
F32 = jnp.float32
BF16 = jnp.bfloat16

ROWS = 4
COLS = 16
TILES_H = ROWS // TILE_H
TILES_W = COLS // TILE_W
CUBE = TILE_T * ROWS * COLS
GROUP = 4
GROUP_H = GROUP * TILES_H
OWN = GROUP_H * TILES_W * TILE
SIDE = GROUP_H * TILE
RIM = (TILES_W + 2) * TILE
ALL = OWN + 2 * SIDE + RIM
SEEN = (TILES_H + 2) * (TILES_W + 2)


def natural_index(row):
    tile_h = row >> 6
    tile_w = (row >> 4) & 3
    t = (row >> 3) & 1
    h = (row >> 2) & 1
    w = row & 3
    return t * (ROWS * COLS) + (tile_h * TILE_H + h) * COLS + tile_w * TILE_W + w


def pack_kernel(first_ref, second_ref, *rest):
    out_ref = rest[-1]
    row = lax.broadcasted_iota(jnp.int32, (CUBE, CUBE), 0)
    col = lax.broadcasted_iota(jnp.int32, (CUBE, CUBE), 1)
    order = jnp.where(natural_index(row) == col, 1.0, 0.0).astype(BF16)
    first = jnp.dot(order, first_ref[...], preferred_element_type=F32).astype(BF16)
    second = jnp.dot(order, second_ref[...], preferred_element_type=F32).astype(BF16)
    groups, _, width = out_ref.shape
    heads = width // PAIR
    for group in range(groups):
        for i in range(heads):
            source = slice((group * heads + i) * HEAD, (group * heads + i + 1) * HEAD)
            out_ref[group, :CUBE, i * PAIR : i * PAIR + HEAD] = first[:, source]
            out_ref[group, :CUBE, i * PAIR + HEAD : (i + 1) * PAIR] = second[:, source]
        if len(rest) > 1:
            pattern = rest[0][...].astype(F32)
            lines = jnp.concatenate([pattern, jnp.zeros_like(pattern)], 0).astype(BF16)
            out_ref[group, CUBE:, :] = jnp.zeros((EXTRA, width), BF16)
            out_ref[group, CUBE:, : pattern.shape[1]] = lines


def pack(first, second, pattern=None):
    width = first.shape[1] // GROUP
    step = GROUP // PACKS
    rows = CUBE + (0 if pattern is None else EXTRA)
    specs = [pl.BlockSpec((CUBE, width * step), lambda g: (0, g))] * 2
    extras = ()
    if pattern is not None:
        specs.append(pl.BlockSpec(pattern.shape, lambda g: (0, 0)))
        extras = (pattern,)
    return pl.pallas_call(
        pack_kernel,
        grid=(PACKS,),
        in_specs=specs,
        out_specs=pl.BlockSpec((step, rows, 2 * width), lambda g: (g, 0, 0)),
        out_shape=jax.ShapeDtypeStruct((GROUP, rows, 2 * width), BF16),
        compiler_params=pltpu.CompilerParams(vmem_limit_bytes=VMEM),
    )(first, second, *extras)


def unpack_kernel(packed_ref, first_ref, second_ref):
    row = lax.broadcasted_iota(jnp.int32, (CUBE, CUBE), 0)
    col = lax.broadcasted_iota(jnp.int32, (CUBE, CUBE), 1)
    order = jnp.where(natural_index(col) == row, 1.0, 0.0).astype(BF16)
    groups, _, width = packed_ref.shape
    heads = width // PAIR
    for group in range(groups):
        both = jnp.dot(order, packed_ref[group], preferred_element_type=F32).astype(BF16)
        for i in range(heads):
            target = slice((group * heads + i) * HEAD, (group * heads + i + 1) * HEAD)
            first_ref[:, target] = both[:, i * PAIR : i * PAIR + HEAD]
            second_ref[:, target] = both[:, i * PAIR + HEAD : (i + 1) * PAIR]


def unpack(packed):
    _, rows, width = packed.shape
    step = GROUP // PACKS
    half = width // 2
    return pl.pallas_call(
        unpack_kernel,
        grid=(PACKS,),
        in_specs=[pl.BlockSpec((step, rows, width), lambda g: (g, 0, 0))],
        out_specs=[pl.BlockSpec((CUBE, half * step), lambda g: (0, g))] * 2,
        out_shape=[jax.ShapeDtypeStruct((CUBE, GROUP * half), BF16)] * 2,
        compiler_params=pltpu.CompilerParams(vmem_limit_bytes=VMEM),
    )(packed)


def block_rows(block):
    low, high = block * TILES_H - 1, (block + 1) * TILES_H + 1
    outer = -1 if low < 0 else GROUP_H if high > GROUP_H else None
    return max(low, 0), min(high, GROUP_H), outer


def seen_tiles(block):
    low, high, outer = block_rows(block)
    tiles = [(h, w) for h in range(low, high) for w in range(TILES_W)]
    tiles += [(h, -1) for h in range(low, high)] + [(h, TILES_W) for h in range(low, high)]
    if outer is not None:
        tiles += [(outer, w) for w in (*range(TILES_W), -1, TILES_W)]
    return tiles


def attention_kernel(
    text_bits,
    length_ref,
    allow_ref,
    qg_ref,
    here_ref,
    below_ref,
    above_ref,
    text_ref,
    od_ref,
    here_out,
    below_out,
    above_out,
    text_out,
    text_away_out,
    below_sum,
    above_sum,
):
    text_count = text_ref.shape[0]
    scale = HEAD**-0.5
    near = (here_ref, below_ref, above_ref)
    sums = (here_out, below_sum, above_sum)
    text_row = lax.broadcasted_iota(jnp.int32, (text_count, CUBE), 0)
    text_place = jnp.zeros_like(text_row)
    for bit, place in enumerate(text_bits):
        text_place += ((text_row >> bit) & 1) << place
    text_ok = (text_place ^ length_ref[1]) < length_ref[0]
    blank = jnp.zeros((CUBE, HEAD), BF16)
    text_kv = text_ref[...]
    line = TILES_W * TILE
    def look(block):
        low, high, outer = block_rows(block)
        count = high - low
        q = qg_ref[block, :, :HEAD]
        g = qg_ref[block, :, HEAD:]
        both = jnp.concatenate(
            [jnp.concatenate([q, blank], 1), jnp.concatenate([blank, g], 1)], 0
        )
        done = 0 if block == 0 else 2
        places = [(low * line, count * line, done * line)]
        for side in range(2):
            places.append((OWN + side * (SIDE + TILE) + low * TILE, count * TILE, done * TILE))
        if outer is not None:
            rim = (OWN + 2 * (SIDE + TILE), OWN + SIDE, OWN + 2 * SIDE + TILE)
            for first, size in zip(rim, (line, TILE, TILE)):
                places.append((first, size, 0 if block == 0 else size))
        keys = []
        masks = []
        for i in range(3):
            parts = [near[i][first : first + size, :] for first, size, _ in places]
            keys.append(jnp.concatenate(parts, 0))
            tiles = allow_ref[block, i * SEEN : (i + 1) * SEEN, :]
            spread = jnp.broadcast_to(tiles[:, None, :], (SEEN, TILE, CUBE))
            masks.append(spread.reshape(SEEN * TILE, CUBE) > 0.5)
        keys.append(text_kv)
        masks.append(text_ok)
        scores = []
        dprobs = []
        for kv, ok in zip(keys, masks):
            mixed = lax.dot_general(
                kv, both, (((1,), (1,)), ((), ())), preferred_element_type=F32
            )
            scores.append(jnp.where(ok, mixed[:, :HEAD] * (scale * LOG2E), NEGATIVE))
            dprobs.append(mixed[:, HEAD:])
        top = functools.reduce(jnp.maximum, [jnp.max(s, 0, keepdims=True) for s in scores])
        return g, both, places, keys, scores, dprobs, top

    def finish(block, found):
        g, both, places, keys, scores, dprobs, top = found
        exps = [jnp.exp2(s - top) for s in scores]
        total = functools.reduce(jnp.add, [jnp.sum(e, 0, keepdims=True) for e in exps])
        inverse = 1.0 / total
        weights = [(e * inverse).astype(BF16) for e in exps]
        attended = jnp.zeros((CUBE, HEAD), F32)
        for w, kv in zip(weights, keys):
            attended += lax.dot_general(
                w, kv[:, HEAD:], (((0,), (0,)), ((), ())), preferred_element_type=F32
            )
        attended = attended.astype(BF16)
        od_ref[block, :, :HEAD] = attended
        product = g.astype(F32) * attended.astype(F32)
        delta = jnp.sum(product.T, 0, keepdims=True)
        dscores = [(e * ((d - delta) * inverse)).astype(BF16) for e, d in zip(exps, dprobs)]
        return both, places, keys, weights, dscores

    def settle_block(block, state):
        both, places, keys, weights, dscores = state
        query_grad = jnp.zeros((CUBE, HEAD), F32)
        for d, kv in zip(dscores, keys):
            query_grad += lax.dot_general(
                d, kv[:, :HEAD], (((0,), (0,)), ((), ())), preferred_element_type=F32
            )
        od_ref[block, :, HEAD:] = (query_grad * scale).astype(BF16)
        for i in range(4):
            change = jnp.dot(
                jnp.concatenate([dscores[i], weights[i]], 1), both, preferred_element_type=F32
            )
            if i == 3:
                middle = text_count // 2
                for target, piece in (
                    (text_out, change[:middle]),
                    (text_away_out, change[middle:]),
                ):
                    if block == 0:
                        target[...] = piece
                    else:
                        target[...] += piece
                continue
            taken = 0
            target = sums[i]
            for first, size, old in places:
                if old:
                    target[first : first + old, :] += change[taken : taken + old]
                if old < size:
                    target[first + old : first + size, :] = change[taken + old : taken + size]
                taken += size
    found = look(0)
    before = None
    for block in range(GROUP):
        following = look(block + 1) if block + 1 < GROUP else None
        now = finish(block, found)
        if before is not None:
            settle_block(block - 1, before)
        before = now
        found = following
    settle_block(GROUP - 1, before)
    lane = lax.broadcasted_iota(jnp.int32, (1, PAIR), 1)
    factor = jnp.where(lane < HEAD, scale, 1.0).astype(F32)
    here_out[...] = here_out[...] * factor
    below_out[...] = (below_sum[...] * factor).astype(BF16)
    above_out[...] = (above_sum[...] * factor).astype(BF16)
    text_out[...] = text_out[...] * factor
    text_away_out[...] = text_away_out[...] * factor


def attention(length, allow, qg, here, below, above, text, text_bits):
    width = qg.shape[-1]
    heads = width // PAIR
    text_count = text.shape[0]

    def spec(rows):
        return pl.BlockSpec((rows, PAIR), lambda h: (0, h))

    def shape(rows, dtype):
        return jax.ShapeDtypeStruct((rows, width), dtype)

    part = pl.BlockSpec((GROUP, CUBE, PAIR), lambda h: (0, 0, h))
    return pl.pallas_call(
        functools.partial(attention_kernel, text_bits),
        grid=(heads,),
        in_specs=[
            pl.BlockSpec(memory_space=pltpu.SMEM),
            pl.BlockSpec(allow.shape, lambda h: (0, 0, 0)),
            part,
        ]
        + [spec(ALL)] * 3
        + [spec(text_count)],
        out_specs=[part] + [spec(ALL)] * 3 + [spec(text_count // 2)] * 2,
        out_shape=[
            jax.ShapeDtypeStruct(qg.shape, BF16),
            shape(ALL, F32),
            shape(ALL, BF16),
            shape(ALL, BF16),
            shape(text_count // 2, F32),
            shape(text_count // 2, F32),
        ],
        scratch_shapes=[pltpu.VMEM((rows, PAIR), F32) for rows in (ALL, ALL)],
        compiler_params=pltpu.CompilerParams(vmem_limit_bytes=VMEM),
    )(length, allow, qg, here, below, above, text)


def settle_kernel(half_ref, own_ref, first_ref, second_ref, rim_ref, left_ref, right_ref, out_ref):
    line = TILES_W * TILE
    rim = rim_ref[...].astype(F32)
    half = half_ref[0]
    groups = out_ref.shape[0]
    for group in range(groups):
        block = pl.program_id(0) * groups + group
        cube = slice(group * CUBE, (group + 1) * CUBE)
        total = own_ref[cube] + first_ref[cube].astype(F32) + second_ref[cube].astype(F32)
        for i in range(TILES_H):
            edge = (block == 0) & (half == 1) if i == 0 else (block == GROUP - 1) & (half == 0)
            part = total[i * line : (i + 1) * line]
            part += jnp.where(edge, rim, 0.0)
            here = slice((group * TILES_H + i) * TILE, (group * TILES_H + i + 1) * TILE)
            pieces = [
                part[:TILE] + left_ref[here].astype(F32),
                part[TILE : line - TILE],
                part[line - TILE :] + right_ref[here].astype(F32),
            ]
            out_ref[group, i * line : (i + 1) * line, :] = jnp.concatenate(pieces, 0).astype(BF16)


def settle(half, own, first, second, rim, left, right):
    width = own.shape[-1]
    step = GROUP // PACKS

    def spec(rows):
        return pl.BlockSpec((rows * step, width), lambda b: (b, 0))

    return pl.pallas_call(
        settle_kernel,
        grid=(PACKS,),
        in_specs=[
            pl.BlockSpec(memory_space=pltpu.SMEM),
            spec(CUBE),
            spec(CUBE),
            spec(CUBE),
            pl.BlockSpec((TILES_W * TILE, width), lambda b: (0, 0)),
            spec(TILES_H * TILE),
            spec(TILES_H * TILE),
        ],
        out_specs=pl.BlockSpec((step, CUBE, width), lambda b: (b, 0, 0)),
        out_shape=jax.ShapeDtypeStruct((GROUP, CUBE, width), BF16),
        compiler_params=pltpu.CompilerParams(vmem_limit_bytes=VMEM),
    )(half, own, first, second, rim, left, right)


def offset_table():
    table = np.full((GROUP, 3, SEEN, TILES_H, TILES_W), -1, np.int32)
    for block in range(GROUP):
        for k, (kh, kw) in enumerate(seen_tiles(block)):
            for qh in range(TILES_H):
                for qw in range(TILES_W):
                    dh, dw = kh - (block * TILES_H + qh), kw - qw
                    if abs(dh) <= 1 and abs(dw) <= 1:
                        for i, dt in enumerate((0, -1, 1)):
                            table[block, i, k, qh, qw] = 9 * dt + 3 * dh + dw + 13
    return table


def allowed_tiles(pattern, half):
    hot = offset_table().reshape(GROUP, 3, SEEN, -1)[..., None] == np.arange(27)
    picked = jnp.sum(jnp.where(hot, pattern[:, None, None], 0.0), -1)
    places = np.array([seen_tiles(block) for block in range(GROUP)])
    t = lax.axis_index("ta") + jnp.array([0, -1, 1])
    t_ok = (t >= 0) & (t < lax.axis_size("ta"))
    w = lax.axis_index("wa") * TILES_W + places[..., 1]
    w_ok = (w >= 0) & (w < TILES_W * lax.axis_size("wa"))
    h = half * GROUP_H + places[..., 0]
    h_ok = (h >= 0) & (h < TILES_H * lax.axis_size("ha"))
    inside = t_ok[None, :, None] & (w_ok & h_ok)[:, None, :]
    picked = jnp.where(inside[..., None], picked, 0.0)
    return jnp.repeat(picked.reshape(GROUP, 3 * SEEN, -1), TILE, axis=2)


def turned_width(value, step):
    count = lax.axis_size("wa")
    return lax.ppermute(value, "wa", [(i, (i + step) % count) for i in range(count)])


def turned_time(value, step):
    count_t, count_h = lax.axis_size("ta"), lax.axis_size("ha")
    pairs = []
    for t in range(count_t):
        for h in range(count_h):
            t_to = t + step
            h_to = h
            if not 0 <= t_to < count_t:
                h_to = (h + count_h // 2) % count_h
            pairs.append((t * count_h + h, t_to % count_t * count_h + h_to))
    return lax.ppermute(value, ("ta", "ha"), pairs)


def swapped(value, axis, bit):
    count = lax.axis_size(axis)
    return lax.ppermute(value, axis, [(i, i ^ bit) for i in range(count)])


def regrouped(value):
    count = lax.axis_size("ha")
    groups = [list(range(i, i + GROUP)) for i in range(0, count, GROUP)]
    return lax.all_to_all(value, "ha", 0, 0, axis_index_groups=groups)


def log2(count):
    return count.bit_length() - 1


def text_steps():
    ta, ha, wa = (lax.axis_size(axis) for axis in ("ta", "ha", "wa"))
    halves = [("ha", ha >> i) for i in range(1, log2(ha) + 1)]
    steps = halves[:-2] + [("ta", ta >> i) for i in range(1, log2(ta))] + halves[-2:]
    steps += [("wa", wa >> i) for i in range(1, log2(wa) + 1)]
    return steps + [("ta", 1)]


def text_bits():
    start = {"wa": 0, "ha": log2(lax.axis_size("wa"))}
    start["ta"] = start["ha"] + log2(lax.axis_size("ha"))
    return tuple(start[axis] + log2(bit) for axis, bit in text_steps())


def is_high(axis, bit):
    return (lax.axis_index(axis) & bit) > 0


def gather_text(value, axis, bit):
    high = is_high(axis, bit)
    mine = theirs = value
    if axis == "ha" and bit < GROUP:
        middle = value.shape[0] // 2
        mine = jnp.where(high, value[middle:], value[:middle])
        theirs = jnp.where(high, value[:middle], value[middle:])
    return jnp.concatenate([mine, swapped(theirs, axis, bit)], 1)


def scatter_text(mine, theirs, axis, bit):
    high = is_high(axis, bit)
    other = swapped(theirs, axis, bit)
    if axis == "ha" and bit < GROUP:
        first = jnp.where(high, other, mine)
        second = jnp.where(high, mine, other)
        return jnp.concatenate([first, second], 0)
    return mine + other


def scatter_halves(value, axis, bit):
    middle = value.shape[1] // 2
    return scatter_text(value[:, :middle], value[:, middle:], axis, bit)


def after(value, *others):
    return lax.optimization_barrier((value, *others))[0]


def local(query, key, value, d_out, text_key, text_value, block_pattern, text_length):
    full = query.shape[-1]
    half = lax.axis_index("ha") // GROUP
    steps = text_steps()
    line = TILES_W * TILE

    kv_out = pack(
        key.reshape(CUBE, full), value.reshape(CUBE, full), block_pattern.reshape(-1, 27)
    )
    text = jnp.stack([text_key.reshape(-1, HEAD), text_value.reshape(-1, HEAD)], 1)
    text = after(text.reshape(GROUP, 1, -1), kv_out)
    for step in steps[:2]:
        text = gather_text(text, *step)
    qg_out = pack(query.reshape(CUBE, full), d_out.reshape(CUBE, full))
    kv_in = regrouped(kv_out)
    width = kv_in.shape[-1]

    own = kv_in[:, :CUBE].reshape(GROUP_H, TILES_W, TILE, width)
    flat = own.reshape(OWN, width)
    edge = jnp.where(half == 0, own[GROUP_H - 1], own[0])
    rim = swapped(edge.reshape(line, width), "ha", GROUP)
    text = gather_text(after(text, kv_in, qg_out), *steps[2])
    to_right = jnp.concatenate([own[:, TILES_W - 1].reshape(SIDE, width), rim[line - TILE :]], 0)
    to_left = jnp.concatenate([own[:, 0].reshape(SIDE, width), rim[:TILE]], 0)
    left = turned_width(to_right, 1)
    right = turned_width(to_left, -1)
    text = after(text, rim)
    for step in steps[3:5]:
        text = gather_text(text, *step)
    here = after(jnp.concatenate([flat, left, right, rim], 0), text)
    below = turned_time(here, 1)
    above = turned_time(here, -1)
    qg = regrouped(after(qg_out, rim))
    text = after(text, here)
    text = gather_text(text, *steps[5])
    text = after(text, qg)
    for step in steps[6:]:
        text = gather_text(text, *step)
    allow = allowed_tiles(kv_in[:, CUBE : CUBE + 8, :27].astype(F32), half)

    me = (lax.axis_index("ta") * lax.axis_size("ha") + lax.axis_index("ha")) * lax.axis_size("wa")
    me = me + lax.axis_index("wa")
    od, here_grad, below_grad, above_grad, text_grad, text_away = attention(
        jnp.concatenate([text_length, me.reshape(1)]),
        allow,
        qg,
        here,
        below,
        above,
        text[0],
        text_bits(),
    )

    first = turned_time(below_grad, -1)
    second = turned_time(above_grad, 1)
    back = steps[::-1]
    text_grad = scatter_text(text_grad[None], text_away[None], *back[0])
    text_grad = scatter_halves(text_grad, *back[1])
    od_in = regrouped(od)
    text_grad = scatter_halves(after(text_grad, od_in), *back[2])
    halo = here_grad[OWN:] + first[OWN:].astype(F32) + second[OWN:].astype(F32)
    side = SIDE + TILE
    to_left = halo[:side].astype(BF16)
    to_right = halo[side : 2 * side].astype(BF16)
    rim_grad = halo[2 * side :]
    right = turned_width(to_left, -1)
    left = turned_width(to_right, 1)
    text_grad = scatter_halves(after(text_grad, to_left, to_right), *back[3])
    rim_out = jnp.concatenate(
        [
            rim_grad[:TILE] + left[SIDE:].astype(F32),
            rim_grad[TILE : line - TILE],
            rim_grad[line - TILE :] + right[SIDE:].astype(F32),
        ],
        0,
    ).astype(BF16)
    rim_in = swapped(rim_out, "ha", GROUP)
    text_grad = scatter_halves(after(text_grad, rim_out), *back[4])
    text_grad = scatter_halves(after(text_grad, rim_in), *back[5])
    grads = settle(half.reshape(1), here_grad, first, second, rim_in, left, right)
    text_grad = after(text_grad, grads)
    for step in back[6:]:
        text_grad = scatter_halves(text_grad, *step)
    attended, query_grad = unpack(od_in)
    key_grad, value_grad = unpack(regrouped(grads))
    text_grad = text_grad.astype(BF16).reshape(-1, 2, HEAD)
    return (
        attended.reshape(query.shape),
        query_grad.reshape(query.shape),
        key_grad.reshape(query.shape),
        value_grad.reshape(query.shape),
        text_grad[:, 0].reshape(1, full),
        text_grad[:, 1].reshape(1, full),
    )


def solution(mesh):
    cube = P("ta", "ha", "wa", None)
    text = P(("ta", "ha", "wa"), None)
    return jax.shard_map(
        local,
        mesh=mesh,
        in_specs=(cube, cube, cube, cube, text, text, cube, P()),
        out_specs=(cube, cube, cube, cube, text, text),
        check_vma=False,
    )
```

```python
import functools

import jax
import jax.numpy as jnp
import numpy as np
from jax import lax
from jax.experimental import pallas as pl
from jax.experimental.pallas import tpu as pltpu
from jax.sharding import PartitionSpec as P

HEAD = 128
PAIR = 2 * HEAD
TILE_T = 2
TILE_H = 2
TILE_W = 4
TILE = TILE_T * TILE_H * TILE_W
NEGATIVE = -1e30
LOG2E = 1.4426950408889634
EXTRA = 16
PACKS = 2
VMEM = 58 * 1024 * 1024
F32 = jnp.float32
BF16 = jnp.bfloat16

ROWS = 4
COLS = 16
TILES_H = ROWS // TILE_H
TILES_W = COLS // TILE_W
CUBE = TILE_T * ROWS * COLS
GROUP = 4
GROUP_H = GROUP * TILES_H
OWN = GROUP_H * TILES_W * TILE
SIDE = GROUP_H * TILE
RIM = (TILES_W + 2) * TILE
ALL = OWN + 2 * SIDE + RIM
SEEN = (TILES_H + 2) * (TILES_W + 2)


def natural_index(row):
    tile_h = row >> 6
    tile_w = (row >> 4) & 3
    t = (row >> 3) & 1
    h = (row >> 2) & 1
    w = row & 3
    return t * (ROWS * COLS) + (tile_h * TILE_H + h) * COLS + tile_w * TILE_W + w


def pack_kernel(first_ref, second_ref, *rest):
    out_ref = rest[-1]
    row = lax.broadcasted_iota(jnp.int32, (CUBE, CUBE), 0)
    col = lax.broadcasted_iota(jnp.int32, (CUBE, CUBE), 1)
    order = jnp.where(natural_index(row) == col, 1.0, 0.0).astype(BF16)
    first = jnp.dot(order, first_ref[...], preferred_element_type=F32).astype(BF16)
    second = jnp.dot(order, second_ref[...], preferred_element_type=F32).astype(BF16)
    groups, _, width = out_ref.shape
    heads = width // PAIR
    for group in range(groups):
        for i in range(heads):
            source = slice((group * heads + i) * HEAD, (group * heads + i + 1) * HEAD)
            out_ref[group, :CUBE, i * PAIR : i * PAIR + HEAD] = first[:, source]
            out_ref[group, :CUBE, i * PAIR + HEAD : (i + 1) * PAIR] = second[:, source]
        if len(rest) > 1:
            pattern = rest[0][...].astype(F32)
            lines = jnp.concatenate([pattern, jnp.zeros_like(pattern)], 0).astype(BF16)
            out_ref[group, CUBE:, :] = jnp.zeros((EXTRA, width), BF16)
            out_ref[group, CUBE:, : pattern.shape[1]] = lines


def pack(first, second, pattern=None):
    width = first.shape[1] // GROUP
    step = GROUP // PACKS
    rows = CUBE + (0 if pattern is None else EXTRA)
    specs = [pl.BlockSpec((CUBE, width * step), lambda g: (0, g))] * 2
    extras = ()
    if pattern is not None:
        specs.append(pl.BlockSpec(pattern.shape, lambda g: (0, 0)))
        extras = (pattern,)
    return pl.pallas_call(
        pack_kernel,
        grid=(PACKS,),
        in_specs=specs,
        out_specs=pl.BlockSpec((step, rows, 2 * width), lambda g: (g, 0, 0)),
        out_shape=jax.ShapeDtypeStruct((GROUP, rows, 2 * width), BF16),
        compiler_params=pltpu.CompilerParams(vmem_limit_bytes=VMEM),
    )(first, second, *extras)


def unpack_kernel(packed_ref, first_ref, second_ref):
    row = lax.broadcasted_iota(jnp.int32, (CUBE, CUBE), 0)
    col = lax.broadcasted_iota(jnp.int32, (CUBE, CUBE), 1)
    order = jnp.where(natural_index(col) == row, 1.0, 0.0).astype(BF16)
    groups, _, width = packed_ref.shape
    heads = width // PAIR
    for group in range(groups):
        both = jnp.dot(order, packed_ref[group], preferred_element_type=F32).astype(BF16)
        for i in range(heads):
            target = slice((group * heads + i) * HEAD, (group * heads + i + 1) * HEAD)
            first_ref[:, target] = both[:, i * PAIR : i * PAIR + HEAD]
            second_ref[:, target] = both[:, i * PAIR + HEAD : (i + 1) * PAIR]


def unpack(packed):
    _, rows, width = packed.shape
    step = GROUP // PACKS
    half = width // 2
    return pl.pallas_call(
        unpack_kernel,
        grid=(PACKS,),
        in_specs=[pl.BlockSpec((step, rows, width), lambda g: (g, 0, 0))],
        out_specs=[pl.BlockSpec((CUBE, half * step), lambda g: (0, g))] * 2,
        out_shape=[jax.ShapeDtypeStruct((CUBE, GROUP * half), BF16)] * 2,
        compiler_params=pltpu.CompilerParams(vmem_limit_bytes=VMEM),
    )(packed)


def block_rows(block):
    low, high = block * TILES_H - 1, (block + 1) * TILES_H + 1
    outer = -1 if low < 0 else GROUP_H if high > GROUP_H else None
    return max(low, 0), min(high, GROUP_H), outer


def seen_tiles(block):
    low, high, outer = block_rows(block)
    tiles = [(h, w) for h in range(low, high) for w in range(TILES_W)]
    tiles += [(h, -1) for h in range(low, high)] + [(h, TILES_W) for h in range(low, high)]
    if outer is not None:
        tiles += [(outer, w) for w in (*range(TILES_W), -1, TILES_W)]
    return tiles


def attention_kernel(
    text_bits,
    length_ref,
    allow_ref,
    qg_ref,
    here_ref,
    below_ref,
    above_ref,
    text_ref,
    od_ref,
    here_out,
    below_out,
    above_out,
    text_out,
    text_away_out,
    below_sum,
    above_sum,
):
    text_count = text_ref.shape[0]
    scale = HEAD**-0.5
    near = (here_ref, below_ref, above_ref)
    sums = (here_out, below_sum, above_sum)
    text_row = lax.broadcasted_iota(jnp.int32, (text_count, CUBE), 0)
    text_place = jnp.zeros_like(text_row)
    for bit, place in enumerate(text_bits):
        text_place += ((text_row >> bit) & 1) << place
    text_ok = (text_place ^ length_ref[1]) < length_ref[0]
    blank = jnp.zeros((CUBE, HEAD), BF16)
    text_kv = text_ref[...]
    line = TILES_W * TILE
    def look(block):
        low, high, outer = block_rows(block)
        count = high - low
        q = qg_ref[block, :, :HEAD]
        g = qg_ref[block, :, HEAD:]
        both = jnp.concatenate(
            [jnp.concatenate([q, blank], 1), jnp.concatenate([blank, g], 1)], 0
        )
        done = 0 if block == 0 else 2
        places = [(low * line, count * line, done * line)]
        for side in range(2):
            places.append((OWN + side * (SIDE + TILE) + low * TILE, count * TILE, done * TILE))
        if outer is not None:
            rim = (OWN + 2 * (SIDE + TILE), OWN + SIDE, OWN + 2 * SIDE + TILE)
            for first, size in zip(rim, (line, TILE, TILE)):
                places.append((first, size, 0 if block == 0 else size))
        keys = []
        masks = []
        for i in range(3):
            parts = [near[i][first : first + size, :] for first, size, _ in places]
            keys.append(jnp.concatenate(parts, 0))
            tiles = allow_ref[block, i * SEEN : (i + 1) * SEEN, :]
            spread = jnp.broadcast_to(tiles[:, None, :], (SEEN, TILE, CUBE))
            masks.append(spread.reshape(SEEN * TILE, CUBE) > 0.5)
        keys.append(text_kv)
        masks.append(text_ok)
        scores = []
        dprobs = []
        for kv, ok in zip(keys, masks):
            mixed = lax.dot_general(
                kv, both, (((1,), (1,)), ((), ())), preferred_element_type=F32
            )
            scores.append(jnp.where(ok, mixed[:, :HEAD] * (scale * LOG2E), NEGATIVE))
            dprobs.append(mixed[:, HEAD:])
        top = functools.reduce(jnp.maximum, [jnp.max(s, 0, keepdims=True) for s in scores])
        return g, both, places, keys, scores, dprobs, top

    def finish(block, found):
        g, both, places, keys, scores, dprobs, top = found
        exps = [jnp.exp2(s - top) for s in scores]
        total = functools.reduce(jnp.add, [jnp.sum(e, 0, keepdims=True) for e in exps])
        inverse = 1.0 / total
        weights = [(e * inverse).astype(BF16) for e in exps]
        attended = jnp.zeros((CUBE, HEAD), F32)
        for w, kv in zip(weights, keys):
            attended += lax.dot_general(
                w, kv[:, HEAD:], (((0,), (0,)), ((), ())), preferred_element_type=F32
            )
        attended = attended.astype(BF16)
        od_ref[block, :, :HEAD] = attended
        product = g.astype(F32) * attended.astype(F32)
        delta = jnp.sum(product.T, 0, keepdims=True)
        dscores = [(e * ((d - delta) * inverse)).astype(BF16) for e, d in zip(exps, dprobs)]
        return both, places, keys, weights, dscores

    def settle_block(block, state):
        both, places, keys, weights, dscores = state
        query_grad = jnp.zeros((CUBE, HEAD), F32)
        for d, kv in zip(dscores, keys):
            query_grad += lax.dot_general(
                d, kv[:, :HEAD], (((0,), (0,)), ((), ())), preferred_element_type=F32
            )
        od_ref[block, :, HEAD:] = (query_grad * scale).astype(BF16)
        for i in range(4):
            change = jnp.dot(
                jnp.concatenate([dscores[i], weights[i]], 1), both, preferred_element_type=F32
            )
            if i == 3:
                middle = text_count // 2
                for target, piece in (
                    (text_out, change[:middle]),
                    (text_away_out, change[middle:]),
                ):
                    if block == 0:
                        target[...] = piece
                    else:
                        target[...] += piece
                continue
            taken = 0
            target = sums[i]
            for first, size, old in places:
                if old:
                    target[first : first + old, :] += change[taken : taken + old]
                if old < size:
                    target[first + old : first + size, :] = change[taken + old : taken + size]
                taken += size
    found = look(0)
    before = None
    for block in range(GROUP):
        following = look(block + 1) if block + 1 < GROUP else None
        now = finish(block, found)
        if before is not None:
            settle_block(block - 1, before)
        before = now
        found = following
    settle_block(GROUP - 1, before)
    lane = lax.broadcasted_iota(jnp.int32, (1, PAIR), 1)
    factor = jnp.where(lane < HEAD, scale, 1.0).astype(F32)
    here_out[...] = here_out[...] * factor
    below_out[...] = (below_sum[...] * factor).astype(BF16)
    above_out[...] = (above_sum[...] * factor).astype(BF16)
    text_out[...] = text_out[...] * factor
    text_away_out[...] = text_away_out[...] * factor


def attention(length, allow, qg, here, below, above, text, text_bits):
    width = qg.shape[-1]
    heads = width // PAIR
    text_count = text.shape[0]

    def spec(rows):
        return pl.BlockSpec((rows, PAIR), lambda h: (0, h))

    def shape(rows, dtype):
        return jax.ShapeDtypeStruct((rows, width), dtype)

    part = pl.BlockSpec((GROUP, CUBE, PAIR), lambda h: (0, 0, h))
    return pl.pallas_call(
        functools.partial(attention_kernel, text_bits),
        grid=(heads,),
        in_specs=[
            pl.BlockSpec(memory_space=pltpu.SMEM),
            pl.BlockSpec(allow.shape, lambda h: (0, 0, 0)),
            part,
        ]
        + [spec(ALL)] * 3
        + [spec(text_count)],
        out_specs=[part] + [spec(ALL)] * 3 + [spec(text_count // 2)] * 2,
        out_shape=[
            jax.ShapeDtypeStruct(qg.shape, BF16),
            shape(ALL, F32),
            shape(ALL, BF16),
            shape(ALL, BF16),
            shape(text_count // 2, F32),
            shape(text_count // 2, F32),
        ],
        scratch_shapes=[pltpu.VMEM((rows, PAIR), F32) for rows in (ALL, ALL)],
        compiler_params=pltpu.CompilerParams(vmem_limit_bytes=VMEM),
    )(length, allow, qg, here, below, above, text)


def settle_kernel(half_ref, own_ref, first_ref, second_ref, rim_ref, left_ref, right_ref, out_ref):
    line = TILES_W * TILE
    rim = rim_ref[...].astype(F32)
    half = half_ref[0]
    groups = out_ref.shape[0]
    for group in range(groups):
        block = pl.program_id(0) * groups + group
        cube = slice(group * CUBE, (group + 1) * CUBE)
        total = own_ref[cube] + first_ref[cube].astype(F32) + second_ref[cube].astype(F32)
        for i in range(TILES_H):
            edge = (block == 0) & (half == 1) if i == 0 else (block == GROUP - 1) & (half == 0)
            part = total[i * line : (i + 1) * line]
            part += jnp.where(edge, rim, 0.0)
            here = slice((group * TILES_H + i) * TILE, (group * TILES_H + i + 1) * TILE)
            pieces = [
                part[:TILE] + left_ref[here].astype(F32),
                part[TILE : line - TILE],
                part[line - TILE :] + right_ref[here].astype(F32),
            ]
            out_ref[group, i * line : (i + 1) * line, :] = jnp.concatenate(pieces, 0).astype(BF16)


def settle(half, own, first, second, rim, left, right):
    width = own.shape[-1]
    step = GROUP // PACKS

    def spec(rows):
        return pl.BlockSpec((rows * step, width), lambda b: (b, 0))

    return pl.pallas_call(
        settle_kernel,
        grid=(PACKS,),
        in_specs=[
            pl.BlockSpec(memory_space=pltpu.SMEM),
            spec(CUBE),
            spec(CUBE),
            spec(CUBE),
            pl.BlockSpec((TILES_W * TILE, width), lambda b: (0, 0)),
            spec(TILES_H * TILE),
            spec(TILES_H * TILE),
        ],
        out_specs=pl.BlockSpec((step, CUBE, width), lambda b: (b, 0, 0)),
        out_shape=jax.ShapeDtypeStruct((GROUP, CUBE, width), BF16),
        compiler_params=pltpu.CompilerParams(vmem_limit_bytes=VMEM),
    )(half, own, first, second, rim, left, right)


def offset_table():
    table = np.full((GROUP, 3, SEEN, TILES_H, TILES_W), -1, np.int32)
    for block in range(GROUP):
        for k, (kh, kw) in enumerate(seen_tiles(block)):
            for qh in range(TILES_H):
                for qw in range(TILES_W):
                    dh, dw = kh - (block * TILES_H + qh), kw - qw
                    if abs(dh) <= 1 and abs(dw) <= 1:
                        for i, dt in enumerate((0, -1, 1)):
                            table[block, i, k, qh, qw] = 9 * dt + 3 * dh + dw + 13
    return table


def allowed_tiles(pattern, half):
    hot = offset_table().reshape(GROUP, 3, SEEN, -1)[..., None] == np.arange(27)
    picked = jnp.sum(jnp.where(hot, pattern[:, None, None], 0.0), -1)
    places = np.array([seen_tiles(block) for block in range(GROUP)])
    t = lax.axis_index("ta") + jnp.array([0, -1, 1])
    t_ok = (t >= 0) & (t < lax.axis_size("ta"))
    w = lax.axis_index("wa") * TILES_W + places[..., 1]
    w_ok = (w >= 0) & (w < TILES_W * lax.axis_size("wa"))
    h = half * GROUP_H + places[..., 0]
    h_ok = (h >= 0) & (h < TILES_H * lax.axis_size("ha"))
    inside = t_ok[None, :, None] & (w_ok & h_ok)[:, None, :]
    picked = jnp.where(inside[..., None], picked, 0.0)
    return jnp.repeat(picked.reshape(GROUP, 3 * SEEN, -1), TILE, axis=2)


def turned_width(value, step):
    count = lax.axis_size("wa")
    return lax.ppermute(value, "wa", [(i, (i + step) % count) for i in range(count)])


def turned_time(value, step):
    count_t, count_h = lax.axis_size("ta"), lax.axis_size("ha")
    pairs = []
    for t in range(count_t):
        for h in range(count_h):
            t_to = t + step
            h_to = h
            if not 0 <= t_to < count_t:
                h_to = (h + count_h // 2) % count_h
            pairs.append((t * count_h + h, t_to % count_t * count_h + h_to))
    return lax.ppermute(value, ("ta", "ha"), pairs)


def swapped(value, axis, bit):
    count = lax.axis_size(axis)
    return lax.ppermute(value, axis, [(i, i ^ bit) for i in range(count)])


def regrouped(value):
    count = lax.axis_size("ha")
    groups = [list(range(i, i + GROUP)) for i in range(0, count, GROUP)]
    return lax.all_to_all(value, "ha", 0, 0, axis_index_groups=groups)


def log2(count):
    return count.bit_length() - 1


def text_steps():
    ta, ha, wa = (lax.axis_size(axis) for axis in ("ta", "ha", "wa"))
    halves = [("ha", ha >> i) for i in range(1, log2(ha) + 1)]
    steps = halves[:-2] + [("ta", ta >> i) for i in range(1, log2(ta))] + halves[-2:]
    steps += [("wa", wa >> i) for i in range(1, log2(wa) + 1)]
    return steps + [("ta", 1)]


def text_bits():
    start = {"wa": 0, "ha": log2(lax.axis_size("wa"))}
    start["ta"] = start["ha"] + log2(lax.axis_size("ha"))
    return tuple(start[axis] + log2(bit) for axis, bit in text_steps())


def is_high(axis, bit):
    return (lax.axis_index(axis) & bit) > 0


def gather_text(value, axis, bit):
    high = is_high(axis, bit)
    mine = theirs = value
    if axis == "ha" and bit < GROUP:
        middle = value.shape[0] // 2
        mine = jnp.where(high, value[middle:], value[:middle])
        theirs = jnp.where(high, value[:middle], value[middle:])
    return jnp.concatenate([mine, swapped(theirs, axis, bit)], 1)


def sent_text(mine, theirs, axis, bit):
    return mine, swapped(theirs, axis, bit), axis, bit


def joined_text(sent, *others):
    mine, other, axis, bit = sent
    if others:
        mine, other = lax.optimization_barrier((mine, other, *others))[:2]
    if axis == "ha" and bit < GROUP:
        high = is_high(axis, bit)
        first = jnp.where(high, other, mine)
        second = jnp.where(high, mine, other)
        return jnp.concatenate([first, second], 0)
    return mine + other


def scatter_text(sent, axis, bit, *others):
    value = joined_text(sent, *others)
    middle = value.shape[1] // 2
    return sent_text(value[:, :middle], value[:, middle:], axis, bit)


def after(value, *others):
    return lax.optimization_barrier((value, *others))[0]


def local(query, key, value, d_out, text_key, text_value, block_pattern, text_length):
    full = query.shape[-1]
    half = lax.axis_index("ha") // GROUP
    steps = text_steps()
    line = TILES_W * TILE

    kv_out = pack(
        key.reshape(CUBE, full), value.reshape(CUBE, full), block_pattern.reshape(-1, 27)
    )
    text = jnp.stack([text_key.reshape(-1, HEAD), text_value.reshape(-1, HEAD)], 1)
    text = after(text.reshape(GROUP, 1, -1), kv_out)
    for step in steps[:2]:
        text = gather_text(text, *step)
    qg_out = pack(query.reshape(CUBE, full), d_out.reshape(CUBE, full))
    kv_in = regrouped(kv_out)
    width = kv_in.shape[-1]

    own = kv_in[:, :CUBE].reshape(GROUP_H, TILES_W, TILE, width)
    flat = own.reshape(OWN, width)
    edge = jnp.where(half == 0, own[GROUP_H - 1], own[0])
    rim = swapped(edge.reshape(line, width), "ha", GROUP)
    text = gather_text(after(text, kv_in, qg_out), *steps[2])
    to_right = jnp.concatenate([own[:, TILES_W - 1].reshape(SIDE, width), rim[line - TILE :]], 0)
    to_left = jnp.concatenate([own[:, 0].reshape(SIDE, width), rim[:TILE]], 0)
    left = turned_width(to_right, 1)
    right = turned_width(to_left, -1)
    text = after(text, rim)
    for step in steps[3:5]:
        text = gather_text(text, *step)
    here = after(jnp.concatenate([flat, left, right, rim], 0), text)
    below = turned_time(here, 1)
    above = turned_time(here, -1)
    qg = regrouped(after(qg_out, rim))
    text = after(text, here)
    for step in steps[5:-1]:
        text = gather_text(text, *step)
    text = gather_text(after(text, qg), *steps[-1])
    allow = allowed_tiles(kv_in[:, CUBE : CUBE + 8, :27].astype(F32), half)

    me = (lax.axis_index("ta") * lax.axis_size("ha") + lax.axis_index("ha")) * lax.axis_size("wa")
    me = me + lax.axis_index("wa")
    od, here_grad, below_grad, above_grad, text_grad, text_away = attention(
        jnp.concatenate([text_length, me.reshape(1)]),
        allow,
        qg,
        here,
        below,
        above,
        text[0],
        text_bits(),
    )

    first = turned_time(below_grad, -1)
    second = turned_time(above_grad, 1)
    back = steps[::-1]
    text_grad = sent_text(text_grad[None], text_away[None], *back[0])
    text_grad = scatter_text(text_grad, *back[1])
    od_in = regrouped(od)
    text_grad = scatter_text(text_grad, *back[2], od_in)
    halo = here_grad[OWN:] + first[OWN:].astype(F32) + second[OWN:].astype(F32)
    side = SIDE + TILE
    to_left = halo[:side].astype(BF16)
    to_right = halo[side : 2 * side].astype(BF16)
    rim_grad = halo[2 * side :]
    right = turned_width(to_left, -1)
    left = turned_width(to_right, 1)
    text_grad = scatter_text(text_grad, *back[3], to_left, to_right)
    rim_out = jnp.concatenate(
        [
            rim_grad[:TILE] + left[SIDE:].astype(F32),
            rim_grad[TILE : line - TILE],
            rim_grad[line - TILE :] + right[SIDE:].astype(F32),
        ],
        0,
    ).astype(BF16)
    rim_in = swapped(rim_out, "ha", GROUP)
    text_grad = scatter_text(text_grad, *back[4], rim_out)
    text_grad = scatter_text(text_grad, *back[5], rim_in)
    grads = settle(half.reshape(1), here_grad, first, second, rim_in, left, right)
    text_grad = scatter_text(text_grad, *back[6], grads)
    text_grad = joined_text(scatter_text(text_grad, *back[7]))
    attended, query_grad = unpack(od_in)
    key_grad, value_grad = unpack(regrouped(grads))
    text_grad = text_grad.astype(BF16).reshape(-1, 2, HEAD)
    return (
        attended.reshape(query.shape),
        query_grad.reshape(query.shape),
        key_grad.reshape(query.shape),
        value_grad.reshape(query.shape),
        text_grad[:, 0].reshape(1, full),
        text_grad[:, 1].reshape(1, full),
    )


def solution(mesh):
    cube = P("ta", "ha", "wa", None)
    text = P(("ta", "ha", "wa"), None)
    return jax.shard_map(
        local,
        mesh=mesh,
        in_specs=(cube, cube, cube, cube, text, text, cube, P()),
        out_specs=(cube, cube, cube, cube, text, text),
        check_vma=False,
    )
```

```python
import functools

import jax
import jax.numpy as jnp
import numpy as np
from jax import lax
from jax.experimental import pallas as pl
from jax.experimental.pallas import tpu as pltpu
from jax.sharding import PartitionSpec as P

HEAD = 128
PAIR = 2 * HEAD
TILE_T = 2
TILE_H = 2
TILE_W = 4
TILE = TILE_T * TILE_H * TILE_W
NEGATIVE = -1e30
LOG2E = 1.4426950408889634
EXTRA = 16
PACKS = 2
VMEM = 58 * 1024 * 1024
F32 = jnp.float32
BF16 = jnp.bfloat16

ROWS = 4
COLS = 16
TILES_H = ROWS // TILE_H
TILES_W = COLS // TILE_W
CUBE = TILE_T * ROWS * COLS
GROUP = 4
GROUP_H = GROUP * TILES_H
OWN = GROUP_H * TILES_W * TILE
SIDE = GROUP_H * TILE
RIM = (TILES_W + 2) * TILE
ALL = OWN + 2 * SIDE + RIM
SEEN = (TILES_H + 2) * (TILES_W + 2)


def natural_index(row):
    tile_h = row >> 6
    tile_w = (row >> 4) & 3
    t = (row >> 3) & 1
    h = (row >> 2) & 1
    w = row & 3
    return t * (ROWS * COLS) + (tile_h * TILE_H + h) * COLS + tile_w * TILE_W + w


def pack_kernel(first_ref, second_ref, *rest):
    out_ref = rest[-1]
    row = lax.broadcasted_iota(jnp.int32, (CUBE, CUBE), 0)
    col = lax.broadcasted_iota(jnp.int32, (CUBE, CUBE), 1)
    order = jnp.where(natural_index(row) == col, 1.0, 0.0).astype(BF16)
    first = jnp.dot(order, first_ref[...], preferred_element_type=F32).astype(BF16)
    second = jnp.dot(order, second_ref[...], preferred_element_type=F32).astype(BF16)
    groups, _, width = out_ref.shape
    heads = width // PAIR
    for group in range(groups):
        for i in range(heads):
            source = slice((group * heads + i) * HEAD, (group * heads + i + 1) * HEAD)
            out_ref[group, :CUBE, i * PAIR : i * PAIR + HEAD] = first[:, source]
            out_ref[group, :CUBE, i * PAIR + HEAD : (i + 1) * PAIR] = second[:, source]
        if len(rest) > 1:
            pattern = rest[0][...].astype(F32)
            lines = jnp.concatenate([pattern, jnp.zeros_like(pattern)], 0).astype(BF16)
            out_ref[group, CUBE:, :] = jnp.zeros((EXTRA, width), BF16)
            out_ref[group, CUBE:, : pattern.shape[1]] = lines


def pack(first, second, pattern=None):
    width = first.shape[1] // GROUP
    step = GROUP // PACKS
    rows = CUBE + (0 if pattern is None else EXTRA)
    specs = [pl.BlockSpec((CUBE, width * step), lambda g: (0, g))] * 2
    extras = ()
    if pattern is not None:
        specs.append(pl.BlockSpec(pattern.shape, lambda g: (0, 0)))
        extras = (pattern,)
    return pl.pallas_call(
        pack_kernel,
        grid=(PACKS,),
        in_specs=specs,
        out_specs=pl.BlockSpec((step, rows, 2 * width), lambda g: (g, 0, 0)),
        out_shape=jax.ShapeDtypeStruct((GROUP, rows, 2 * width), BF16),
        compiler_params=pltpu.CompilerParams(vmem_limit_bytes=VMEM),
    )(first, second, *extras)


def unpack_kernel(packed_ref, first_ref, second_ref):
    row = lax.broadcasted_iota(jnp.int32, (CUBE, CUBE), 0)
    col = lax.broadcasted_iota(jnp.int32, (CUBE, CUBE), 1)
    order = jnp.where(natural_index(col) == row, 1.0, 0.0).astype(BF16)
    groups, _, width = packed_ref.shape
    heads = width // PAIR
    for group in range(groups):
        both = jnp.dot(order, packed_ref[group], preferred_element_type=F32).astype(BF16)
        for i in range(heads):
            target = slice((group * heads + i) * HEAD, (group * heads + i + 1) * HEAD)
            first_ref[:, target] = both[:, i * PAIR : i * PAIR + HEAD]
            second_ref[:, target] = both[:, i * PAIR + HEAD : (i + 1) * PAIR]


def unpack(packed):
    _, rows, width = packed.shape
    step = GROUP // PACKS
    half = width // 2
    return pl.pallas_call(
        unpack_kernel,
        grid=(PACKS,),
        in_specs=[pl.BlockSpec((step, rows, width), lambda g: (g, 0, 0))],
        out_specs=[pl.BlockSpec((CUBE, half * step), lambda g: (0, g))] * 2,
        out_shape=[jax.ShapeDtypeStruct((CUBE, GROUP * half), BF16)] * 2,
        compiler_params=pltpu.CompilerParams(vmem_limit_bytes=VMEM),
    )(packed)


def block_rows(block):
    low, high = block * TILES_H - 1, (block + 1) * TILES_H + 1
    outer = -1 if low < 0 else GROUP_H if high > GROUP_H else None
    return max(low, 0), min(high, GROUP_H), outer


def seen_tiles(block):
    low, high, outer = block_rows(block)
    tiles = [(h, w) for h in range(low, high) for w in range(TILES_W)]
    tiles += [(h, -1) for h in range(low, high)] + [(h, TILES_W) for h in range(low, high)]
    if outer is not None:
        tiles += [(outer, w) for w in (*range(TILES_W), -1, TILES_W)]
    return tiles


def attention_kernel(
    text_bits,
    length_ref,
    allow_ref,
    qg_ref,
    here_ref,
    below_ref,
    above_ref,
    text_ref,
    od_ref,
    here_out,
    own_below_out,
    own_above_out,
    halo_below_out,
    halo_above_out,
    text_out,
    text_away_out,
    below_sum,
    above_sum,
):
    text_count = text_ref.shape[0]
    scale = HEAD**-0.5
    near = (here_ref, below_ref, above_ref)
    sums = (here_out, below_sum, above_sum)
    text_row = lax.broadcasted_iota(jnp.int32, (text_count, CUBE), 0)
    text_place = jnp.zeros_like(text_row)
    for bit, place in enumerate(text_bits):
        text_place += ((text_row >> bit) & 1) << place
    text_ok = (text_place ^ length_ref[1]) < length_ref[0]
    blank = jnp.zeros((CUBE, HEAD), BF16)
    text_kv = text_ref[...]
    line = TILES_W * TILE
    def look(block):
        low, high, outer = block_rows(block)
        count = high - low
        q = qg_ref[block, :, :HEAD]
        g = qg_ref[block, :, HEAD:]
        both = jnp.concatenate(
            [jnp.concatenate([q, blank], 1), jnp.concatenate([blank, g], 1)], 0
        )
        done = 0 if block == 0 else 2
        places = [(low * line, count * line, done * line)]
        for side in range(2):
            places.append((OWN + side * (SIDE + TILE) + low * TILE, count * TILE, done * TILE))
        if outer is not None:
            rim = (OWN + 2 * (SIDE + TILE), OWN + SIDE, OWN + 2 * SIDE + TILE)
            for first, size in zip(rim, (line, TILE, TILE)):
                places.append((first, size, 0 if block == 0 else size))
        keys = []
        masks = []
        for i in range(3):
            parts = [near[i][first : first + size, :] for first, size, _ in places]
            keys.append(jnp.concatenate(parts, 0))
            tiles = allow_ref[block, i * SEEN : (i + 1) * SEEN, :]
            spread = jnp.broadcast_to(tiles[:, None, :], (SEEN, TILE, CUBE))
            masks.append(spread.reshape(SEEN * TILE, CUBE) > 0.5)
        keys.append(text_kv)
        masks.append(text_ok)
        scores = []
        dprobs = []
        for kv, ok in zip(keys, masks):
            mixed = lax.dot_general(
                kv, both, (((1,), (1,)), ((), ())), preferred_element_type=F32
            )
            scores.append(jnp.where(ok, mixed[:, :HEAD] * (scale * LOG2E), NEGATIVE))
            dprobs.append(mixed[:, HEAD:])
        top = functools.reduce(jnp.maximum, [jnp.max(s, 0, keepdims=True) for s in scores])
        return g, both, places, keys, scores, dprobs, top

    def finish(block, found):
        g, both, places, keys, scores, dprobs, top = found
        exps = [jnp.exp2(s - top) for s in scores]
        total = functools.reduce(jnp.add, [jnp.sum(e, 0, keepdims=True) for e in exps])
        inverse = 1.0 / total
        weights = [(e * inverse).astype(BF16) for e in exps]
        attended = jnp.zeros((CUBE, HEAD), F32)
        for w, kv in zip(weights, keys):
            attended += lax.dot_general(
                w, kv[:, HEAD:], (((0,), (0,)), ((), ())), preferred_element_type=F32
            )
        attended = attended.astype(BF16)
        od_ref[block, :, :HEAD] = attended
        product = g.astype(F32) * attended.astype(F32)
        delta = jnp.sum(product.T, 0, keepdims=True)
        dscores = [(e * ((d - delta) * inverse)).astype(BF16) for e, d in zip(exps, dprobs)]
        return both, places, keys, weights, dscores

    def settle_block(block, state):
        both, places, keys, weights, dscores = state
        query_grad = jnp.zeros((CUBE, HEAD), F32)
        for d, kv in zip(dscores, keys):
            query_grad += lax.dot_general(
                d, kv[:, :HEAD], (((0,), (0,)), ((), ())), preferred_element_type=F32
            )
        od_ref[block, :, HEAD:] = (query_grad * scale).astype(BF16)
        for i in range(4):
            change = jnp.dot(
                jnp.concatenate([dscores[i], weights[i]], 1), both, preferred_element_type=F32
            )
            if i == 3:
                middle = text_count // 2
                for target, piece in (
                    (text_out, change[:middle]),
                    (text_away_out, change[middle:]),
                ):
                    if block == 0:
                        target[...] = piece
                    else:
                        target[...] += piece
                continue
            taken = 0
            target = sums[i]
            for first, size, old in places:
                if old:
                    target[first : first + old, :] += change[taken : taken + old]
                if old < size:
                    target[first + old : first + size, :] = change[taken + old : taken + size]
                taken += size
    found = look(0)
    before = None
    for block in range(GROUP):
        following = look(block + 1) if block + 1 < GROUP else None
        now = finish(block, found)
        if before is not None:
            settle_block(block - 1, before)
        before = now
        found = following
    settle_block(GROUP - 1, before)
    lane = lax.broadcasted_iota(jnp.int32, (1, PAIR), 1)
    factor = jnp.where(lane < HEAD, scale, 1.0).astype(F32)
    here_out[...] = here_out[...] * factor
    own_below_out[...] = (below_sum[:OWN, :] * factor).astype(BF16)
    own_above_out[...] = (above_sum[:OWN, :] * factor).astype(BF16)
    halo_below_out[...] = (below_sum[OWN:, :] * factor).astype(BF16)
    halo_above_out[...] = (above_sum[OWN:, :] * factor).astype(BF16)
    text_out[...] = text_out[...] * factor
    text_away_out[...] = text_away_out[...] * factor


def attention(length, allow, qg, here, below, above, text, text_bits):
    width = qg.shape[-1]
    heads = width // PAIR
    text_count = text.shape[0]

    def spec(rows):
        return pl.BlockSpec((rows, PAIR), lambda h: (0, h))

    def shape(rows, dtype):
        return jax.ShapeDtypeStruct((rows, width), dtype)

    part = pl.BlockSpec((GROUP, CUBE, PAIR), lambda h: (0, 0, h))
    return pl.pallas_call(
        functools.partial(attention_kernel, text_bits),
        grid=(heads,),
        in_specs=[
            pl.BlockSpec(memory_space=pltpu.SMEM),
            pl.BlockSpec(allow.shape, lambda h: (0, 0, 0)),
            part,
        ]
        + [spec(ALL)] * 3
        + [spec(text_count)],
        out_specs=[part, spec(ALL)]
        + [spec(OWN)] * 2
        + [spec(ALL - OWN)] * 2
        + [spec(text_count // 2)] * 2,
        out_shape=[
            jax.ShapeDtypeStruct(qg.shape, BF16),
            shape(ALL, F32),
            shape(OWN, BF16),
            shape(OWN, BF16),
            shape(ALL - OWN, BF16),
            shape(ALL - OWN, BF16),
            shape(text_count // 2, F32),
            shape(text_count // 2, F32),
        ],
        scratch_shapes=[pltpu.VMEM((rows, PAIR), F32) for rows in (ALL, ALL)],
        compiler_params=pltpu.CompilerParams(vmem_limit_bytes=VMEM),
    )(length, allow, qg, here, below, above, text)


def settle_kernel(half_ref, own_ref, first_ref, second_ref, rim_ref, left_ref, right_ref, out_ref):
    line = TILES_W * TILE
    rim = rim_ref[...].astype(F32)
    half = half_ref[0]
    groups = out_ref.shape[0]
    for group in range(groups):
        block = pl.program_id(0) * groups + group
        cube = slice(group * CUBE, (group + 1) * CUBE)
        total = own_ref[cube] + first_ref[cube].astype(F32) + second_ref[cube].astype(F32)
        for i in range(TILES_H):
            edge = (block == 0) & (half == 1) if i == 0 else (block == GROUP - 1) & (half == 0)
            part = total[i * line : (i + 1) * line]
            part += jnp.where(edge, rim, 0.0)
            here = slice((group * TILES_H + i) * TILE, (group * TILES_H + i + 1) * TILE)
            pieces = [
                part[:TILE] + left_ref[here].astype(F32),
                part[TILE : line - TILE],
                part[line - TILE :] + right_ref[here].astype(F32),
            ]
            out_ref[group, i * line : (i + 1) * line, :] = jnp.concatenate(pieces, 0).astype(BF16)


def settle(half, own, first, second, rim, left, right):
    width = own.shape[-1]
    step = GROUP // PACKS

    def spec(rows):
        return pl.BlockSpec((rows * step, width), lambda b: (b, 0))

    return pl.pallas_call(
        settle_kernel,
        grid=(PACKS,),
        in_specs=[
            pl.BlockSpec(memory_space=pltpu.SMEM),
            spec(CUBE),
            spec(CUBE),
            spec(CUBE),
            pl.BlockSpec((TILES_W * TILE, width), lambda b: (0, 0)),
            spec(TILES_H * TILE),
            spec(TILES_H * TILE),
        ],
        out_specs=pl.BlockSpec((step, CUBE, width), lambda b: (b, 0, 0)),
        out_shape=jax.ShapeDtypeStruct((GROUP, CUBE, width), BF16),
        compiler_params=pltpu.CompilerParams(vmem_limit_bytes=VMEM),
    )(half, own, first, second, rim, left, right)


def offset_table():
    table = np.full((GROUP, 3, SEEN, TILES_H, TILES_W), -1, np.int32)
    for block in range(GROUP):
        for k, (kh, kw) in enumerate(seen_tiles(block)):
            for qh in range(TILES_H):
                for qw in range(TILES_W):
                    dh, dw = kh - (block * TILES_H + qh), kw - qw
                    if abs(dh) <= 1 and abs(dw) <= 1:
                        for i, dt in enumerate((0, -1, 1)):
                            table[block, i, k, qh, qw] = 9 * dt + 3 * dh + dw + 13
    return table


def allowed_tiles(pattern, half):
    hot = offset_table().reshape(GROUP, 3, SEEN, -1)[..., None] == np.arange(27)
    picked = jnp.sum(jnp.where(hot, pattern[:, None, None], 0.0), -1)
    places = np.array([seen_tiles(block) for block in range(GROUP)])
    t = lax.axis_index("ta") + jnp.array([0, -1, 1])
    t_ok = (t >= 0) & (t < lax.axis_size("ta"))
    w = lax.axis_index("wa") * TILES_W + places[..., 1]
    w_ok = (w >= 0) & (w < TILES_W * lax.axis_size("wa"))
    h = half * GROUP_H + places[..., 0]
    h_ok = (h >= 0) & (h < TILES_H * lax.axis_size("ha"))
    inside = t_ok[None, :, None] & (w_ok & h_ok)[:, None, :]
    picked = jnp.where(inside[..., None], picked, 0.0)
    return jnp.repeat(picked.reshape(GROUP, 3 * SEEN, -1), TILE, axis=2)


def turned_width(value, step):
    count = lax.axis_size("wa")
    return lax.ppermute(value, "wa", [(i, (i + step) % count) for i in range(count)])


def turned_time(value, step):
    count_t, count_h = lax.axis_size("ta"), lax.axis_size("ha")
    pairs = []
    for t in range(count_t):
        for h in range(count_h):
            t_to = t + step
            h_to = h
            if not 0 <= t_to < count_t:
                h_to = (h + count_h // 2) % count_h
            pairs.append((t * count_h + h, t_to % count_t * count_h + h_to))
    return lax.ppermute(value, ("ta", "ha"), pairs)


def swapped(value, axis, bit):
    count = lax.axis_size(axis)
    return lax.ppermute(value, axis, [(i, i ^ bit) for i in range(count)])


def regrouped(value):
    count = lax.axis_size("ha")
    groups = [list(range(i, i + GROUP)) for i in range(0, count, GROUP)]
    return lax.all_to_all(value, "ha", 0, 0, axis_index_groups=groups)


def log2(count):
    return count.bit_length() - 1


def text_steps():
    ta, ha, wa = (lax.axis_size(axis) for axis in ("ta", "ha", "wa"))
    halves = [("ha", ha >> i) for i in range(1, log2(ha) + 1)]
    steps = halves[:-2] + [("ta", ta >> i) for i in range(1, log2(ta))] + halves[-2:]
    steps += [("wa", wa >> i) for i in range(1, log2(wa) + 1)]
    return steps + [("ta", 1)]


def text_bits():
    start = {"wa": 0, "ha": log2(lax.axis_size("wa"))}
    start["ta"] = start["ha"] + log2(lax.axis_size("ha"))
    return tuple(start[axis] + log2(bit) for axis, bit in text_steps())


def is_high(axis, bit):
    return (lax.axis_index(axis) & bit) > 0


def gather_text(value, axis, bit):
    high = is_high(axis, bit)
    mine = theirs = value
    if axis == "ha" and bit < GROUP:
        middle = value.shape[0] // 2
        mine = jnp.where(high, value[middle:], value[:middle])
        theirs = jnp.where(high, value[:middle], value[middle:])
    return jnp.concatenate([mine, swapped(theirs, axis, bit)], 1)


def sent_text(mine, theirs, axis, bit):
    return mine, swapped(theirs, axis, bit), axis, bit


def joined_text(sent, *others):
    mine, other, axis, bit = sent
    if others:
        mine, other = lax.optimization_barrier((mine, other, *others))[:2]
    if axis == "ha" and bit < GROUP:
        high = is_high(axis, bit)
        first = jnp.where(high, other, mine)
        second = jnp.where(high, mine, other)
        return jnp.concatenate([first, second], 0)
    return mine + other


def scatter_text(sent, axis, bit, *others):
    value = joined_text(sent, *others)
    middle = value.shape[1] // 2
    return sent_text(value[:, :middle], value[:, middle:], axis, bit)


def after(value, *others):
    return lax.optimization_barrier((value, *others))[0]


def local(query, key, value, d_out, text_key, text_value, block_pattern, text_length):
    full = query.shape[-1]
    half = lax.axis_index("ha") // GROUP
    steps = text_steps()
    line = TILES_W * TILE

    kv_out = pack(
        key.reshape(CUBE, full), value.reshape(CUBE, full), block_pattern.reshape(-1, 27)
    )
    text = jnp.stack([text_key.reshape(-1, HEAD), text_value.reshape(-1, HEAD)], 1)
    text = after(text.reshape(GROUP, 1, -1), kv_out)
    for step in steps[:2]:
        text = gather_text(text, *step)
    qg_out = pack(query.reshape(CUBE, full), d_out.reshape(CUBE, full))
    kv_in = regrouped(kv_out)
    width = kv_in.shape[-1]

    own = kv_in[:, :CUBE].reshape(GROUP_H, TILES_W, TILE, width)
    flat = own.reshape(OWN, width)
    edge = jnp.where(half == 0, own[GROUP_H - 1], own[0])
    rim = swapped(edge.reshape(line, width), "ha", GROUP)
    text = gather_text(after(text, kv_in, qg_out), *steps[2])
    to_right = jnp.concatenate([own[:, TILES_W - 1].reshape(SIDE, width), rim[line - TILE :]], 0)
    to_left = jnp.concatenate([own[:, 0].reshape(SIDE, width), rim[:TILE]], 0)
    left = turned_width(to_right, 1)
    right = turned_width(to_left, -1)
    text = after(text, rim)
    for step in steps[3:5]:
        text = gather_text(text, *step)
    here = after(jnp.concatenate([flat, left, right, rim], 0), text)
    below = turned_time(here, 1)
    above = turned_time(here, -1)
    qg = regrouped(after(qg_out, rim))
    text = after(text, here)
    for step in steps[5:-1]:
        text = gather_text(text, *step)
    text = gather_text(after(text, qg), *steps[-1])
    allow = allowed_tiles(kv_in[:, CUBE : CUBE + 8, :27].astype(F32), half)

    me = (lax.axis_index("ta") * lax.axis_size("ha") + lax.axis_index("ha")) * lax.axis_size("wa")
    me = me + lax.axis_index("wa")
    od, here_grad, own_below, own_above, halo_below, halo_above, text_grad, text_away = attention(
        jnp.concatenate([text_length, me.reshape(1)]),
        allow,
        qg,
        here,
        below,
        above,
        text[0],
        text_bits(),
    )

    halo_first = turned_time(halo_below, -1)
    halo_second = turned_time(halo_above, 1)
    first = turned_time(after(own_below, halo_first, halo_second), -1)
    second = turned_time(after(own_above, halo_first, halo_second), 1)
    back = steps[::-1]
    text_grad = sent_text(text_grad[None], text_away[None], *back[0])
    text_grad = scatter_text(text_grad, *back[1])
    od_in = regrouped(od)
    halo = here_grad[OWN:] + halo_first.astype(F32) + halo_second.astype(F32)
    side = SIDE + TILE
    to_left = halo[:side].astype(BF16)
    to_right = halo[side : 2 * side].astype(BF16)
    rim_grad = halo[2 * side :]
    right = turned_width(to_left, -1)
    left = turned_width(to_right, 1)
    text_grad = scatter_text(text_grad, *back[2], to_left, to_right)
    rim_out = jnp.concatenate(
        [
            rim_grad[:TILE] + left[SIDE:].astype(F32),
            rim_grad[TILE : line - TILE],
            rim_grad[line - TILE :] + right[SIDE:].astype(F32),
        ],
        0,
    ).astype(BF16)
    rim_in = swapped(rim_out, "ha", GROUP)
    text_grad = scatter_text(text_grad, *back[3], rim_out)
    text_grad = scatter_text(text_grad, *back[4], rim_in, first, second)
    grads = settle(half.reshape(1), here_grad, first, second, rim_in, left, right)
    text_grad = scatter_text(text_grad, *back[5], grads)
    for step in back[6:]:
        text_grad = scatter_text(text_grad, *step)
    text_grad = joined_text(text_grad)
    attended, query_grad = unpack(od_in)
    key_grad, value_grad = unpack(regrouped(grads))
    text_grad = text_grad.astype(BF16).reshape(-1, 2, HEAD)
    return (
        attended.reshape(query.shape),
        query_grad.reshape(query.shape),
        key_grad.reshape(query.shape),
        value_grad.reshape(query.shape),
        text_grad[:, 0].reshape(1, full),
        text_grad[:, 1].reshape(1, full),
    )


def solution(mesh):
    cube = P("ta", "ha", "wa", None)
    text = P(("ta", "ha", "wa"), None)
    return jax.shard_map(
        local,
        mesh=mesh,
        in_specs=(cube, cube, cube, cube, text, text, cube, P()),
        out_specs=(cube, cube, cube, cube, text, text),
        check_vma=False,
    )
```

```python
import functools

import jax
import jax.numpy as jnp
import numpy as np
from jax import lax
from jax.experimental import pallas as pl
from jax.experimental.pallas import tpu as pltpu
from jax.sharding import PartitionSpec as P

HEAD = 128
PAIR = 2 * HEAD
TILE_T = 2
TILE_H = 2
TILE_W = 4
TILE = TILE_T * TILE_H * TILE_W
NEGATIVE = -1e30
LOG2E = 1.4426950408889634
EXTRA = 16
PACKS = 2
VMEM = 58 * 1024 * 1024
F32 = jnp.float32
BF16 = jnp.bfloat16

ROWS = 4
COLS = 16
TILES_H = ROWS // TILE_H
TILES_W = COLS // TILE_W
CUBE = TILE_T * ROWS * COLS
GROUP = 4
GROUP_H = GROUP * TILES_H
OWN = GROUP_H * TILES_W * TILE
SIDE = GROUP_H * TILE
RIM = (TILES_W + 2) * TILE
ALL = OWN + 2 * SIDE + RIM
SEEN = (TILES_H + 2) * (TILES_W + 2)


def natural_index(row):
    tile_h = row >> 6
    tile_w = (row >> 4) & 3
    t = (row >> 3) & 1
    h = (row >> 2) & 1
    w = row & 3
    return t * (ROWS * COLS) + (tile_h * TILE_H + h) * COLS + tile_w * TILE_W + w


def pack_kernel(first_ref, second_ref, *rest):
    out_ref = rest[-1]
    row = lax.broadcasted_iota(jnp.int32, (CUBE, CUBE), 0)
    col = lax.broadcasted_iota(jnp.int32, (CUBE, CUBE), 1)
    order = jnp.where(natural_index(row) == col, 1.0, 0.0).astype(BF16)
    first = jnp.dot(order, first_ref[...], preferred_element_type=F32).astype(BF16)
    second = jnp.dot(order, second_ref[...], preferred_element_type=F32).astype(BF16)
    groups, _, width = out_ref.shape
    heads = width // PAIR
    for group in range(groups):
        for i in range(heads):
            source = slice((group * heads + i) * HEAD, (group * heads + i + 1) * HEAD)
            out_ref[group, :CUBE, i * PAIR : i * PAIR + HEAD] = first[:, source]
            out_ref[group, :CUBE, i * PAIR + HEAD : (i + 1) * PAIR] = second[:, source]
        if len(rest) > 1:
            pattern = rest[0][...].astype(F32)
            lines = jnp.concatenate([pattern, jnp.zeros_like(pattern)], 0).astype(BF16)
            out_ref[group, CUBE:, :] = jnp.zeros((EXTRA, width), BF16)
            out_ref[group, CUBE:, : pattern.shape[1]] = lines


def pack(first, second, pattern=None):
    width = first.shape[1] // GROUP
    step = GROUP // PACKS
    rows = CUBE + (0 if pattern is None else EXTRA)
    specs = [pl.BlockSpec((CUBE, width * step), lambda g: (0, g))] * 2
    extras = ()
    if pattern is not None:
        specs.append(pl.BlockSpec(pattern.shape, lambda g: (0, 0)))
        extras = (pattern,)
    return pl.pallas_call(
        pack_kernel,
        grid=(PACKS,),
        in_specs=specs,
        out_specs=pl.BlockSpec((step, rows, 2 * width), lambda g: (g, 0, 0)),
        out_shape=jax.ShapeDtypeStruct((GROUP, rows, 2 * width), BF16),
        compiler_params=pltpu.CompilerParams(vmem_limit_bytes=VMEM),
    )(first, second, *extras)


def unpack_kernel(packed_ref, first_ref, second_ref):
    row = lax.broadcasted_iota(jnp.int32, (CUBE, CUBE), 0)
    col = lax.broadcasted_iota(jnp.int32, (CUBE, CUBE), 1)
    order = jnp.where(natural_index(col) == row, 1.0, 0.0).astype(BF16)
    groups, _, width = packed_ref.shape
    heads = width // PAIR
    for group in range(groups):
        both = jnp.dot(order, packed_ref[group], preferred_element_type=F32).astype(BF16)
        for i in range(heads):
            target = slice((group * heads + i) * HEAD, (group * heads + i + 1) * HEAD)
            first_ref[:, target] = both[:, i * PAIR : i * PAIR + HEAD]
            second_ref[:, target] = both[:, i * PAIR + HEAD : (i + 1) * PAIR]


def unpack(packed):
    _, rows, width = packed.shape
    step = GROUP // PACKS
    half = width // 2
    return pl.pallas_call(
        unpack_kernel,
        grid=(PACKS,),
        in_specs=[pl.BlockSpec((step, rows, width), lambda g: (g, 0, 0))],
        out_specs=[pl.BlockSpec((CUBE, half * step), lambda g: (0, g))] * 2,
        out_shape=[jax.ShapeDtypeStruct((CUBE, GROUP * half), BF16)] * 2,
        compiler_params=pltpu.CompilerParams(vmem_limit_bytes=VMEM),
    )(packed)


def block_rows(block):
    low, high = block * TILES_H - 1, (block + 1) * TILES_H + 1
    outer = -1 if low < 0 else GROUP_H if high > GROUP_H else None
    return max(low, 0), min(high, GROUP_H), outer


def seen_tiles(block):
    low, high, outer = block_rows(block)
    tiles = [(h, w) for h in range(low, high) for w in range(TILES_W)]
    tiles += [(h, -1) for h in range(low, high)] + [(h, TILES_W) for h in range(low, high)]
    if outer is not None:
        tiles += [(outer, w) for w in (*range(TILES_W), -1, TILES_W)]
    return tiles


def attention_kernel(
    text_bits,
    length_ref,
    allow_ref,
    qg_ref,
    here_ref,
    below_ref,
    above_ref,
    text_ref,
    od_ref,
    here_out,
    own_below_out,
    own_above_out,
    halo_below_out,
    halo_above_out,
    text_out,
    text_away_out,
    below_sum,
    above_sum,
):
    text_count = text_ref.shape[0]
    scale = HEAD**-0.5
    near = (here_ref, below_ref, above_ref)
    sums = (here_out, below_sum, above_sum)
    text_row = lax.broadcasted_iota(jnp.int32, (text_count, CUBE), 0)
    text_place = jnp.zeros_like(text_row)
    for bit, place in enumerate(text_bits):
        text_place += ((text_row >> bit) & 1) << place
    text_ok = (text_place ^ length_ref[1]) < length_ref[0]
    blank = jnp.zeros((CUBE, HEAD), BF16)
    text_kv = text_ref[...]
    line = TILES_W * TILE
    def look(block):
        low, high, outer = block_rows(block)
        count = high - low
        q = qg_ref[block, :, :HEAD]
        g = qg_ref[block, :, HEAD:]
        both = jnp.concatenate(
            [jnp.concatenate([q, blank], 1), jnp.concatenate([blank, g], 1)], 0
        )
        done = 0 if block == 0 else 2
        places = [(low * line, count * line, done * line)]
        for side in range(2):
            places.append((OWN + side * (SIDE + TILE) + low * TILE, count * TILE, done * TILE))
        if outer is not None:
            rim = (OWN + 2 * (SIDE + TILE), OWN + SIDE, OWN + 2 * SIDE + TILE)
            for first, size in zip(rim, (line, TILE, TILE)):
                places.append((first, size, 0 if block == 0 else size))
        keys = []
        masks = []
        for i in range(3):
            parts = [near[i][first : first + size, :] for first, size, _ in places]
            keys.append(jnp.concatenate(parts, 0))
            tiles = allow_ref[block, i * SEEN : (i + 1) * SEEN, :]
            spread = jnp.broadcast_to(tiles[:, None, :], (SEEN, TILE, CUBE))
            masks.append(spread.reshape(SEEN * TILE, CUBE) > 0.5)
        keys.append(text_kv)
        masks.append(text_ok)
        scores = []
        dprobs = []
        for kv, ok in zip(keys, masks):
            mixed = lax.dot_general(
                kv, both, (((1,), (1,)), ((), ())), preferred_element_type=F32
            )
            scores.append(jnp.where(ok, mixed[:, :HEAD] * (scale * LOG2E), NEGATIVE))
            dprobs.append(mixed[:, HEAD:])
        top = functools.reduce(jnp.maximum, [jnp.max(s, 0, keepdims=True) for s in scores])
        return g, both, places, keys, scores, dprobs, top

    def finish(block, found):
        g, both, places, keys, scores, dprobs, top = found
        exps = [jnp.exp2(s - top) for s in scores]
        total = functools.reduce(jnp.add, [jnp.sum(e, 0, keepdims=True) for e in exps])
        inverse = 1.0 / total
        weights = [(e * inverse).astype(BF16) for e in exps]
        attended = jnp.zeros((CUBE, HEAD), F32)
        for w, kv in zip(weights, keys):
            attended += lax.dot_general(
                w, kv[:, HEAD:], (((0,), (0,)), ((), ())), preferred_element_type=F32
            )
        attended = attended.astype(BF16)
        od_ref[block, :, :HEAD] = attended
        product = g.astype(F32) * attended.astype(F32)
        delta = jnp.sum(product.T, 0, keepdims=True)
        dscores = [(e * ((d - delta) * inverse)).astype(BF16) for e, d in zip(exps, dprobs)]
        return both, places, keys, weights, dscores

    def settle_block(block, state):
        both, places, keys, weights, dscores = state
        query_grad = jnp.zeros((CUBE, HEAD), F32)
        for d, kv in zip(dscores, keys):
            query_grad += lax.dot_general(
                d, kv[:, :HEAD], (((0,), (0,)), ((), ())), preferred_element_type=F32
            )
        od_ref[block, :, HEAD:] = (query_grad * scale).astype(BF16)
        for i in range(4):
            change = jnp.dot(
                jnp.concatenate([dscores[i], weights[i]], 1), both, preferred_element_type=F32
            )
            if i == 3:
                middle = text_count // 2
                for target, piece in (
                    (text_out, change[:middle]),
                    (text_away_out, change[middle:]),
                ):
                    if block == 0:
                        target[...] = piece
                    else:
                        target[...] += piece
                continue
            taken = 0
            target = sums[i]
            for first, size, old in places:
                if old:
                    target[first : first + old, :] += change[taken : taken + old]
                if old < size:
                    target[first + old : first + size, :] = change[taken + old : taken + size]
                taken += size
    found = look(0)
    before = None
    for block in range(GROUP):
        following = look(block + 1) if block + 1 < GROUP else None
        now = finish(block, found)
        if before is not None:
            settle_block(block - 1, before)
        before = now
        found = following
    settle_block(GROUP - 1, before)
    lane = lax.broadcasted_iota(jnp.int32, (1, PAIR), 1)
    factor = jnp.where(lane < HEAD, scale, 1.0).astype(F32)
    here_out[...] = here_out[...] * factor
    own_below_out[...] = (below_sum[:OWN, :] * factor).astype(BF16)
    own_above_out[...] = (above_sum[:OWN, :] * factor).astype(BF16)
    halo_below_out[...] = (below_sum[OWN:, :] * factor).astype(BF16)
    halo_above_out[...] = (above_sum[OWN:, :] * factor).astype(BF16)
    text_out[...] = text_out[...] * factor
    text_away_out[...] = text_away_out[...] * factor


def attention(length, allow, qg, here, below, above, text, text_bits):
    width = qg.shape[-1]
    heads = width // PAIR
    text_count = text.shape[0]

    def spec(rows):
        return pl.BlockSpec((rows, PAIR), lambda h: (0, h))

    def shape(rows, dtype):
        return jax.ShapeDtypeStruct((rows, width), dtype)

    part = pl.BlockSpec((GROUP, CUBE, PAIR), lambda h: (0, 0, h))
    return pl.pallas_call(
        functools.partial(attention_kernel, text_bits),
        grid=(heads,),
        in_specs=[
            pl.BlockSpec(memory_space=pltpu.SMEM),
            pl.BlockSpec(allow.shape, lambda h: (0, 0, 0)),
            part,
        ]
        + [spec(ALL)] * 3
        + [spec(text_count)],
        out_specs=[part, spec(ALL)]
        + [spec(OWN)] * 2
        + [spec(ALL - OWN)] * 2
        + [spec(text_count // 2)] * 2,
        out_shape=[
            jax.ShapeDtypeStruct(qg.shape, BF16),
            shape(ALL, F32),
            shape(OWN, BF16),
            shape(OWN, BF16),
            shape(ALL - OWN, BF16),
            shape(ALL - OWN, BF16),
            shape(text_count // 2, F32),
            shape(text_count // 2, F32),
        ],
        scratch_shapes=[pltpu.VMEM((rows, PAIR), F32) for rows in (ALL, ALL)],
        compiler_params=pltpu.CompilerParams(vmem_limit_bytes=VMEM),
    )(length, allow, qg, here, below, above, text)


def settle_kernel(half_ref, own_ref, first_ref, second_ref, rim_ref, left_ref, right_ref, out_ref):
    line = TILES_W * TILE
    rim = rim_ref[...].astype(F32)
    half = half_ref[0]
    groups = out_ref.shape[0]
    for group in range(groups):
        block = pl.program_id(0) * groups + group
        cube = slice(group * CUBE, (group + 1) * CUBE)
        total = own_ref[cube] + first_ref[cube].astype(F32) + second_ref[cube].astype(F32)
        for i in range(TILES_H):
            edge = (block == 0) & (half == 1) if i == 0 else (block == GROUP - 1) & (half == 0)
            part = total[i * line : (i + 1) * line]
            part += jnp.where(edge, rim, 0.0)
            here = slice((group * TILES_H + i) * TILE, (group * TILES_H + i + 1) * TILE)
            pieces = [
                part[:TILE] + left_ref[here].astype(F32),
                part[TILE : line - TILE],
                part[line - TILE :] + right_ref[here].astype(F32),
            ]
            out_ref[group, i * line : (i + 1) * line, :] = jnp.concatenate(pieces, 0).astype(BF16)


def settle(half, own, first, second, rim, left, right):
    width = own.shape[-1]
    step = GROUP // PACKS

    def spec(rows):
        return pl.BlockSpec((rows * step, width), lambda b: (b, 0))

    return pl.pallas_call(
        settle_kernel,
        grid=(PACKS,),
        in_specs=[
            pl.BlockSpec(memory_space=pltpu.SMEM),
            spec(CUBE),
            spec(CUBE),
            spec(CUBE),
            pl.BlockSpec((TILES_W * TILE, width), lambda b: (0, 0)),
            spec(TILES_H * TILE),
            spec(TILES_H * TILE),
        ],
        out_specs=pl.BlockSpec((step, CUBE, width), lambda b: (b, 0, 0)),
        out_shape=jax.ShapeDtypeStruct((GROUP, CUBE, width), BF16),
        compiler_params=pltpu.CompilerParams(vmem_limit_bytes=VMEM),
    )(half, own, first, second, rim, left, right)


def offset_table():
    table = np.full((GROUP, 3, SEEN, TILES_H, TILES_W), -1, np.int32)
    for block in range(GROUP):
        for k, (kh, kw) in enumerate(seen_tiles(block)):
            for qh in range(TILES_H):
                for qw in range(TILES_W):
                    dh, dw = kh - (block * TILES_H + qh), kw - qw
                    if abs(dh) <= 1 and abs(dw) <= 1:
                        for i, dt in enumerate((0, -1, 1)):
                            table[block, i, k, qh, qw] = 9 * dt + 3 * dh + dw + 13
    return table


def allowed_tiles(pattern, half):
    hot = offset_table().reshape(GROUP, 3, SEEN, -1)[..., None] == np.arange(27)
    picked = jnp.sum(jnp.where(hot, pattern[:, None, None], 0.0), -1)
    places = np.array([seen_tiles(block) for block in range(GROUP)])
    t = lax.axis_index("ta") + jnp.array([0, -1, 1])
    t_ok = (t >= 0) & (t < lax.axis_size("ta"))
    w = lax.axis_index("wa") * TILES_W + places[..., 1]
    w_ok = (w >= 0) & (w < TILES_W * lax.axis_size("wa"))
    h = half * GROUP_H + places[..., 0]
    h_ok = (h >= 0) & (h < TILES_H * lax.axis_size("ha"))
    inside = t_ok[None, :, None] & (w_ok & h_ok)[:, None, :]
    picked = jnp.where(inside[..., None], picked, 0.0)
    return jnp.repeat(picked.reshape(GROUP, 3 * SEEN, -1), TILE, axis=2)


def turned_width(value, step):
    count = lax.axis_size("wa")
    return lax.ppermute(value, "wa", [(i, (i + step) % count) for i in range(count)])


def turned_time(value, step):
    count_t, count_h = lax.axis_size("ta"), lax.axis_size("ha")
    pairs = []
    for t in range(count_t):
        for h in range(count_h):
            t_to = t + step
            h_to = h
            if not 0 <= t_to < count_t:
                h_to = (h + count_h // 2) % count_h
            pairs.append((t * count_h + h, t_to % count_t * count_h + h_to))
    return lax.ppermute(value, ("ta", "ha"), pairs)


def swapped(value, axis, bit):
    count = lax.axis_size(axis)
    return lax.ppermute(value, axis, [(i, i ^ bit) for i in range(count)])


def regrouped(value):
    count = lax.axis_size("ha")
    groups = [list(range(i, i + GROUP)) for i in range(0, count, GROUP)]
    return lax.all_to_all(value, "ha", 0, 0, axis_index_groups=groups)


def log2(count):
    return count.bit_length() - 1


def text_steps():
    ta, ha, wa = (lax.axis_size(axis) for axis in ("ta", "ha", "wa"))
    halves = [("ha", ha >> i) for i in range(1, log2(ha) + 1)]
    steps = halves[:-2] + [("ta", ta >> i) for i in range(1, log2(ta))] + halves[-2:]
    steps += [("wa", wa >> i) for i in range(1, log2(wa) + 1)]
    return steps + [("ta", 1)]


def text_bits():
    start = {"wa": 0, "ha": log2(lax.axis_size("wa"))}
    start["ta"] = start["ha"] + log2(lax.axis_size("ha"))
    return tuple(start[axis] + log2(bit) for axis, bit in text_steps())


def is_high(axis, bit):
    return (lax.axis_index(axis) & bit) > 0


def gather_text(value, axis, bit):
    high = is_high(axis, bit)
    mine = theirs = value
    if axis == "ha" and bit < GROUP:
        middle = value.shape[0] // 2
        mine = jnp.where(high, value[middle:], value[:middle])
        theirs = jnp.where(high, value[:middle], value[middle:])
    return jnp.concatenate([mine, swapped(theirs, axis, bit)], 1)


def sent_text(mine, theirs, axis, bit):
    return mine, swapped(theirs, axis, bit), axis, bit


def joined_text(sent, *others):
    mine, other, axis, bit = sent
    if others:
        mine, other = lax.optimization_barrier((mine, other, *others))[:2]
    if axis == "ha" and bit < GROUP:
        high = is_high(axis, bit)
        first = jnp.where(high, other, mine)
        second = jnp.where(high, mine, other)
        return jnp.concatenate([first, second], 0)
    return mine + other


def scatter_text(sent, axis, bit, *others):
    value = joined_text(sent, *others)
    middle = value.shape[1] // 2
    return sent_text(value[:, :middle], value[:, middle:], axis, bit)


def after(value, *others):
    return lax.optimization_barrier((value, *others))[0]


def local(query, key, value, d_out, text_key, text_value, block_pattern, text_length):
    full = query.shape[-1]
    half = lax.axis_index("ha") // GROUP
    steps = text_steps()
    line = TILES_W * TILE

    kv_out = pack(
        key.reshape(CUBE, full), value.reshape(CUBE, full), block_pattern.reshape(-1, 27)
    )
    text = jnp.stack([text_key.reshape(-1, HEAD), text_value.reshape(-1, HEAD)], 1)
    text = after(text.reshape(GROUP, 1, -1), kv_out)
    for step in steps[:2]:
        text = gather_text(text, *step)
    qg_out = pack(query.reshape(CUBE, full), d_out.reshape(CUBE, full))
    kv_in = regrouped(kv_out)
    width = kv_in.shape[-1]

    own = kv_in[:, :CUBE].reshape(GROUP_H, TILES_W, TILE, width)
    flat = own.reshape(OWN, width)
    edge = jnp.where(half == 0, own[GROUP_H - 1], own[0])
    rim = swapped(edge.reshape(line, width), "ha", GROUP)
    text = gather_text(after(text, kv_in, qg_out), *steps[2])
    to_right = jnp.concatenate([own[:, TILES_W - 1].reshape(SIDE, width), rim[line - TILE :]], 0)
    to_left = jnp.concatenate([own[:, 0].reshape(SIDE, width), rim[:TILE]], 0)
    left = turned_width(to_right, 1)
    right = turned_width(to_left, -1)
    text = after(text, rim)
    for step in steps[3:5]:
        text = gather_text(text, *step)
    here = after(jnp.concatenate([flat, left, right, rim], 0), text)
    below = turned_time(here, 1)
    above = turned_time(here, -1)
    qg = regrouped(after(qg_out, rim))
    text = after(text, here)
    for step in steps[5:-1]:
        text = gather_text(text, *step)
    text = gather_text(after(text, qg), *steps[-1])
    allow = allowed_tiles(kv_in[:, CUBE : CUBE + 8, :27].astype(F32), half)

    me = (lax.axis_index("ta") * lax.axis_size("ha") + lax.axis_index("ha")) * lax.axis_size("wa")
    me = me + lax.axis_index("wa")
    od, here_grad, own_below, own_above, halo_below, halo_above, text_grad, text_away = attention(
        jnp.concatenate([text_length, me.reshape(1)]),
        allow,
        qg,
        here,
        below,
        above,
        text[0],
        text_bits(),
    )

    halo_first = turned_time(halo_below, -1)
    halo_second = turned_time(halo_above, 1)
    first = turned_time(after(own_below, halo_first, halo_second), -1)
    second = turned_time(after(own_above, halo_first, halo_second), 1)
    back = steps[::-1]
    text_grad = sent_text(text_grad[None], text_away[None], *back[0])
    text_grad = scatter_text(text_grad, *back[1])
    text_grad = scatter_text(text_grad, *back[2])
    od_in = regrouped(od)
    halo = here_grad[OWN:] + halo_first.astype(F32) + halo_second.astype(F32)
    side = SIDE + TILE
    to_left = halo[:side].astype(BF16)
    to_right = halo[side : 2 * side].astype(BF16)
    rim_grad = halo[2 * side :]
    right = turned_width(to_left, -1)
    left = turned_width(to_right, 1)
    text_grad = scatter_text(text_grad, *back[3], to_left, to_right, od_in)
    rim_out = jnp.concatenate(
        [
            rim_grad[:TILE] + left[SIDE:].astype(F32),
            rim_grad[TILE : line - TILE],
            rim_grad[line - TILE :] + right[SIDE:].astype(F32),
        ],
        0,
    ).astype(BF16)
    rim_in = swapped(rim_out, "ha", GROUP)
    text_grad = scatter_text(text_grad, *back[4], rim_out)
    text_grad = scatter_text(text_grad, *back[5], rim_in, first, second)
    grads = settle(half.reshape(1), here_grad, first, second, rim_in, left, right)
    text_grad = scatter_text(text_grad, *back[6], grads)
    for step in back[7:]:
        text_grad = scatter_text(text_grad, *step)
    text_grad = joined_text(text_grad)
    attended, query_grad = unpack(od_in)
    key_grad, value_grad = unpack(regrouped(grads))
    text_grad = text_grad.astype(BF16).reshape(-1, 2, HEAD)
    return (
        attended.reshape(query.shape),
        query_grad.reshape(query.shape),
        key_grad.reshape(query.shape),
        value_grad.reshape(query.shape),
        text_grad[:, 0].reshape(1, full),
        text_grad[:, 1].reshape(1, full),
    )


def solution(mesh):
    cube = P("ta", "ha", "wa", None)
    text = P(("ta", "ha", "wa"), None)
    return jax.shard_map(
        local,
        mesh=mesh,
        in_specs=(cube, cube, cube, cube, text, text, cube, P()),
        out_specs=(cube, cube, cube, cube, text, text),
        check_vma=False,
    )
```
